128 devices in a mesh: expert: 16 (over x, y), tensor: 8 (over z, core).
Axes of the slice: x: 4, y: 4, z: 4, core: 2. Of those that a mesh axis runs over, the one named last changes fastest.
Arguments:
- tokens: bfloat16 [2048, 7168], P('expert', 'tensor'), may hold values from -6 to 6
- cotangent: bfloat16 [2048, 7168], P('expert', 'tensor'), may hold values from -6 to 6
- routes: int32 [2048, 2], P('expert'), may hold values from 0 to 15, all different within a row; in each aligned block of 128 rows (0 to 127, 128 to 255, ...) at most 32 rows name the same one
- route_weights: bfloat16 [2048, 2], P('expert'), may hold values from 0.099609375 to 1
- capacity_plan: int32 [16], replicated, may hold values from 1 to 32, as said below
- up_weight: bfloat16 [16, 7168, 2432], P('expert', 'tensor'), may hold values from -0.0625 to 0.0625
- down_weight: bfloat16 [16, 2432, 7168], P('expert', None, 'tensor'), may hold values from -0.125 to 0.125
Outputs:
- layer_out: bfloat16 [2048, 7168], P('expert', 'tensor')
- token_grad: bfloat16 [2048, 7168], P('expert', 'tensor')
- up_grad: bfloat16 [16, 7168, 2432], P('expert', 'tensor')
- down_grad: bfloat16 [16, 2432, 7168], P('expert', None, 'tensor')
The draws below stay inside these ranges and needn't reach their ends.
Inputs may be any that keep to these rules, and one draw needn't show every extreme that they name: `routes`: within each aligned block of 128 tokens no expert is named more than 32 times, and a token's two experts differ. `capacity_plan`: some expert has exactly 32 and some exactly 1.
All inputs are finite; a program needn't handle non-finite values.
Results may differ from the reference program's by a relative error of at most 0.0063.
Values may be sent and summed in bfloat16 or wider, within the bound.
A program may use at most 128 MiB of HBM per device.

```python
import math
import jax
import jax.numpy as jnp
import numpy as np
from jax import lax

D = 7168
FFW = 2432
TOK_DEV = 128
EXPERTS = 16
CAP = 32
TOKENS = 2048
N_EXPERT = 16


def draw_capacity_plan(key, part):
    key = jax.random.fold_in(key, 11)
    leading, second = jax.random.split(key)
    ranking = jax.random.permutation(leading, EXPERTS)
    values = jax.random.randint(second, (EXPERTS,), 1, CAP + 1)
    values = values.at[ranking[0]].set(CAP).at[ranking[1]].set(1)
    return values.astype(jnp.int32)


def block_scale(stream_key, extent, cuts, least, top_value):
    gain, own = 1.0, jax.random.fold_in(stream_key, 6)
    for dim, shards_of in cuts:
        steps = jnp.exp(jax.random.uniform(jax.random.fold_in(own, dim), (shards_of,), jnp.float32, least / len(cuts), top_value / len(cuts)))
        gain = gain * jnp.repeat(steps, extent[dim] // shards_of).reshape([-1 if axis == dim else 1 for axis in range(len(extent))])
    return gain


def deal_out(stream_key, own, number, rows, count, top, bound, skew):
    order = jax.random.permutation(stream_key, count)
    crowded, usual = shares(count, rows * top, bound, skew, True), shares(count, rows * top, bound, skew, False)
    places = jnp.arange(count)

    def named(sizes, rotation):
        used = int((sizes > 0).sum())
        fixed = max(1, used // 4)
        passed = fixed + (places - fixed + rotation * (used - fixed)) % max(1, count - fixed)
        return jnp.zeros((count,), jnp.int32).at[order[jnp.where(places < fixed, places, passed)]].set(jnp.asarray(sizes, jnp.int32))

    sizes = jnp.where(number % 4 == 0, named(crowded, number // 4), named(usual, number - number // 4 - 1))
    mixed = jax.random.permutation(jax.random.fold_in(own, 3), count)
    donor, receiver = mixed[0:count // 2 * 2:2], mixed[1:count // 2 * 2:2]
    slack = jnp.minimum(sizes[donor] - 1, bound - sizes[receiver]) // 2
    slack = jnp.where((donor == order[0]) | (receiver == order[0]) | (sizes[receiver] == 0), 0, jnp.maximum(slack, 0))
    passed = jax.random.randint(jax.random.fold_in(own, 4), (count // 2,), 0, 1 << 20) % (slack + 1)
    sizes = sizes.at[donor].add(-passed).at[receiver].add(passed)
    members = jnp.searchsorted(jnp.cumsum(sizes), jnp.arange(rows * top), side="right").astype(jnp.int32)
    listing = members.reshape(top, rows).T
    listing = listing[jax.random.permutation(jax.random.fold_in(own, 1), rows)]
    rotation = jax.random.randint(jax.random.fold_in(own, 2), (rows, 1), 0, top)
    return jnp.take_along_axis(listing, (jnp.arange(top)[None, :] + rotation) % top, axis=1)


def shares(number_of, total, bound, skew, full):
    loads = [(1 << 20) // math.isqrt(standing ** skew) + 1 for standing in range(1, number_of + 1)]
    largest = bound if full else min(bound, max(-(-total // number_of), total * loads[0] // sum(loads)))
    least = 1 if total - largest >= number_of - 1 else 0
    counts, spare = [largest] + [least] * (number_of - 1), total - largest - least * (number_of - 1)
    while spare > 0:
        movable = [i for i in range(1, number_of) if counts[i] < largest] or [i for i in range(1, number_of) if counts[i] < bound]
        pool, budget = sum([loads[i] for i in movable]), spare
        for i in movable:
            more = min(bound - counts[i], max(1, budget * loads[i] // pool), spare)
            counts[i] = counts[i] + more
            spare = spare - more
    return np.array(counts)


def bell_draw(rng, shape, scale, bound, cuts=(), kind=jnp.bfloat16):
    result = jax.random.normal(rng, shape, jnp.float32) * scale
    if len(cuts) > 0:
        result = block_scale(rng, shape, cuts, -0.22, 0.18) * result
    return jnp.clip(result, min=-bound, max=bound).astype(kind)


def setup_inputs(seed: int = 0) -> dict:
    arg_keys = jax.random.split(jax.random.key(seed), 8)
    tokens = bell_draw(arg_keys[0], (TOKENS, D), 1.0, 6.0, ((0, 16), (1, 8)))
    cotangent = bell_draw(arg_keys[1], (TOKENS, D), 1.0, 6.0, ((0, 16), (1, 8)))
    routes_keys = jax.random.split(jax.random.fold_in(arg_keys[2], 1), TOKENS // TOK_DEV)
    routes_turns = jax.random.permutation(jax.random.fold_in(arg_keys[2], 3), TOKENS // TOK_DEV)
    routes = jax.vmap(lambda own, number: deal_out(jax.random.fold_in(arg_keys[2], 2), own, number, TOK_DEV, EXPERTS, 2, CAP, 2))(routes_keys, routes_turns).reshape((TOKENS, 2))
    route_weights = jnp.clip(0.099609375 + 0.9003906 * jax.random.uniform(arg_keys[3], (TOKENS, 2), jnp.float32) ** block_scale(arg_keys[3], (TOKENS, 2), ((0, 16),), -0.2, 0.2), 0.099609375, 1.0).astype(jnp.bfloat16)
    capacity_plan = draw_capacity_plan(jax.random.fold_in(arg_keys[7], 71), 0)
    up_weight = bell_draw(arg_keys[5], (EXPERTS, D, FFW), D ** -0.5, 0.0625, ((0, 16), (1, 8)))
    down_weight = bell_draw(arg_keys[6], (EXPERTS, FFW, D), FFW ** -0.5, 0.125, ((0, 16), (2, 8)))
    return {"tokens": tokens, "cotangent": cotangent, "routes": routes, "route_weights": route_weights, "capacity_plan": capacity_plan, "up_weight": up_weight, "down_weight": down_weight}


def slot_layout(routes, capacity_plan):
    blocks = routes.reshape(N_EXPERT, TOK_DEV * 2)
    onehot = (blocks[:, :, None] == jnp.arange(EXPERTS, dtype=jnp.int32)[None, None, :]).astype(jnp.int32)
    earlier = jnp.cumsum(onehot, axis=1) - onehot
    position = jnp.sum(earlier * onehot, axis=2)
    limits = jnp.sum(onehot * capacity_plan[None, None, :], axis=2)
    kept_mask = position < limits
    source = jnp.arange(N_EXPERT, dtype=jnp.int32)[:, None]
    dump_slot = EXPERTS * N_EXPERT * CAP
    flat_slot = jnp.where(kept_mask, (blocks * N_EXPERT + source) * CAP + position, dump_slot)
    return flat_slot.reshape(TOKENS, 2).astype(jnp.int32), kept_mask.reshape(TOKENS, 2)


def reference(tokens, cotangent, routes, route_weights, capacity_plan, up_weight, down_weight):
    flat_slot, kept_mask = slot_layout(routes, capacity_plan)
    total = EXPERTS * N_EXPERT * CAP
    token_ids = jnp.broadcast_to(jnp.arange(TOKENS, dtype=jnp.int32)[:, None], (TOKENS, 2))
    table = jnp.full((total + 1,), TOKENS, jnp.int32).at[flat_slot.reshape(-1)].set(token_ids.reshape(-1))
    weight_table = jnp.zeros((total + 1,), jnp.bfloat16).at[flat_slot.reshape(-1)].set(route_weights.reshape(-1))
    table = table[:total].reshape(EXPERTS, N_EXPERT * CAP)
    weight_table = weight_table[:total].reshape(EXPERTS, N_EXPERT * CAP)
    padded_x = jnp.concatenate([tokens, jnp.zeros((1, D), jnp.bfloat16)], axis=0)
    padded_dy = jnp.concatenate([cotangent, jnp.zeros((1, D), jnp.bfloat16)], axis=0)

    def expert_pass(operands):
        row_ids, slot_weight, up_one, down_one = operands
        rows_x = padded_x[row_ids]
        rows_dy = padded_dy[row_ids]
        pre_act = jnp.dot(rows_x, up_one, preferred_element_type=jnp.float32)
        gate_sig = jax.nn.sigmoid(pre_act)
        hidden = (pre_act * gate_sig).astype(jnp.bfloat16)
        expert_out = jnp.dot(hidden, down_one, preferred_element_type=jnp.float32).astype(jnp.bfloat16)
        grad_rows = (slot_weight.astype(jnp.float32)[:, None] * rows_dy.astype(jnp.float32)).astype(jnp.bfloat16)
        down_grad = jnp.dot(hidden.T, grad_rows, preferred_element_type=jnp.float32).astype(jnp.bfloat16)
        d_hidden = jnp.dot(grad_rows, down_one.T, preferred_element_type=jnp.float32)
        slope = (d_hidden * gate_sig * (1.0 + pre_act * (1.0 - gate_sig))).astype(jnp.bfloat16)
        up_grad = jnp.dot(rows_x.T, slope, preferred_element_type=jnp.float32).astype(jnp.bfloat16)
        row_grad = jnp.dot(slope, up_one.T, preferred_element_type=jnp.float32).astype(jnp.bfloat16)
        return expert_out, row_grad, up_grad, down_grad

    expert_out, row_grad, up_grad, down_grad = lax.map(expert_pass, (table, weight_table, up_weight, down_weight))
    spare = jnp.zeros((1, D), jnp.bfloat16)
    out_flat = jnp.concatenate([expert_out.reshape(total, D), spare], axis=0)
    grad_flat = jnp.concatenate([row_grad.reshape(total, D), spare], axis=0)
    kept_float = kept_mask.astype(jnp.float32)
    scale = kept_float * route_weights.astype(jnp.float32)
    picked = out_flat[flat_slot].astype(jnp.float32)
    layer_out = jnp.sum(scale[:, :, None] * picked, axis=1).astype(jnp.bfloat16)
    picked_grad = grad_flat[flat_slot].astype(jnp.float32)
    token_grad = jnp.sum(kept_float[:, :, None] * picked_grad, axis=1).astype(jnp.bfloat16)
    return layer_out, token_grad, up_grad, down_grad
```

```python
import functools

import jax
import jax.numpy as jnp
from jax import lax
from jax.experimental import pallas as pl
from jax.experimental.pallas import tpu as pltpu
from jax.sharding import PartitionSpec as P

MESH = pl.DeviceIdType.MESH
F32 = jnp.float32
BF16 = jnp.bfloat16
NX = 4
NZ = 4
CAP = 32
SOURCES = tuple((s % NX, (s + s // NX) % NX) for s in range(NX * NX))
CHUNKS = ((0, 4), (4, 12), (12, 16))
ORDER = (
    "P01", "P10", "P00", "P11", "P21", "A01", "B01", "P20", "A10", "A00", "C01", "B10",
    "B00", "A11", "C10", "C00", "B11", "D10", "A21", "C11", "A20", "E10", "B20", "D11",
    "F10", "D00", "G10", "C20", "E11", "B21", "D20", "E00", "F11", "D01", "C21", "G11",
    "E20", "F00", "E01", "D21", "F20", "G00", "F01", "E21", "G20", "F21", "G01", "G21",
)
VMEM_LIMIT = 60 * 1024 * 1024


def contract_last(left, right):
    return lax.dot_general(left, right, (((1,), (1,)), ((), ())), preferred_element_type=F32)


def contract_first(left, right):
    return lax.dot_general(left, right, (((0,), (0,)), ((), ())), preferred_element_type=F32)


def column_tiles(width, tile=512):
    return [(start, min(start + tile, width)) for start in range(0, width, tile)]


def wrap(value, size):
    return lax.rem(value + size, size)


def moe_kernel(
    tokens_hbm, cotangent_hbm, routes, route_weights, plan, up_hbm, down_hbm,
    returned, rows_hbm, acts_hbm, placer, weighted,
    up, down, tokens, cotangent, sent, rows, part, core_out, core_in,
    first_out, first_in, second_out, second_in, acts, results,
    load_sem, own_sem, sent_sem, rows_sem, core_send, core_recv,
    first_send, first_recv, second_send, second_recv,
    near_send, near_recv, far_send, far_recv, mate_send, mate_recv,
    ret_send, ret_recv, store_sem,
):
    expert = lax.axis_index("expert")
    place = lax.axis_index("tensor")
    x, y = lax.div(expert, NX), lax.rem(expert, NX)
    z, core = lax.div(place, 2), lax.rem(place, 2)
    z_next, z_prev, z_far = wrap(z + 1, NZ), wrap(z - 1, NZ), wrap(z + 2, NZ)
    other = 1 - core
    n_tok, features = tokens.shape
    hidden_units = up.shape[1]
    split = ((hidden_units // 128 + 1) // 2) * 128
    tiles = column_tiles(hidden_units)
    half_a, half_b = pl.ds(0, split), pl.ds(split, hidden_units - split)
    n_experts, slots = NX * NX, NX * NX * CAP

    def at_z(which):
        return {"expert": expert, "tensor": which * 2 + core}

    next_chip, prev_chip = at_z(z_next), at_z(z_prev)
    mate = {"expert": expert, "tensor": z * 2 + other}
    owners = [wrap(x - dx, NX) * NX + wrap(y - dy, NX) for dx, dy in SOURCES]
    sources = [wrap(x + dx, NX) * NX + wrap(y + dy, NX) for dx, dy in SOURCES]

    def remote(src, dst, send, recv, device):
        return pltpu.make_async_remote_copy(
            src_ref=src, dst_ref=dst, send_sem=send, recv_sem=recv, device_id=device, device_id_type=MESH
        )

    def await_received(ref, sem):
        remote(ref, ref, sem, sem, mate).wait_recv()

    def await_sent(ref, sem):
        remote(ref, ref, sem, sem, mate).wait_send()

    barrier = pltpu.get_barrier_semaphore()
    load_tokens = pltpu.make_async_copy(tokens_hbm, tokens, load_sem.at[2])
    load_cotangent = pltpu.make_async_copy(cotangent_hbm, cotangent, load_sem.at[3])
    load_up = pltpu.make_async_copy(up_hbm.at[0], up, load_sem.at[0])
    load_down = pltpu.make_async_copy(down_hbm.at[0], down, load_sem.at[1])
    for load in (load_tokens, load_cotangent, load_up, load_down):
        load.start()
    for peer in sources[1:]:
        pl.semaphore_signal(barrier, inc=1, device_id={"expert": peer, "tensor": place}, device_id_type=MESH)
    for device in (next_chip, prev_chip, mate):
        pl.semaphore_signal(barrier, inc=1, device_id=device, device_id_type=MESH)

    expert_id = lax.broadcasted_iota(jnp.int32, (n_experts, n_tok), 0)
    first, second = routes[0:1, :], routes[1:2, :]
    named_first = (expert_id == first).astype(F32)
    named_second = (expert_id == second).astype(F32)
    before = lax.broadcasted_iota(jnp.int32, (n_tok, n_tok), 0) < lax.broadcasted_iota(jnp.int32, (n_tok, n_tok), 1)
    earlier = jnp.dot(
        (named_first + named_second).astype(BF16), before.astype(F32).astype(BF16), preferred_element_type=F32
    )
    limit = jnp.zeros((n_experts, 1), F32)
    expert_one = lax.broadcasted_iota(jnp.int32, (n_experts, 1), 0)
    for which in range(n_experts):
        limit = limit + jnp.where(expert_one == which, plan[which].astype(F32), 0.0)
    slot_id = lax.broadcasted_iota(jnp.int32, (slots, n_tok), 0).astype(F32)
    ones = jnp.zeros((slots, n_tok), F32)
    scaled = jnp.zeros((slots, n_tok), F32)
    pairs = ((first, named_first, earlier), (second, named_second, earlier + named_first))
    for k, (named_id, named, count) in enumerate(pairs):
        position = jnp.sum(count * named, axis=0, keepdims=True)
        allowed = jnp.sum(limit * named, axis=0, keepdims=True)
        slot = jnp.where(position < allowed, named_id.astype(F32) * CAP + position, -1.0)
        hit = slot_id == slot
        ones = ones + jnp.where(hit, 1.0, 0.0)
        scaled = scaled + jnp.where(hit, route_weights[k : k + 1, :].astype(F32), 0.0)
    placer[...] = ones.astype(BF16)
    weighted[...] = scaled.astype(BF16)

    def source_rows(s, count=1):
        return pl.ds(s * CAP, count * CAP)

    def chunk_rows(c):
        lo, hi = CHUNKS[c]
        return pl.ds(lo * CAP, (hi - lo) * CAP)

    def block_size(c):
        lo, hi = CHUNKS[c]
        return (hi - lo) * CAP // (2 * NZ)

    def block(c, side, which, count=1):
        size = block_size(c)
        return pl.ds(pl.multiple_of(CHUNKS[c][0] * CAP + (side * NZ + which) * size, 16), count * size)

    def half_block(c, which, count=1):
        size = block_size(c)
        return pl.ds(pl.multiple_of(CHUNKS[c][0] * CAP // 2 + which * size, 16), count * size)

    def small_block(c):
        return pl.ds(CHUNKS[c][0] * CAP // (2 * NZ), block_size(c))

    def remote_sources(c):
        lo, hi = CHUNKS[c]
        return range(max(lo, 1), hi)

    def make_rows(c, k):
        matrix, picker = ((tokens, placer), (cotangent, weighted))[k]
        for s in range(*CHUNKS[c]):
            pick = pl.ds(pl.multiple_of(owners[s] * CAP, CAP), CAP)
            sent[k, source_rows(s), :] = jnp.dot(
                picker[pick, :], matrix[...], preferred_element_type=F32
            ).astype(BF16)
            if s == 0:
                own_rows(k).start()
            else:
                remote(
                    sent.at[k, source_rows(s)], rows.at[k, source_rows(s)], sent_sem.at[k], rows_sem.at[c, k],
                    {"expert": owners[s], "tensor": place},
                ).start()

    def own_rows(k):
        return pltpu.make_async_copy(sent.at[k, source_rows(0)], rows.at[k, source_rows(0)], own_sem.at[0, k])

    def own_back(k):
        return pltpu.make_async_copy(results.at[k, source_rows(0)], returned.at[k, expert], own_sem.at[1, k])

    def save_acts(c, k):
        return pltpu.make_async_copy(acts.at[k, chunk_rows(c)], acts_hbm.at[k, chunk_rows(c)], store_sem.at[0, c, k])

    def save_rows(k):
        return pltpu.make_async_copy(rows.at[k], rows_hbm.at[k], store_sem.at[1, 0, k])

    partial_order = [(int(step[1]), int(step[2])) for step in ORDER if step[0] == "A"]

    def stage_partial(c, k):
        if c == 0:
            own_rows(k).wait()
        if (c, k) == next((step_c, step_k) for step_c, step_k in partial_order if step_k == k):
            (load_up if k == 0 else load_down).wait()
        arriving = remote_sources(c)
        await_received(rows.at[k, source_rows(arriving[0], len(arriving))], rows_sem.at[c, k])
        taken = rows[k, chunk_rows(c), :]
        for lo, hi in tiles:
            if k == 0:
                product = jnp.dot(taken, up[:, lo:hi], preferred_element_type=F32)
            else:
                product = contract_last(taken, down[lo:hi, :])
            part[k, chunk_rows(c), lo:hi] = product
        away = half_block(c, 0, NZ)
        core_out[k, away, :] = part[k, block(c, other, 0, NZ), :].astype(BF16)
        remote(core_out.at[k, away], core_in.at[k, away], core_send.at[0], core_recv.at[c, k], mate).start()
        if c == len(CHUNKS) - 1:
            save_rows(k).start()

    def chip_sum(c, k, which, half):
        return part[k, block(c, core, which), half] + core_in[k, half_block(c, which), half].astype(F32)

    def send_second(c, k, side, half):
        remote(
            second_out.at[k, side, small_block(c), half], second_in.at[k, side, small_block(c), half],
            second_send.at[0], second_recv.at[c, k], next_chip if side == 0 else prev_chip,
        ).start()

    def stage_core(c, k):
        await_received(core_in.at[k, half_block(c, 0, NZ)], core_recv.at[c, k])
        here = small_block(c)
        for half, device in ((half_a, next_chip), (half_b, prev_chip)):
            first_out[k, here, half] = chip_sum(c, k, z_far, half).astype(BF16)
            remote(
                first_out.at[k, here, half], first_in.at[k, here, half], first_send.at[0], first_recv.at[c, k], device
            ).start()
        second_out[k, 0, here, half_b] = chip_sum(c, k, z_next, half_b).astype(BF16)
        send_second(c, k, 0, half_b)
        second_out[k, 1, here, half_a] = chip_sum(c, k, z_prev, half_a).astype(BF16)
        send_second(c, k, 1, half_a)

    def stage_relay(c, k):
        here = small_block(c)
        await_received(first_in.at[k, here], first_recv.at[c, k])
        for side, which, half in ((0, z_next, half_a), (1, z_prev, half_b)):
            total = chip_sum(c, k, which, half) + first_in[k, here, half].astype(F32)
            second_out[k, side, here, half] = total.astype(BF16)
            send_second(c, k, side, half)

    def stage_activate(c, k):
        here = small_block(c)
        await_received(second_in.at[k, :, here], second_recv.at[c, k])
        total = chip_sum(c, k, z, pl.ds(0, hidden_units))
        total = total + (second_in[k, 0, here, :].astype(F32) + second_in[k, 1, here, :].astype(F32))
        mine = block(c, core, z)
        if k == 0:
            part[0, mine, :] = total
            acts[0, mine, :] = (total * jax.nn.sigmoid(total)).astype(BF16)
        else:
            pre = part[0, mine, :]
            gate = jax.nn.sigmoid(pre)
            acts[1, mine, :] = (total * gate * (1.0 + pre * (1.0 - gate))).astype(BF16)
        ref = acts.at[k, mine]
        remote(ref, ref, near_send.at[0], near_recv.at[c, k], next_chip).start()
        remote(ref, ref, near_send.at[0], near_recv.at[c, k], prev_chip).start()
        remote(ref, ref, mate_send.at[0], mate_recv.at[c, k], mate).start()

    def stage_forward(c, k):
        await_received(acts.at[k, block(c, core, 0, 2)], near_recv.at[c, k])
        for which, half, device in ((z_prev, half_a, next_chip), (z_next, half_b, prev_chip)):
            ref = acts.at[k, block(c, core, which), half]
            remote(ref, ref, far_send.at[0], far_recv.at[c, k], device).start()
        for which in (z_prev, z_next):
            ref = acts.at[k, block(c, core, which)]
            remote(ref, ref, mate_send.at[0], mate_recv.at[c, k], mate).start()

    def stage_last(c, k):
        ref = acts.at[k, block(c, core, z_far)]
        await_received(ref, far_recv.at[c, k])
        remote(ref, ref, mate_send.at[0], mate_recv.at[c, k], mate).start()

    def stage_result(c, k):
        await_received(acts.at[k, block(c, other, 0, NZ)], mate_recv.at[c, k])
        taken = acts[k, chunk_rows(c), :]
        for lo, hi in column_tiles(features):
            if k == 0:
                product = jnp.dot(taken, down[:, lo:hi], preferred_element_type=F32)
            else:
                product = contract_last(taken, up[lo:hi, :])
            results[k, chunk_rows(c), lo:hi] = product.astype(BF16)
        if c == 0:
            own_back(k).start()
        for s in remote_sources(c):
            remote(
                results.at[k, source_rows(s)], returned.at[k, expert], ret_send.at[k], ret_recv.at[k],
                {"expert": sources[s], "tensor": place},
            ).start()
        save_acts(c, k).start()

    stages = {
        "P": make_rows, "A": stage_partial, "B": stage_core, "C": stage_relay, "D": stage_activate,
        "E": stage_forward, "F": stage_last, "G": stage_result,
    }

    load_tokens.wait()
    load_cotangent.wait()
    pl.semaphore_wait(barrier, n_experts - 1 + 3)
    for step in ORDER:
        stages[step[0]](int(step[1]), int(step[2]))

    for k in range(2):
        await_sent(sent.at[k, source_rows(1, n_experts - 1)], sent_sem.at[k])
        save_rows(k).wait()
        own_back(k).wait()
        for c in range(len(CHUNKS)):
            save_acts(c, k).wait()
    quarter = slots // NZ
    await_sent(core_out, core_send.at[0])
    await_sent(first_out, first_send.at[0])
    await_sent(second_out, second_send.at[0])
    await_sent(acts.at[:, pl.ds(0, quarter)], near_send.at[0])
    await_sent(acts.at[:, pl.ds(0, quarter // 2)], far_send.at[0])
    await_sent(acts.at[:, pl.ds(0, 2 * quarter)], mate_send.at[0])
    for k in range(2):
        await_received(returned.at[k, pl.ds(0, n_experts - 1)], ret_recv.at[k])
        await_sent(results.at[k, source_rows(1, n_experts - 1)], ret_send.at[k])


def weight_grad_kernel(
    rows_hbm, acts_hbm, returned_hbm, placer, weighted,
    layer_out, token_grad, up_grad, down_grad,
    rows, acts, returned, flipped, up_tile, down_tile, load_sem, acts_sem, store_sem,
):
    features = rows.shape[-1]
    hidden_units = acts.shape[-1]
    slots = rows.shape[1]
    tiles = column_tiles(hidden_units)
    loads = [pltpu.make_async_copy(rows_hbm.at[kind], rows.at[kind], load_sem.at[kind]) for kind in range(2)]
    loads[0].start()
    acts_loads = [
        [
            pltpu.make_async_copy(acts_hbm.at[kind, :, lo:hi], acts.at[kind, :, lo:hi], acts_sem.at[kind, index])
            for index, (lo, hi) in enumerate(tiles)
        ]
        for kind in range(2)
    ]
    for load in acts_loads[1]:
        load.start()
    loads[1].start()
    for load in acts_loads[0]:
        load.start()
    load_returned = pltpu.make_async_copy(returned_hbm, returned, load_sem.at[2])
    load_returned.start()
    stores = []
    loads[0].wait()
    flipped[...] = rows[0].T
    for index, (lo, hi) in enumerate(tiles):
        acts_loads[1][index].wait()
        up_tile[:, lo:hi] = jnp.dot(flipped[...], acts[1, :, lo:hi], preferred_element_type=F32).astype(BF16)
        store = pltpu.make_async_copy(up_tile.at[:, lo:hi], up_grad.at[0, :, lo:hi], store_sem.at[0, index])
        store.start()
        stores.append(store)
    loads[1].wait()
    for index, (lo, hi) in enumerate(tiles):
        acts_loads[0][index].wait()
        down_tile[lo:hi, :] = contract_first(acts[0, :, lo:hi], rows[1]).astype(BF16)
        store = pltpu.make_async_copy(down_tile.at[lo:hi, :], down_grad.at[0, lo:hi, :], store_sem.at[1, index])
        store.start()
        stores.append(store)
    load_returned.wait()
    layer_out[...] = contract_first(weighted[...], returned[0].reshape(slots, features)).astype(BF16)
    token_grad[...] = contract_first(placer[...], returned[1].reshape(slots, features)).astype(BF16)
    for store in stores:
        store.wait()


def per_device(tokens, cotangent, routes, route_weights, capacity_plan, up_weight, down_weight):
    n_tok, features = tokens.shape
    hidden_units = up_weight.shape[2]
    slots = NX * NX * CAP
    vmem = pl.BlockSpec(memory_space=pltpu.VMEM)
    hbm = pl.BlockSpec(memory_space=pl.ANY)
    dma = pltpu.SemaphoreType.DMA
    flops = 8 * slots * features * hidden_units
    n_chunks = len(CHUNKS)
    returned, rows, acts, placer, weighted = pl.pallas_call(
        moe_kernel,
        out_shape=(
            jax.ShapeDtypeStruct((2, NX * NX, CAP, features), BF16),
            jax.ShapeDtypeStruct((2, slots, features), BF16),
            jax.ShapeDtypeStruct((2, slots, hidden_units), BF16),
            jax.ShapeDtypeStruct((slots, n_tok), BF16),
            jax.ShapeDtypeStruct((slots, n_tok), BF16),
        ),
        in_specs=[hbm, hbm, vmem, vmem, pl.BlockSpec(memory_space=pltpu.SMEM), hbm, hbm],
        out_specs=(hbm, hbm, hbm, vmem, vmem),
        scratch_shapes=[
            pltpu.VMEM((features, hidden_units), BF16),
            pltpu.VMEM((hidden_units, features), BF16),
            pltpu.VMEM((n_tok, features), BF16),
            pltpu.VMEM((n_tok, features), BF16),
            pltpu.VMEM((2, slots, features), BF16),
            pltpu.VMEM((2, slots, features), BF16),
            pltpu.VMEM((2, slots, hidden_units), F32),
            pltpu.VMEM((2, slots // 2, hidden_units), BF16),
            pltpu.VMEM((2, slots // 2, hidden_units), BF16),
            pltpu.VMEM((2, slots // (2 * NZ), hidden_units), BF16),
            pltpu.VMEM((2, slots // (2 * NZ), hidden_units), BF16),
            pltpu.VMEM((2, 2, slots // (2 * NZ), hidden_units), BF16),
            pltpu.VMEM((2, 2, slots // (2 * NZ), hidden_units), BF16),
            pltpu.VMEM((2, slots, hidden_units), BF16),
            pltpu.VMEM((2, slots, features), BF16),
            dma((4,)),
            dma((2, 2)),
            dma((2,)),
            dma((n_chunks, 2)),
            dma((1,)),
            dma((n_chunks, 2)),
            dma((1,)),
            dma((n_chunks, 2)),
            dma((1,)),
            dma((n_chunks, 2)),
            dma((1,)),
            dma((n_chunks, 2)),
            dma((1,)),
            dma((n_chunks, 2)),
            dma((1,)),
            dma((n_chunks, 2)),
            dma((2,)),
            dma((2,)),
            dma((2, n_chunks, 2)),
        ],
        compiler_params=pltpu.CompilerParams(
            collective_id=0, has_side_effects=True, vmem_limit_bytes=VMEM_LIMIT
        ),
        cost_estimate=pl.CostEstimate(
            flops=flops, bytes_accessed=4 * features * hidden_units, transcendentals=slots * hidden_units // 8
        ),
        name="moe_exchange",
    )(tokens, cotangent, routes.T, route_weights.T, capacity_plan, up_weight, down_weight)
    n_tiles = len(column_tiles(hidden_units))
    layer_out, token_grad, up_grad, down_grad = pl.pallas_call(
        weight_grad_kernel,
        out_shape=(
            jax.ShapeDtypeStruct((n_tok, features), BF16),
            jax.ShapeDtypeStruct((n_tok, features), BF16),
            jax.ShapeDtypeStruct((1, features, hidden_units), BF16),
            jax.ShapeDtypeStruct((1, hidden_units, features), BF16),
        ),
        in_specs=[hbm, hbm, hbm, vmem, vmem],
        out_specs=(vmem, vmem, hbm, hbm),
        scratch_shapes=[
            pltpu.VMEM((2, slots, features), BF16),
            pltpu.VMEM((2, slots, hidden_units), BF16),
            pltpu.VMEM((2, NX * NX, CAP, features), BF16),
            pltpu.VMEM((features, slots), BF16),
            pltpu.VMEM((features, hidden_units), BF16),
            pltpu.VMEM((hidden_units, features), BF16),
            dma((3,)),
            dma((2, n_tiles)),
            dma((2, n_tiles)),
        ],
        compiler_params=pltpu.CompilerParams(vmem_limit_bytes=VMEM_LIMIT),
        cost_estimate=pl.CostEstimate(
            flops=flops // 2, bytes_accessed=4 * features * hidden_units, transcendentals=0
        ),
        name="weight_grads",
    )(rows, acts, returned, placer, weighted)
    return layer_out, token_grad, up_grad, down_grad


def solution(mesh):
    placed = (
        P("expert", "tensor"),
        P("expert", "tensor"),
        P("expert", None),
        P("expert", None),
        P(),
        P("expert", "tensor", None),
        P("expert", None, "tensor"),
    )
    return jax.shard_map(
        per_device,
        mesh=mesh,
        in_specs=placed,
        out_specs=(
            P("expert", "tensor"),
            P("expert", "tensor"),
            P("expert", "tensor", None),
            P("expert", None, "tensor"),
        ),
        check_vma=False,
    )
```

```python
import functools

import jax
import jax.numpy as jnp
from jax import lax
from jax.experimental import pallas as pl
from jax.experimental.pallas import tpu as pltpu
from jax.sharding import PartitionSpec as P

MESH = pl.DeviceIdType.MESH
F32 = jnp.float32
BF16 = jnp.bfloat16
NX = 4
NZ = 4
CAP = 32
SOURCES = tuple((s % NX, (s + s // NX) % NX) for s in range(NX * NX))
CHUNKS = ((0, 4), (4, 12), (12, 16))
ORDER = (
    "P01", "P00", "P10", "P11", "A01", "A00", "B01", "B00", "A10", "C00", "P20", "C01",
    "D00", "D01", "E00", "B10", "P21", "C10", "E01", "A11", "D10", "A21", "F01", "E10",
    "B11", "F00", "A20", "F10", "C11", "B21", "G00", "D11", "G01", "G10", "E11", "B20",
    "F11", "C20", "C21", "D20", "D21", "G11", "E21", "X00", "F21", "E20", "F20", "G21",
    "G20",
)
TILE = 512
PIECES = 4
VMEM_LIMIT = 60 * 1024 * 1024
COMBINE_VMEM_LIMIT = 60 * 1024 * 1024


def contract_last(left, right):
    return lax.dot_general(left, right, (((1,), (1,)), ((), ())), preferred_element_type=F32)


def contract_first(left, right):
    return lax.dot_general(left, right, (((0,), (0,)), ((), ())), preferred_element_type=F32)


def column_tiles(width, tile=TILE):
    return [(start, min(start + tile, width)) for start in range(0, width, tile)]


def wrap(value, size):
    return lax.rem(value + size, size)


def moe_kernel(
    tokens_hbm, cotangent_hbm, routes_hbm, weights_hbm, plan_hbm, up_hbm, down_hbm,
    returned, up_grad, down_grad, placer, weighted,
    up, down, flipped, tokens, cotangent, routes, route_weights, plan, sent, rows, part, core_out, core_in,
    first_out, first_in, second_out, second_in, acts, results,
    load_sem, own_sem, sent_sem, rows_sem, core_send, core_recv,
    first_send, first_recv, second_send, second_recv,
    near_send, near_recv, far_send, far_recv, mate_send, mate_recv,
    ret_send, ret_recv, store_sem,
):
    expert = lax.axis_index("expert")
    place = lax.axis_index("tensor")
    x, y = lax.div(expert, NX), lax.rem(expert, NX)
    z, core = lax.div(place, 2), lax.rem(place, 2)
    z_next, z_prev, z_far = wrap(z + 1, NZ), wrap(z - 1, NZ), wrap(z + 2, NZ)
    other = 1 - core
    n_tok, features = tokens.shape
    hidden_units = up.shape[1]
    split = ((hidden_units // 128 + 1) // 2) * 128
    tiles = column_tiles(hidden_units)
    half_a, half_b = pl.ds(0, split), pl.ds(split, hidden_units - split)
    n_experts, slots = NX * NX, NX * NX * CAP

    def at_z(which):
        return {"expert": expert, "tensor": which * 2 + core}

    next_chip, prev_chip = at_z(z_next), at_z(z_prev)
    mate = {"expert": expert, "tensor": z * 2 + other}
    owners = [wrap(x - dx, NX) * NX + wrap(y - dy, NX) for dx, dy in SOURCES]
    sources = [wrap(x + dx, NX) * NX + wrap(y + dy, NX) for dx, dy in SOURCES]

    def remote(src, dst, send, recv, device):
        return pltpu.make_async_remote_copy(
            src_ref=src, dst_ref=dst, send_sem=send, recv_sem=recv, device_id=device, device_id_type=MESH
        )

    def await_received(ref, sem):
        remote(ref, ref, sem, sem, mate).wait_recv()

    def await_sent(ref, sem):
        remote(ref, ref, sem, sem, mate).wait_send()

    barrier = pltpu.get_barrier_semaphore()
    load_tokens = pltpu.make_async_copy(tokens_hbm, tokens, load_sem.at[2])
    load_cotangent = pltpu.make_async_copy(cotangent_hbm, cotangent, load_sem.at[3])
    load_up = pltpu.make_async_copy(up_hbm.at[0], up, load_sem.at[0])
    load_down = pltpu.make_async_copy(down_hbm.at[0], down, load_sem.at[1])
    load_routing = [
        pltpu.make_async_copy(source, target, load_sem.at[4 + which])
        for which, (source, target) in enumerate(
            ((routes_hbm, routes), (weights_hbm, route_weights), (plan_hbm, plan))
        )
    ]
    for load in (*load_routing, load_tokens, load_cotangent, load_up, load_down):
        load.start()
    for peer in sources[1:]:
        pl.semaphore_signal(barrier, inc=1, device_id={"expert": peer, "tensor": place}, device_id_type=MESH)
    for device in (next_chip, prev_chip, mate):
        pl.semaphore_signal(barrier, inc=1, device_id=device, device_id_type=MESH)

    for load in load_routing:
        load.wait()

    expert_id = lax.broadcasted_iota(jnp.int32, (n_experts, n_tok), 0)
    first, second = routes[0:1, :], routes[1:2, :]
    named_first = (expert_id == first).astype(F32)
    named_second = (expert_id == second).astype(F32)
    before = lax.broadcasted_iota(jnp.int32, (n_tok, n_tok), 0) < lax.broadcasted_iota(jnp.int32, (n_tok, n_tok), 1)
    earlier = jnp.dot(
        (named_first + named_second).astype(BF16), before.astype(F32).astype(BF16), preferred_element_type=F32
    )
    diagonal = lax.broadcasted_iota(jnp.int32, (n_experts, n_experts), 0) == lax.broadcasted_iota(
        jnp.int32, (n_experts, n_experts), 1
    )
    limit = jnp.sum(jnp.where(diagonal, plan[...].astype(F32), 0.0), axis=1, keepdims=True)
    slot_id = lax.broadcasted_iota(jnp.int32, (slots, n_tok), 0).astype(F32)
    ones = jnp.zeros((slots, n_tok), F32)
    scaled = jnp.zeros((slots, n_tok), F32)
    pairs = ((first, named_first, earlier), (second, named_second, earlier + named_first))
    for k, (named_id, named, count) in enumerate(pairs):
        position = jnp.sum(count * named, axis=0, keepdims=True)
        allowed = jnp.sum(limit * named, axis=0, keepdims=True)
        slot = jnp.where(position < allowed, named_id.astype(F32) * CAP + position, -1.0)
        hit = slot_id == slot
        ones = ones + jnp.where(hit, 1.0, 0.0)
        scaled = scaled + jnp.where(hit, route_weights[k : k + 1, :].astype(F32), 0.0)
    placer[...] = ones.astype(BF16)
    weighted[...] = scaled.astype(BF16)

    def source_rows(s, count=1):
        return pl.ds(s * CAP, count * CAP)

    def chunk_rows(c):
        lo, hi = CHUNKS[c]
        return pl.ds(lo * CAP, (hi - lo) * CAP)

    def block_size(c):
        lo, hi = CHUNKS[c]
        return (hi - lo) * CAP // (2 * NZ)

    def block(c, side, which, count=1):
        size = block_size(c)
        return pl.ds(pl.multiple_of(CHUNKS[c][0] * CAP + (side * NZ + which) * size, 16), count * size)

    def half_block(c, which, count=1):
        size = block_size(c)
        return pl.ds(pl.multiple_of(CHUNKS[c][0] * CAP // 2 + which * size, 16), count * size)

    def small_block(c):
        return pl.ds(CHUNKS[c][0] * CAP // (2 * NZ), block_size(c))

    def remote_sources(c):
        lo, hi = CHUNKS[c]
        return range(max(lo, 1), hi)

    def make_rows(c, k):
        matrix, picker = ((tokens, placer), (cotangent, weighted))[k]
        for s in range(*CHUNKS[c]):
            pick = pl.ds(pl.multiple_of(owners[s] * CAP, CAP), CAP)
            sent[k, source_rows(s), :] = jnp.dot(
                picker[pick, :], matrix[...], preferred_element_type=F32
            ).astype(BF16)
            if s == 0:
                own_rows(k).start()
            else:
                remote(
                    sent.at[k, source_rows(s)], rows.at[k, source_rows(s)], sent_sem.at[k], rows_sem.at[c, k],
                    {"expert": owners[s], "tensor": place},
                ).start()

    def own_rows(k):
        return pltpu.make_async_copy(sent.at[k, source_rows(0)], rows.at[k, source_rows(0)], own_sem.at[0, k])

    def own_back(k):
        return pltpu.make_async_copy(results.at[k, source_rows(0)], returned.at[k, expert], own_sem.at[1, k])

    partial_order = [(int(step[1]), int(step[2])) for step in ORDER if step[0] == "A"]

    def stage_partial(c, k):
        if c == 0:
            own_rows(k).wait()
        if (c, k) == next((step_c, step_k) for step_c, step_k in partial_order if step_k == k):
            (load_up if k == 0 else load_down).wait()
        arriving = remote_sources(c)
        await_received(rows.at[k, source_rows(arriving[0], len(arriving))], rows_sem.at[c, k])
        taken = rows[k, chunk_rows(c), :]
        for lo, hi in tiles:
            if k == 0:
                product = jnp.dot(taken, up[:, lo:hi], preferred_element_type=F32)
            else:
                product = contract_last(taken, down[lo:hi, :])
            part[k, chunk_rows(c), lo:hi] = product
        away = half_block(c, 0, NZ)
        core_out[k, away, :] = part[k, block(c, other, 0, NZ), :].astype(BF16)
        remote(core_out.at[k, away], core_in.at[k, away], core_send.at[0], core_recv.at[c, k], mate).start()

    def chip_sum(c, k, which, half):
        return part[k, block(c, core, which), half] + core_in[k, half_block(c, which), half].astype(F32)

    def send_second(c, k, side, half):
        remote(
            second_out.at[k, side, small_block(c), half], second_in.at[k, side, small_block(c), half],
            second_send.at[0], second_recv.at[c, k], next_chip if side == 0 else prev_chip,
        ).start()

    def stage_core(c, k):
        await_received(core_in.at[k, half_block(c, 0, NZ)], core_recv.at[c, k])
        here = small_block(c)
        for half, device in ((half_a, next_chip), (half_b, prev_chip)):
            first_out[k, here, half] = chip_sum(c, k, z_far, half).astype(BF16)
            remote(
                first_out.at[k, here, half], first_in.at[k, here, half], first_send.at[0], first_recv.at[c, k], device
            ).start()
        second_out[k, 0, here, half_b] = chip_sum(c, k, z_next, half_b).astype(BF16)
        send_second(c, k, 0, half_b)
        second_out[k, 1, here, half_a] = chip_sum(c, k, z_prev, half_a).astype(BF16)
        send_second(c, k, 1, half_a)

    def stage_relay(c, k):
        here = small_block(c)
        await_received(first_in.at[k, here], first_recv.at[c, k])
        for side, which, half in ((0, z_next, half_a), (1, z_prev, half_b)):
            total = chip_sum(c, k, which, half) + first_in[k, here, half].astype(F32)
            second_out[k, side, here, half] = total.astype(BF16)
            send_second(c, k, side, half)

    def stage_activate(c, k):
        here = small_block(c)
        await_received(second_in.at[k, :, here], second_recv.at[c, k])
        total = chip_sum(c, k, z, pl.ds(0, hidden_units))
        total = total + (second_in[k, 0, here, :].astype(F32) + second_in[k, 1, here, :].astype(F32))
        mine = block(c, core, z)
        if k == 0:
            part[0, mine, :] = total
            acts[0, mine, :] = (total * jax.nn.sigmoid(total)).astype(BF16)
        else:
            pre = part[0, mine, :]
            gate = jax.nn.sigmoid(pre)
            acts[1, mine, :] = (total * gate * (1.0 + pre * (1.0 - gate))).astype(BF16)
        ref = acts.at[k, mine]
        remote(ref, ref, near_send.at[0], near_recv.at[c, k], next_chip).start()
        remote(ref, ref, near_send.at[0], near_recv.at[c, k], prev_chip).start()
        remote(ref, ref, mate_send.at[0], mate_recv.at[c, k], mate).start()

    def stage_forward(c, k):
        await_received(acts.at[k, block(c, core, 0, 2)], near_recv.at[c, k])
        for which, half, device in ((z_prev, half_a, next_chip), (z_next, half_b, prev_chip)):
            ref = acts.at[k, block(c, core, which), half]
            remote(ref, ref, far_send.at[0], far_recv.at[c, k], device).start()
        for which in (z_prev, z_next):
            ref = acts.at[k, block(c, core, which)]
            remote(ref, ref, mate_send.at[0], mate_recv.at[c, k], mate).start()

    def stage_last(c, k):
        ref = acts.at[k, block(c, core, z_far)]
        await_received(ref, far_recv.at[c, k])
        remote(ref, ref, mate_send.at[0], mate_recv.at[c, k], mate).start()

    def stage_result(c, k):
        await_received(acts.at[k, block(c, other, 0, NZ)], mate_recv.at[c, k])
        taken = acts[k, chunk_rows(c), :]
        for lo, hi in column_tiles(features):
            if k == 0:
                product = jnp.dot(taken, down[:, lo:hi], preferred_element_type=F32)
            else:
                product = contract_last(taken, up[lo:hi, :])
            results[k, chunk_rows(c), lo:hi] = product.astype(BF16)
        if c == 0:
            own_back(k).start()
        for s in remote_sources(c):
            remote(
                results.at[k, source_rows(s)], returned.at[k, expert], ret_send.at[k], ret_recv.at[k],
                {"expert": sources[s], "tensor": place},
            ).start()

    def stage_flip(c, k):
        flipped[...] = rows[0].T

    def make_up_grad(pick):
        up[:, pick] = jnp.dot(flipped[...], acts[1, :, pick], preferred_element_type=F32).astype(BF16)
        pltpu.make_async_copy(up.at[:, pick], up_grad.at[0, :, pick], store_sem.at[0]).start()

    def make_down_grad(pick):
        down[pick, :] = contract_first(acts[0, :, pick], rows[1]).astype(BF16)
        pltpu.make_async_copy(down.at[pick], down_grad.at[0, pick], store_sem.at[1]).start()

    def make_weight_grads():
        whole = hidden_units // TILE
        rest = pl.ds(whole * TILE, hidden_units - whole * TILE)
        for make in (make_up_grad, make_down_grad):

            def body(t, carry, make=make):
                make(pl.ds(pl.multiple_of(t * TILE, TILE), TILE))
                return carry

            lax.fori_loop(0, whole, body, 0)
            make(rest)

    stages = {
        "P": make_rows, "A": stage_partial, "B": stage_core, "C": stage_relay, "D": stage_activate,
        "E": stage_forward, "F": stage_last, "G": stage_result, "X": stage_flip,
    }

    load_tokens.wait()
    load_cotangent.wait()
    pl.semaphore_wait(barrier, n_experts - 1 + 3)
    for step in ORDER:
        stages[step[0]](int(step[1]), int(step[2]))
    make_weight_grads()

    for k in range(2):
        await_sent(sent.at[k, source_rows(1, n_experts - 1)], sent_sem.at[k])
        own_back(k).wait()
    quarter = slots // NZ
    await_sent(core_out, core_send.at[0])
    await_sent(first_out, first_send.at[0])
    await_sent(second_out, second_send.at[0])
    await_sent(acts.at[:, pl.ds(0, quarter)], near_send.at[0])
    await_sent(acts.at[:, pl.ds(0, quarter // 2)], far_send.at[0])
    await_sent(acts.at[:, pl.ds(0, 2 * quarter)], mate_send.at[0])
    for k in range(2):
        await_received(returned.at[k, pl.ds(0, n_experts - 1)], ret_recv.at[k])
        await_sent(results.at[k, source_rows(1, n_experts - 1)], ret_send.at[k])
    pltpu.make_async_copy(up, up_grad.at[0], store_sem.at[0]).wait()
    pltpu.make_async_copy(down, down_grad.at[0], store_sem.at[1]).wait()


def combine_kernel(
    returned_hbm, placer_hbm, weighted_hbm, up_hbm, down_hbm,
    layer_hbm, token_hbm, up_grad, down_grad,
    returned, placer, weighted, layer_out, token_grad, up, down, load_sem, out_sem, in_sem, copy_sem,
):
    slots, features = placer.shape[0], layer_out.shape[1]
    first = [
        pltpu.make_async_copy(weighted_hbm, weighted, load_sem.at[0]),
        pltpu.make_async_copy(returned_hbm.at[0], returned.at[0], load_sem.at[1]),
    ]
    second = [
        pltpu.make_async_copy(placer_hbm, placer, load_sem.at[2]),
        pltpu.make_async_copy(returned_hbm.at[1], returned.at[1], load_sem.at[3]),
    ]
    pieces = []
    for which, (source, between, target) in enumerate(((up_hbm, up, up_grad), (down_hbm, down, down_grad))):
        size = between.shape[0] // PIECES
        for piece in range(PIECES):
            pick = pl.ds(piece * size, size)
            pieces.append(
                (
                    pltpu.make_async_copy(source.at[0, pick], between.at[pick], in_sem.at[which, piece]),
                    pltpu.make_async_copy(between.at[pick], target.at[0, pick], copy_sem.at[which, piece]),
                )
            )
    outs = [
        pltpu.make_async_copy(layer_out, layer_hbm, out_sem.at[0]),
        pltpu.make_async_copy(token_grad, token_hbm, out_sem.at[1]),
    ]
    for load in (pieces[0][0], *first, pieces[1][0], *second, *(piece[0] for piece in pieces[2:])):
        load.start()

    def pass_on(some):
        for load, store in some:
            load.wait()
            store.start()

    pass_on(pieces[:1])
    for load in first:
        load.wait()
    layer_out[...] = contract_first(weighted[...], returned[0].reshape(slots, features)).astype(BF16)
    outs[0].start()
    pass_on(pieces[1:2])
    for load in second:
        load.wait()
    token_grad[...] = contract_first(placer[...], returned[1].reshape(slots, features)).astype(BF16)
    outs[1].start()
    pass_on(pieces[2:])
    for copy in (*outs, *(piece[1] for piece in pieces)):
        copy.wait()


def per_device(tokens, cotangent, routes, route_weights, capacity_plan, up_weight, down_weight):
    n_tok, features = tokens.shape
    hidden_units = up_weight.shape[2]
    slots = NX * NX * CAP
    vmem = pl.BlockSpec(memory_space=pltpu.VMEM)
    hbm = pl.BlockSpec(memory_space=pl.ANY)
    dma = pltpu.SemaphoreType.DMA
    flops = 12 * slots * features * hidden_units
    n_chunks = len(CHUNKS)
    returned, up_made, down_made, placer, weighted = pl.pallas_call(
        moe_kernel,
        out_shape=(
            jax.ShapeDtypeStruct((2, NX * NX, CAP, features), BF16),
            jax.ShapeDtypeStruct((1, features, hidden_units), BF16),
            jax.ShapeDtypeStruct((1, hidden_units, features), BF16),
            jax.ShapeDtypeStruct((slots, n_tok), BF16),
            jax.ShapeDtypeStruct((slots, n_tok), BF16),
        ),
        in_specs=[pl.BlockSpec(memory_space=pltpu.HBM)] * 7,
        out_specs=(hbm, hbm, hbm, vmem, vmem),
        scratch_shapes=[
            pltpu.VMEM((features, hidden_units), BF16),
            pltpu.VMEM((hidden_units, features), BF16),
            pltpu.VMEM((features, slots), BF16),
            pltpu.VMEM((n_tok, features), BF16),
            pltpu.VMEM((n_tok, features), BF16),
            pltpu.VMEM((2, n_tok), jnp.int32),
            pltpu.VMEM((2, n_tok), BF16),
            pltpu.VMEM((1, NX * NX), jnp.int32),
            pltpu.VMEM((2, slots, features), BF16),
            pltpu.VMEM((2, slots, features), BF16),
            pltpu.VMEM((2, slots, hidden_units), F32),
            pltpu.VMEM((2, slots // 2, hidden_units), BF16),
            pltpu.VMEM((2, slots // 2, hidden_units), BF16),
            pltpu.VMEM((2, slots // (2 * NZ), hidden_units), BF16),
            pltpu.VMEM((2, slots // (2 * NZ), hidden_units), BF16),
            pltpu.VMEM((2, 2, slots // (2 * NZ), hidden_units), BF16),
            pltpu.VMEM((2, 2, slots // (2 * NZ), hidden_units), BF16),
            pltpu.VMEM((2, slots, hidden_units), BF16),
            pltpu.VMEM((2, slots, features), BF16),
            dma((7,)),
            dma((2, 2)),
            dma((2,)),
            dma((n_chunks, 2)),
            dma((1,)),
            dma((n_chunks, 2)),
            dma((1,)),
            dma((n_chunks, 2)),
            dma((1,)),
            dma((n_chunks, 2)),
            dma((1,)),
            dma((n_chunks, 2)),
            dma((1,)),
            dma((n_chunks, 2)),
            dma((1,)),
            dma((n_chunks, 2)),
            dma((2,)),
            dma((2,)),
            dma((2,)),
        ],
        compiler_params=pltpu.CompilerParams(
            collective_id=0, has_side_effects=True, vmem_limit_bytes=VMEM_LIMIT
        ),
        cost_estimate=pl.CostEstimate(
            flops=flops, bytes_accessed=4 * features * hidden_units, transcendentals=slots * hidden_units // 8
        ),
        name="moe_exchange",
    )(tokens, cotangent, routes.T, route_weights.T, capacity_plan[None], up_weight, down_weight)
    return pl.pallas_call(
        combine_kernel,
        out_shape=(
            jax.ShapeDtypeStruct((n_tok, features), BF16),
            jax.ShapeDtypeStruct((n_tok, features), BF16),
            jax.ShapeDtypeStruct((1, features, hidden_units), BF16),
            jax.ShapeDtypeStruct((1, hidden_units, features), BF16),
        ),
        in_specs=[hbm] * 5,
        out_specs=(hbm,) * 4,
        scratch_shapes=[
            pltpu.VMEM((2, NX * NX, CAP, features), BF16),
            pltpu.VMEM((slots, n_tok), BF16),
            pltpu.VMEM((slots, n_tok), BF16),
            pltpu.VMEM((n_tok, features), BF16),
            pltpu.VMEM((n_tok, features), BF16),
            pltpu.VMEM((features, hidden_units), BF16),
            pltpu.VMEM((hidden_units, features), BF16),
            dma((4,)),
            dma((2,)),
            dma((2, PIECES)),
            dma((2, PIECES)),
        ],
        compiler_params=pltpu.CompilerParams(vmem_limit_bytes=COMBINE_VMEM_LIMIT),
        cost_estimate=pl.CostEstimate(
            flops=4 * slots * n_tok * features, bytes_accessed=8 * features * hidden_units, transcendentals=0
        ),
        name="combine",
    )(returned, placer, weighted, up_made, down_made)


def solution(mesh):
    placed = (
        P("expert", "tensor"),
        P("expert", "tensor"),
        P("expert", None),
        P("expert", None),
        P(),
        P("expert", "tensor", None),
        P("expert", None, "tensor"),
    )
    return jax.shard_map(
        per_device,
        mesh=mesh,
        in_specs=placed,
        out_specs=(
            P("expert", "tensor"),
            P("expert", "tensor"),
            P("expert", "tensor", None),
            P("expert", None, "tensor"),
        ),
        check_vma=False,
    )
```

```python
import functools

import jax
import jax.numpy as jnp
from jax import lax
from jax.experimental import pallas as pl
from jax.experimental.pallas import tpu as pltpu
from jax.sharding import PartitionSpec as P

MESH = pl.DeviceIdType.MESH
F32 = jnp.float32
BF16 = jnp.bfloat16
NX = 4
NZ = 4
CAP = 32
SOURCES = tuple((s % NX, (s + s // NX) % NX) for s in range(NX * NX))
CHUNKS = ((0, 4), (4, 12), (12, 16))
ORDER = (
    "P01", "P00", "P10", "A01", "B01", "P11", "C01", "A00", "A10", "B10", "B00", "P20",
    "C10", "A11", "B11", "D10", "C11", "A20", "P21", "B20", "E10", "D11", "C00", "A21",
    "F10", "B21", "C20", "E11", "G10", "D00", "D20", "F11", "D01", "C21", "G11", "E20",
    "E00", "E01", "D21", "F20", "G20", "F01", "E21", "X00", "F00", "G01", "G00", "F21",
    "G21",
)
TILE = 512
PIECES = 4
VMEM_LIMIT = 60 * 1024 * 1024
COMBINE_VMEM_LIMIT = 60 * 1024 * 1024


def contract_last(left, right):
    return lax.dot_general(left, right, (((1,), (1,)), ((), ())), preferred_element_type=F32)


def contract_first(left, right):
    return lax.dot_general(left, right, (((0,), (0,)), ((), ())), preferred_element_type=F32)


def column_tiles(width, tile=TILE):
    return [(start, min(start + tile, width)) for start in range(0, width, tile)]


def wrap(value, size):
    return lax.rem(value + size, size)


def moe_kernel(
    tokens_hbm, cotangent_hbm, routes_hbm, weights_hbm, plan_hbm, up_hbm, down_hbm,
    returned, up_grad, down_grad, placer, weighted,
    up, down, flipped, tokens, cotangent, routes, route_weights, plan, sent, rows, part, core_out, core_in,
    first_out, first_in, second_out, second_in, acts, results,
    load_sem, own_sem, sent_sem, rows_sem, core_send, core_recv,
    first_send, first_recv, second_send, second_recv,
    near_send, near_recv, far_send, far_recv, mate_send, mate_recv,
    ret_send, ret_recv, store_sem,
):
    expert = lax.axis_index("expert")
    place = lax.axis_index("tensor")
    x, y = lax.div(expert, NX), lax.rem(expert, NX)
    z, core = lax.div(place, 2), lax.rem(place, 2)
    z_next, z_prev, z_far = wrap(z + 1, NZ), wrap(z - 1, NZ), wrap(z + 2, NZ)
    other = 1 - core
    n_tok, features = tokens.shape
    hidden_units = up.shape[1]
    split = ((hidden_units // 128 + 1) // 2) * 128
    tiles = column_tiles(hidden_units)
    half_a, half_b = pl.ds(0, split), pl.ds(split, hidden_units - split)
    n_experts, slots = NX * NX, NX * NX * CAP

    def at_z(which):
        return {"expert": expert, "tensor": which * 2 + core}

    next_chip, prev_chip = at_z(z_next), at_z(z_prev)
    mate = {"expert": expert, "tensor": z * 2 + other}
    owners = [wrap(x - dx, NX) * NX + wrap(y - dy, NX) for dx, dy in SOURCES]
    sources = [wrap(x + dx, NX) * NX + wrap(y + dy, NX) for dx, dy in SOURCES]

    def remote(src, dst, send, recv, device):
        return pltpu.make_async_remote_copy(
            src_ref=src, dst_ref=dst, send_sem=send, recv_sem=recv, device_id=device, device_id_type=MESH
        )

    def await_received(ref, sem):
        remote(ref, ref, sem, sem, mate).wait_recv()

    def await_sent(ref, sem):
        remote(ref, ref, sem, sem, mate).wait_send()

    barrier = pltpu.get_barrier_semaphore()
    load_tokens = pltpu.make_async_copy(tokens_hbm, tokens, load_sem.at[2])
    load_cotangent = pltpu.make_async_copy(cotangent_hbm, cotangent, load_sem.at[3])
    load_up = pltpu.make_async_copy(up_hbm.at[0], up, load_sem.at[0])
    load_down = pltpu.make_async_copy(down_hbm.at[0], down, load_sem.at[1])
    load_routing = [
        pltpu.make_async_copy(source, target, load_sem.at[4 + which])
        for which, (source, target) in enumerate(
            ((routes_hbm, routes), (weights_hbm, route_weights), (plan_hbm, plan))
        )
    ]
    for load in (*load_routing, load_tokens, load_cotangent, load_up, load_down):
        load.start()
    for peer in sources[1:]:
        pl.semaphore_signal(barrier, inc=1, device_id={"expert": peer, "tensor": place}, device_id_type=MESH)
    for device in (next_chip, prev_chip, mate):
        pl.semaphore_signal(barrier, inc=1, device_id=device, device_id_type=MESH)

    for load in load_routing:
        load.wait()

    expert_id = lax.broadcasted_iota(jnp.int32, (n_experts, n_tok), 0)
    first, second = routes[0:1, :], routes[1:2, :]
    named_first = (expert_id == first).astype(F32)
    named_second = (expert_id == second).astype(F32)
    before = lax.broadcasted_iota(jnp.int32, (n_tok, n_tok), 0) < lax.broadcasted_iota(jnp.int32, (n_tok, n_tok), 1)
    earlier = jnp.dot(
        (named_first + named_second).astype(BF16), before.astype(F32).astype(BF16), preferred_element_type=F32
    )
    diagonal = lax.broadcasted_iota(jnp.int32, (n_experts, n_experts), 0) == lax.broadcasted_iota(
        jnp.int32, (n_experts, n_experts), 1
    )
    limit = jnp.sum(jnp.where(diagonal, plan[...].astype(F32), 0.0), axis=1, keepdims=True)
    slot_id = lax.broadcasted_iota(jnp.int32, (slots, n_tok), 0).astype(F32)
    ones = jnp.zeros((slots, n_tok), F32)
    scaled = jnp.zeros((slots, n_tok), F32)
    pairs = ((first, named_first, earlier), (second, named_second, earlier + named_first))
    for k, (named_id, named, count) in enumerate(pairs):
        position = jnp.sum(count * named, axis=0, keepdims=True)
        allowed = jnp.sum(limit * named, axis=0, keepdims=True)
        slot = jnp.where(position < allowed, named_id.astype(F32) * CAP + position, -1.0)
        hit = slot_id == slot
        ones = ones + jnp.where(hit, 1.0, 0.0)
        scaled = scaled + jnp.where(hit, route_weights[k : k + 1, :].astype(F32), 0.0)
    placer[...] = ones.astype(BF16)
    weighted[...] = scaled.astype(BF16)

    def source_rows(s, count=1):
        return pl.ds(s * CAP, count * CAP)

    def chunk_rows(c):
        lo, hi = CHUNKS[c]
        return pl.ds(lo * CAP, (hi - lo) * CAP)

    def block_size(c):
        lo, hi = CHUNKS[c]
        return (hi - lo) * CAP // (2 * NZ)

    def block(c, side, which, count=1):
        size = block_size(c)
        return pl.ds(pl.multiple_of(CHUNKS[c][0] * CAP + (side * NZ + which) * size, 16), count * size)

    def half_block(c, which, count=1):
        size = block_size(c)
        return pl.ds(pl.multiple_of(CHUNKS[c][0] * CAP // 2 + which * size, 16), count * size)

    def small_block(c):
        return pl.ds(CHUNKS[c][0] * CAP // (2 * NZ), block_size(c))

    def remote_sources(c):
        lo, hi = CHUNKS[c]
        return range(max(lo, 1), hi)

    def make_rows(c, k):
        matrix, picker = ((tokens, placer), (cotangent, weighted))[k]
        for s in range(*CHUNKS[c]):
            pick = pl.ds(pl.multiple_of(owners[s] * CAP, CAP), CAP)
            sent[k, source_rows(s), :] = jnp.dot(
                picker[pick, :], matrix[...], preferred_element_type=F32
            ).astype(BF16)
            if s == 0:
                own_rows(k).start()
            else:
                remote(
                    sent.at[k, source_rows(s)], rows.at[k, source_rows(s)], sent_sem.at[k], rows_sem.at[c, k],
                    {"expert": owners[s], "tensor": place},
                ).start()

    def own_rows(k):
        return pltpu.make_async_copy(sent.at[k, source_rows(0)], rows.at[k, source_rows(0)], own_sem.at[0, k])

    def own_back(k):
        return pltpu.make_async_copy(results.at[k, source_rows(0)], returned.at[k, expert], own_sem.at[1, k])

    partial_order = [(int(step[1]), int(step[2])) for step in ORDER if step[0] == "A"]

    def stage_partial(c, k):
        if c == 0:
            own_rows(k).wait()
        if (c, k) == next((step_c, step_k) for step_c, step_k in partial_order if step_k == k):
            (load_up if k == 0 else load_down).wait()
        arriving = remote_sources(c)
        await_received(rows.at[k, source_rows(arriving[0], len(arriving))], rows_sem.at[c, k])
        taken = rows[k, chunk_rows(c), :]
        for lo, hi in tiles:
            if k == 0:
                product = jnp.dot(taken, up[:, lo:hi], preferred_element_type=F32)
            else:
                product = contract_last(taken, down[lo:hi, :])
            part[k, chunk_rows(c), lo:hi] = product
        away = half_block(c, 0, NZ)
        core_out[k, away, :] = part[k, block(c, other, 0, NZ), :].astype(BF16)
        remote(core_out.at[k, away], core_in.at[k, away], core_send.at[0], core_recv.at[c, k], mate).start()

    def chip_sum(c, k, which, half):
        return part[k, block(c, core, which), half] + core_in[k, half_block(c, which), half].astype(F32)

    def send_second(c, k, side, half):
        remote(
            second_out.at[k, side, small_block(c), half], second_in.at[k, side, small_block(c), half],
            second_send.at[0], second_recv.at[c, k], next_chip if side == 0 else prev_chip,
        ).start()

    def stage_core(c, k):
        await_received(core_in.at[k, half_block(c, 0, NZ)], core_recv.at[c, k])
        here = small_block(c)
        for half, device in ((half_a, next_chip), (half_b, prev_chip)):
            first_out[k, here, half] = chip_sum(c, k, z_far, half).astype(BF16)
            remote(
                first_out.at[k, here, half], first_in.at[k, here, half], first_send.at[0], first_recv.at[c, k], device
            ).start()
        second_out[k, 0, here, half_b] = chip_sum(c, k, z_next, half_b).astype(BF16)
        send_second(c, k, 0, half_b)
        second_out[k, 1, here, half_a] = chip_sum(c, k, z_prev, half_a).astype(BF16)
        send_second(c, k, 1, half_a)

    def stage_relay(c, k):
        here = small_block(c)
        await_received(first_in.at[k, here], first_recv.at[c, k])
        for side, which, half in ((0, z_next, half_a), (1, z_prev, half_b)):
            total = chip_sum(c, k, which, half) + first_in[k, here, half].astype(F32)
            second_out[k, side, here, half] = total.astype(BF16)
            send_second(c, k, side, half)

    def stage_activate(c, k):
        here = small_block(c)
        await_received(second_in.at[k, :, here], second_recv.at[c, k])
        total = chip_sum(c, k, z, pl.ds(0, hidden_units))
        total = total + (second_in[k, 0, here, :].astype(F32) + second_in[k, 1, here, :].astype(F32))
        mine = block(c, core, z)
        if k == 0:
            part[0, mine, :] = total
            acts[0, mine, :] = (total * jax.nn.sigmoid(total)).astype(BF16)
        else:
            pre = part[0, mine, :]
            gate = jax.nn.sigmoid(pre)
            acts[1, mine, :] = (total * gate * (1.0 + pre * (1.0 - gate))).astype(BF16)
        ref = acts.at[k, mine]
        remote(ref, ref, near_send.at[0], near_recv.at[c, k], next_chip).start()
        remote(ref, ref, near_send.at[0], near_recv.at[c, k], prev_chip).start()

    def stage_forward(c, k):
        await_received(acts.at[k, block(c, core, 0, 2)], near_recv.at[c, k])
        for which, half, device in ((z_prev, half_a, next_chip), (z_next, half_b, prev_chip)):
            ref = acts.at[k, block(c, core, which), half]
            remote(ref, ref, far_send.at[0], far_recv.at[c, k], device).start()

    def stage_last(c, k):
        await_received(acts.at[k, block(c, core, z_far)], far_recv.at[c, k])
        ref = acts.at[k, block(c, core, 0, NZ)]
        remote(ref, ref, mate_send.at[0], mate_recv.at[c, k], mate).start()

    def stage_result(c, k):
        await_received(acts.at[k, block(c, other, 0, NZ)], mate_recv.at[c, k])
        taken = acts[k, chunk_rows(c), :]
        for lo, hi in column_tiles(features):
            if k == 0:
                product = jnp.dot(taken, down[:, lo:hi], preferred_element_type=F32)
            else:
                product = contract_last(taken, up[lo:hi, :])
            results[k, chunk_rows(c), lo:hi] = product.astype(BF16)
        if c == 0:
            own_back(k).start()
        for s in remote_sources(c):
            remote(
                results.at[k, source_rows(s)], returned.at[k, expert], ret_send.at[k], ret_recv.at[k],
                {"expert": sources[s], "tensor": place},
            ).start()

    def stage_flip(c, k):
        flipped[...] = rows[0].T

    def make_up_grad(pick):
        up[:, pick] = jnp.dot(flipped[...], acts[1, :, pick], preferred_element_type=F32).astype(BF16)
        pltpu.make_async_copy(up.at[:, pick], up_grad.at[0, :, pick], store_sem.at[0]).start()

    def make_down_grad(pick):
        down[pick, :] = contract_first(acts[0, :, pick], rows[1]).astype(BF16)
        pltpu.make_async_copy(down.at[pick], down_grad.at[0, pick], store_sem.at[1]).start()

    def make_weight_grads():
        whole = hidden_units // TILE
        rest = pl.ds(whole * TILE, hidden_units - whole * TILE)
        for make in (make_up_grad, make_down_grad):

            def body(t, carry, make=make):
                make(pl.ds(pl.multiple_of(t * TILE, TILE), TILE))
                return carry

            lax.fori_loop(0, whole, body, 0)
            make(rest)

    stages = {
        "P": make_rows, "A": stage_partial, "B": stage_core, "C": stage_relay, "D": stage_activate,
        "E": stage_forward, "F": stage_last, "G": stage_result, "X": stage_flip,
    }

    load_tokens.wait()
    load_cotangent.wait()
    pl.semaphore_wait(barrier, n_experts - 1 + 3)
    for step in ORDER:
        stages[step[0]](int(step[1]), int(step[2]))
    make_weight_grads()

    for k in range(2):
        await_sent(sent.at[k, source_rows(1, n_experts - 1)], sent_sem.at[k])
        own_back(k).wait()
    quarter = slots // NZ
    await_sent(core_out, core_send.at[0])
    await_sent(first_out, first_send.at[0])
    await_sent(second_out, second_send.at[0])
    await_sent(acts.at[:, pl.ds(0, quarter)], near_send.at[0])
    await_sent(acts.at[:, pl.ds(0, quarter // 2)], far_send.at[0])
    await_sent(acts.at[:, pl.ds(0, 2 * quarter)], mate_send.at[0])
    for k in range(2):
        await_received(returned.at[k, pl.ds(0, n_experts - 1)], ret_recv.at[k])
        await_sent(results.at[k, source_rows(1, n_experts - 1)], ret_send.at[k])
    pltpu.make_async_copy(up, up_grad.at[0], store_sem.at[0]).wait()
    pltpu.make_async_copy(down, down_grad.at[0], store_sem.at[1]).wait()


def combine_kernel(
    returned_hbm, placer_hbm, weighted_hbm, up_hbm, down_hbm,
    layer_hbm, token_hbm, up_grad, down_grad,
    returned, placer, weighted, layer_out, token_grad, up, down, load_sem, out_sem, in_sem, copy_sem,
):
    slots, features = placer.shape[0], layer_out.shape[1]
    first = [
        pltpu.make_async_copy(weighted_hbm, weighted, load_sem.at[0]),
        pltpu.make_async_copy(returned_hbm.at[0], returned.at[0], load_sem.at[1]),
    ]
    second = [
        pltpu.make_async_copy(placer_hbm, placer, load_sem.at[2]),
        pltpu.make_async_copy(returned_hbm.at[1], returned.at[1], load_sem.at[3]),
    ]
    pieces = []
    for which, (source, between, target) in enumerate(((up_hbm, up, up_grad), (down_hbm, down, down_grad))):
        size = between.shape[0] // PIECES
        for piece in range(PIECES):
            pick = pl.ds(piece * size, size)
            pieces.append(
                (
                    pltpu.make_async_copy(source.at[0, pick], between.at[pick], in_sem.at[which, piece]),
                    pltpu.make_async_copy(between.at[pick], target.at[0, pick], copy_sem.at[which, piece]),
                )
            )
    outs = [
        pltpu.make_async_copy(layer_out, layer_hbm, out_sem.at[0]),
        pltpu.make_async_copy(token_grad, token_hbm, out_sem.at[1]),
    ]
    for load in (pieces[0][0], *first, pieces[1][0], *second, *(piece[0] for piece in pieces[2:])):
        load.start()

    def pass_on(some):
        for load, store in some:
            load.wait()
            store.start()

    pass_on(pieces[:1])
    for load in first:
        load.wait()
    layer_out[...] = contract_first(weighted[...], returned[0].reshape(slots, features)).astype(BF16)
    outs[0].start()
    pass_on(pieces[1:2])
    for load in second:
        load.wait()
    token_grad[...] = contract_first(placer[...], returned[1].reshape(slots, features)).astype(BF16)
    outs[1].start()
    pass_on(pieces[2:])
    for copy in (*outs, *(piece[1] for piece in pieces)):
        copy.wait()


def per_device(tokens, cotangent, routes, route_weights, capacity_plan, up_weight, down_weight):
    n_tok, features = tokens.shape
    hidden_units = up_weight.shape[2]
    slots = NX * NX * CAP
    vmem = pl.BlockSpec(memory_space=pltpu.VMEM)
    hbm = pl.BlockSpec(memory_space=pl.ANY)
    dma = pltpu.SemaphoreType.DMA
    flops = 12 * slots * features * hidden_units
    n_chunks = len(CHUNKS)
    returned, up_made, down_made, placer, weighted = pl.pallas_call(
        moe_kernel,
        out_shape=(
            jax.ShapeDtypeStruct((2, NX * NX, CAP, features), BF16),
            jax.ShapeDtypeStruct((1, features, hidden_units), BF16),
            jax.ShapeDtypeStruct((1, hidden_units, features), BF16),
            jax.ShapeDtypeStruct((slots, n_tok), BF16),
            jax.ShapeDtypeStruct((slots, n_tok), BF16),
        ),
        in_specs=[pl.BlockSpec(memory_space=pltpu.HBM)] * 7,
        out_specs=(hbm, hbm, hbm, vmem, vmem),
        scratch_shapes=[
            pltpu.VMEM((features, hidden_units), BF16),
            pltpu.VMEM((hidden_units, features), BF16),
            pltpu.VMEM((features, slots), BF16),
            pltpu.VMEM((n_tok, features), BF16),
            pltpu.VMEM((n_tok, features), BF16),
            pltpu.VMEM((2, n_tok), jnp.int32),
            pltpu.VMEM((2, n_tok), BF16),
            pltpu.VMEM((1, NX * NX), jnp.int32),
            pltpu.VMEM((2, slots, features), BF16),
            pltpu.VMEM((2, slots, features), BF16),
            pltpu.VMEM((2, slots, hidden_units), F32),
            pltpu.VMEM((2, slots // 2, hidden_units), BF16),
            pltpu.VMEM((2, slots // 2, hidden_units), BF16),
            pltpu.VMEM((2, slots // (2 * NZ), hidden_units), BF16),
            pltpu.VMEM((2, slots // (2 * NZ), hidden_units), BF16),
            pltpu.VMEM((2, 2, slots // (2 * NZ), hidden_units), BF16),
            pltpu.VMEM((2, 2, slots // (2 * NZ), hidden_units), BF16),
            pltpu.VMEM((2, slots, hidden_units), BF16),
            pltpu.VMEM((2, slots, features), BF16),
            dma((7,)),
            dma((2, 2)),
            dma((2,)),
            dma((n_chunks, 2)),
            dma((1,)),
            dma((n_chunks, 2)),
            dma((1,)),
            dma((n_chunks, 2)),
            dma((1,)),
            dma((n_chunks, 2)),
            dma((1,)),
            dma((n_chunks, 2)),
            dma((1,)),
            dma((n_chunks, 2)),
            dma((1,)),
            dma((n_chunks, 2)),
            dma((2,)),
            dma((2,)),
            dma((2,)),
        ],
        compiler_params=pltpu.CompilerParams(
            collective_id=0, has_side_effects=True, vmem_limit_bytes=VMEM_LIMIT
        ),
        cost_estimate=pl.CostEstimate(
            flops=flops, bytes_accessed=4 * features * hidden_units, transcendentals=slots * hidden_units // 8
        ),
        name="moe_exchange",
    )(tokens, cotangent, routes.T, route_weights.T, capacity_plan[None], up_weight, down_weight)
    return pl.pallas_call(
        combine_kernel,
        out_shape=(
            jax.ShapeDtypeStruct((n_tok, features), BF16),
            jax.ShapeDtypeStruct((n_tok, features), BF16),
            jax.ShapeDtypeStruct((1, features, hidden_units), BF16),
            jax.ShapeDtypeStruct((1, hidden_units, features), BF16),
        ),
        in_specs=[hbm] * 5,
        out_specs=(hbm,) * 4,
        scratch_shapes=[
            pltpu.VMEM((2, NX * NX, CAP, features), BF16),
            pltpu.VMEM((slots, n_tok), BF16),
            pltpu.VMEM((slots, n_tok), BF16),
            pltpu.VMEM((n_tok, features), BF16),
            pltpu.VMEM((n_tok, features), BF16),
            pltpu.VMEM((features, hidden_units), BF16),
            pltpu.VMEM((hidden_units, features), BF16),
            dma((4,)),
            dma((2,)),
            dma((2, PIECES)),
            dma((2, PIECES)),
        ],
        compiler_params=pltpu.CompilerParams(vmem_limit_bytes=COMBINE_VMEM_LIMIT),
        cost_estimate=pl.CostEstimate(
            flops=4 * slots * n_tok * features, bytes_accessed=8 * features * hidden_units, transcendentals=0
        ),
        name="combine",
    )(returned, placer, weighted, up_made, down_made)


def solution(mesh):
    placed = (
        P("expert", "tensor"),
        P("expert", "tensor"),
        P("expert", None),
        P("expert", None),
        P(),
        P("expert", "tensor", None),
        P("expert", None, "tensor"),
    )
    return jax.shard_map(
        per_device,
        mesh=mesh,
        in_specs=placed,
        out_specs=(
            P("expert", "tensor"),
            P("expert", "tensor"),
            P("expert", "tensor", None),
            P("expert", None, "tensor"),
        ),
        check_vma=False,
    )
```

```python
import functools

import jax
import jax.numpy as jnp
from jax import lax
from jax.experimental import pallas as pl
from jax.experimental.pallas import tpu as pltpu
from jax.sharding import PartitionSpec as P

MESH = pl.DeviceIdType.MESH
F32 = jnp.float32
BF16 = jnp.bfloat16
NX = 4
NZ = 4
CAP = 32
SOURCES = tuple((s % NX, (s + s // NX) % NX) for s in range(NX * NX))
CHUNKS = ((0, 4), (4, 12), (12, 16))
ORDER = (
    "P01", "P00", "P10", "A01", "A00", "P11", "B01", "A10", "B00", "B10", "C00", "C01",
    "A11", "C10", "P21", "B11", "D10", "C11", "P20", "D00", "E10", "A20", "B20", "D11",
    "F10", "D01", "A21", "G10", "C20", "E11", "B21", "D20", "F11", "E01", "C21", "E00",
    "G11", "E20", "F01", "D21", "F20", "X00", "F00", "G01", "E21", "G20", "F21", "G00",
    "Y00", "G21",
)
TILE = 512
PIECES = 4
VMEM_LIMIT = 60 * 1024 * 1024
COMBINE_VMEM_LIMIT = 60 * 1024 * 1024


def contract_last(left, right):
    return lax.dot_general(left, right, (((1,), (1,)), ((), ())), preferred_element_type=F32)


def contract_first(left, right):
    return lax.dot_general(left, right, (((0,), (0,)), ((), ())), preferred_element_type=F32)


def column_tiles(width, tile=TILE):
    return [(start, min(start + tile, width)) for start in range(0, width, tile)]


def wrap(value, size):
    return lax.rem(value + size, size)


def moe_kernel(
    tokens_hbm, cotangent_hbm, routes_hbm, weights_hbm, plan_hbm, up_hbm, down_hbm,
    returned, slope_hbm, flipped_hbm, down_grad, placer_hbm, weighted_hbm,
    up, down, flipped, placer, weighted, tokens, cotangent, routes, route_weights, plan, sent, rows, part, core_out, core_in,
    first_out, first_in, second_out, second_in, acts, results,
    load_sem, own_sem, sent_sem, rows_sem, core_send, core_recv,
    first_send, first_recv, second_send, second_recv,
    near_send, near_recv, far_send, far_recv, mate_send, mate_recv,
    ret_send, ret_recv, store_sem, slope_sem,
):
    expert = lax.axis_index("expert")
    place = lax.axis_index("tensor")
    x, y = lax.div(expert, NX), lax.rem(expert, NX)
    z, core = lax.div(place, 2), lax.rem(place, 2)
    z_next, z_prev, z_far = wrap(z + 1, NZ), wrap(z - 1, NZ), wrap(z + 2, NZ)
    other = 1 - core
    n_tok, features = tokens.shape
    hidden_units = up.shape[1]
    split = ((hidden_units // 128 + 1) // 2) * 128
    tiles = column_tiles(hidden_units)
    half_a, half_b = pl.ds(0, split), pl.ds(split, hidden_units - split)
    n_experts, slots = NX * NX, NX * NX * CAP

    def at_z(which):
        return {"expert": expert, "tensor": which * 2 + core}

    next_chip, prev_chip = at_z(z_next), at_z(z_prev)
    mate = {"expert": expert, "tensor": z * 2 + other}
    owners = [wrap(x - dx, NX) * NX + wrap(y - dy, NX) for dx, dy in SOURCES]
    sources = [wrap(x + dx, NX) * NX + wrap(y + dy, NX) for dx, dy in SOURCES]

    def remote(src, dst, send, recv, device):
        return pltpu.make_async_remote_copy(
            src_ref=src, dst_ref=dst, send_sem=send, recv_sem=recv, device_id=device, device_id_type=MESH
        )

    def await_received(ref, sem):
        remote(ref, ref, sem, sem, mate).wait_recv()

    def await_sent(ref, sem):
        remote(ref, ref, sem, sem, mate).wait_send()

    barrier = pltpu.get_barrier_semaphore()
    load_tokens = pltpu.make_async_copy(tokens_hbm, tokens, load_sem.at[2])
    load_cotangent = pltpu.make_async_copy(cotangent_hbm, cotangent, load_sem.at[3])
    load_up = pltpu.make_async_copy(up_hbm.at[0], up, load_sem.at[0])
    load_down = pltpu.make_async_copy(down_hbm.at[0], down, load_sem.at[1])
    load_routing = [
        pltpu.make_async_copy(source, target, load_sem.at[4 + which])
        for which, (source, target) in enumerate(
            ((routes_hbm, routes), (weights_hbm, route_weights), (plan_hbm, plan))
        )
    ]
    for load in (*load_routing, load_tokens, load_cotangent, load_up, load_down):
        load.start()
    for peer in sources[1:]:
        pl.semaphore_signal(barrier, inc=1, device_id={"expert": peer, "tensor": place}, device_id_type=MESH)
    for device in (next_chip, prev_chip, mate):
        pl.semaphore_signal(barrier, inc=1, device_id=device, device_id_type=MESH)

    for load in load_routing:
        load.wait()

    expert_id = lax.broadcasted_iota(jnp.int32, (n_experts, n_tok), 0)
    first, second = routes[0:1, :], routes[1:2, :]
    named_first = (expert_id == first).astype(F32)
    named_second = (expert_id == second).astype(F32)
    before = lax.broadcasted_iota(jnp.int32, (n_tok, n_tok), 0) < lax.broadcasted_iota(jnp.int32, (n_tok, n_tok), 1)
    earlier = jnp.dot(
        (named_first + named_second).astype(BF16), before.astype(F32).astype(BF16), preferred_element_type=F32
    )
    diagonal = lax.broadcasted_iota(jnp.int32, (n_experts, n_experts), 0) == lax.broadcasted_iota(
        jnp.int32, (n_experts, n_experts), 1
    )
    limit = jnp.sum(jnp.where(diagonal, plan[...].astype(F32), 0.0), axis=1, keepdims=True)
    slot_id = lax.broadcasted_iota(jnp.int32, (slots, n_tok), 0).astype(F32)
    ones = jnp.zeros((slots, n_tok), F32)
    scaled = jnp.zeros((slots, n_tok), F32)
    pairs = ((first, named_first, earlier), (second, named_second, earlier + named_first))
    for k, (named_id, named, count) in enumerate(pairs):
        position = jnp.sum(count * named, axis=0, keepdims=True)
        allowed = jnp.sum(limit * named, axis=0, keepdims=True)
        slot = jnp.where(position < allowed, named_id.astype(F32) * CAP + position, -1.0)
        hit = slot_id == slot
        ones = ones + jnp.where(hit, 1.0, 0.0)
        scaled = scaled + jnp.where(hit, route_weights[k : k + 1, :].astype(F32), 0.0)
    placer[...] = ones.astype(BF16)
    weighted[...] = scaled.astype(BF16)

    def source_rows(s, count=1):
        return pl.ds(s * CAP, count * CAP)

    def chunk_rows(c):
        lo, hi = CHUNKS[c]
        return pl.ds(lo * CAP, (hi - lo) * CAP)

    def block_size(c):
        lo, hi = CHUNKS[c]
        return (hi - lo) * CAP // (2 * NZ)

    def block(c, side, which, count=1):
        size = block_size(c)
        return pl.ds(pl.multiple_of(CHUNKS[c][0] * CAP + (side * NZ + which) * size, 16), count * size)

    def half_block(c, which, count=1):
        size = block_size(c)
        return pl.ds(pl.multiple_of(CHUNKS[c][0] * CAP // 2 + which * size, 16), count * size)

    def small_block(c):
        return pl.ds(CHUNKS[c][0] * CAP // (2 * NZ), block_size(c))

    def remote_sources(c):
        lo, hi = CHUNKS[c]
        return range(max(lo, 1), hi)

    def make_rows(c, k):
        matrix, picker = ((tokens, placer), (cotangent, weighted))[k]
        picked = [picker[pl.ds(pl.multiple_of(owners[s] * CAP, CAP), CAP), :] for s in range(*CHUNKS[c])]
        sent[k, chunk_rows(c), :] = jnp.dot(
            jnp.concatenate(picked, axis=0), matrix[...], preferred_element_type=F32
        ).astype(BF16)
        if c == 0:
            own_rows(k).start()
        for s in remote_sources(c):
            remote(
                sent.at[k, source_rows(s)], rows.at[k, source_rows(s)], sent_sem.at[k], rows_sem.at[c, k],
                {"expert": owners[s], "tensor": place},
            ).start()

    def own_rows(k):
        return pltpu.make_async_copy(sent.at[k, source_rows(0)], rows.at[k, source_rows(0)], own_sem.at[0, k])

    def own_back(k):
        return pltpu.make_async_copy(results.at[k, source_rows(0)], returned.at[k, expert], own_sem.at[1, k])

    partial_order = [(int(step[1]), int(step[2])) for step in ORDER if step[0] == "A"]

    def stage_partial(c, k):
        if c == 0:
            own_rows(k).wait()
        if (c, k) == next((step_c, step_k) for step_c, step_k in partial_order if step_k == k):
            (load_up if k == 0 else load_down).wait()
        arriving = remote_sources(c)
        await_received(rows.at[k, source_rows(arriving[0], len(arriving))], rows_sem.at[c, k])
        taken = rows[k, chunk_rows(c), :]
        for lo, hi in tiles:
            if k == 0:
                product = jnp.dot(taken, up[:, lo:hi], preferred_element_type=F32)
            else:
                product = contract_last(taken, down[lo:hi, :])
            part[k, chunk_rows(c), lo:hi] = product
        away = half_block(c, 0, NZ)
        core_out[k, away, :] = part[k, block(c, other, 0, NZ), :].astype(BF16)
        remote(core_out.at[k, away], core_in.at[k, away], core_send.at[0], core_recv.at[c, k], mate).start()

    def chip_sum(c, k, which, half):
        return part[k, block(c, core, which), half] + core_in[k, half_block(c, which), half].astype(F32)

    def send_second(c, k, side, half):
        remote(
            second_out.at[k, side, small_block(c), half], second_in.at[k, side, small_block(c), half],
            second_send.at[0], second_recv.at[c, k], next_chip if side == 0 else prev_chip,
        ).start()

    def stage_core(c, k):
        await_received(core_in.at[k, half_block(c, 0, NZ)], core_recv.at[c, k])
        here = small_block(c)
        for half in (half_a, half_b):
            first_out[k, here, half] = chip_sum(c, k, z_far, half).astype(BF16)
        second_out[k, 0, here, half_b] = chip_sum(c, k, z_next, half_b).astype(BF16)
        second_out[k, 1, here, half_a] = chip_sum(c, k, z_prev, half_a).astype(BF16)
        for half, device in ((half_a, next_chip), (half_b, prev_chip)):
            remote(
                first_out.at[k, here, half], first_in.at[k, here, half], first_send.at[0], first_recv.at[c, k], device
            ).start()
        send_second(c, k, 0, half_b)
        send_second(c, k, 1, half_a)

    def stage_relay(c, k):
        here = small_block(c)
        relays = ((0, z_next, half_a), (1, z_prev, half_b))
        await_received(first_in.at[k, here], first_recv.at[c, k])
        for side, which, half in relays:
            total = chip_sum(c, k, which, half) + first_in[k, here, half].astype(F32)
            second_out[k, side, here, half] = total.astype(BF16)
        for side, which, half in relays:
            send_second(c, k, side, half)

    def stage_activate(c, k):
        here = small_block(c)
        await_received(second_in.at[k, :, here], second_recv.at[c, k])
        total = chip_sum(c, k, z, pl.ds(0, hidden_units))
        total = total + (second_in[k, 0, here, :].astype(F32) + second_in[k, 1, here, :].astype(F32))
        mine = block(c, core, z)
        if k == 0:
            part[0, mine, :] = total
            acts[0, mine, :] = (total * jax.nn.sigmoid(total)).astype(BF16)
        else:
            pre = part[0, mine, :]
            gate = jax.nn.sigmoid(pre)
            acts[1, mine, :] = (total * gate * (1.0 + pre * (1.0 - gate))).astype(BF16)
        ref = acts.at[k, mine]
        remote(ref, ref, near_send.at[0], near_recv.at[c, k], next_chip).start()
        remote(ref, ref, near_send.at[0], near_recv.at[c, k], prev_chip).start()

    def stage_forward(c, k):
        await_received(acts.at[k, block(c, core, 0, 2)], near_recv.at[c, k])
        for which, half, device in ((z_prev, half_a, next_chip), (z_next, half_b, prev_chip)):
            ref = acts.at[k, block(c, core, which), half]
            remote(ref, ref, far_send.at[0], far_recv.at[c, k], device).start()

    def stage_last(c, k):
        await_received(acts.at[k, block(c, core, z_far)], far_recv.at[c, k])
        ref = acts.at[k, block(c, core, 0, NZ)]
        remote(ref, ref, mate_send.at[0], mate_recv.at[c, k], mate).start()

    def stage_result(c, k):
        await_received(acts.at[k, block(c, other, 0, NZ)], mate_recv.at[c, k])
        taken = acts[k, chunk_rows(c), :]
        for lo, hi in column_tiles(features):
            if k == 0:
                product = jnp.dot(taken, down[:, lo:hi], preferred_element_type=F32)
            else:
                product = contract_last(taken, up[lo:hi, :])
            results[k, chunk_rows(c), lo:hi] = product.astype(BF16)
        if c == 0:
            own_back(k).start()
        for s in remote_sources(c):
            remote(
                results.at[k, source_rows(s)], returned.at[k, expert], ret_send.at[k], ret_recv.at[k],
                {"expert": sources[s], "tensor": place},
            ).start()
        if k == 1:
            save_slope(c).start()

    def stage_flip(c, k):
        flipped[...] = rows[0].T
        save_flipped.start()

    def stage_down_grad(c, k):
        for lo, hi in tiles:
            down[lo:hi, :] = contract_first(acts[0, :, lo:hi], rows[1]).astype(BF16)
        save_down.start()

    save_placer = pltpu.make_async_copy(placer, placer_hbm, store_sem.at[0])
    save_weighted = pltpu.make_async_copy(weighted, weighted_hbm, store_sem.at[1])
    save_flipped = pltpu.make_async_copy(flipped, flipped_hbm, store_sem.at[2])
    save_down = pltpu.make_async_copy(down, down_grad.at[0], store_sem.at[3])

    def save_slope(c):
        return pltpu.make_async_copy(acts.at[1, chunk_rows(c)], slope_hbm.at[chunk_rows(c)], slope_sem.at[c])

    stages = {
        "P": make_rows, "A": stage_partial, "B": stage_core, "C": stage_relay, "D": stage_activate,
        "E": stage_forward, "F": stage_last, "G": stage_result, "X": stage_flip, "Y": stage_down_grad,
    }

    save_placer.start()
    save_weighted.start()
    load_tokens.wait()
    load_cotangent.wait()
    pl.semaphore_wait(barrier, n_experts - 1 + 3)
    for step in ORDER:
        stages[step[0]](int(step[1]), int(step[2]))

    for k in range(2):
        await_sent(sent.at[k, source_rows(1, n_experts - 1)], sent_sem.at[k])
        own_back(k).wait()
    for save in (save_placer, save_weighted, save_flipped, *map(save_slope, range(len(CHUNKS)))):
        save.wait()
    quarter = slots // NZ
    await_sent(core_out, core_send.at[0])
    await_sent(first_out, first_send.at[0])
    await_sent(second_out, second_send.at[0])
    await_sent(acts.at[:, pl.ds(0, quarter)], near_send.at[0])
    await_sent(acts.at[:, pl.ds(0, quarter // 2)], far_send.at[0])
    await_sent(acts.at[:, pl.ds(0, 2 * quarter)], mate_send.at[0])
    for k in range(2):
        await_received(returned.at[k, pl.ds(0, n_experts - 1)], ret_recv.at[k])
        await_sent(results.at[k, source_rows(1, n_experts - 1)], ret_send.at[k])
    save_down.wait()


def combine_kernel(
    returned_hbm, placer_hbm, weighted_hbm, flipped_hbm, slope_hbm, down_hbm,
    layer_hbm, token_hbm, up_grad, down_grad,
    returned, placer, weighted, flipped, slope, layer_out, token_grad, up, down,
    load_sem, out_sem, in_sem, copy_sem, slope_sem, up_sem,
):
    slots, features = placer.shape[0], layer_out.shape[1]
    hidden_units = up.shape[1]
    tiles = column_tiles(hidden_units)
    load_flipped = pltpu.make_async_copy(flipped_hbm, flipped, load_sem.at[4])
    load_slope = [
        pltpu.make_async_copy(slope_hbm.at[:, lo:hi], slope.at[:, lo:hi], slope_sem.at[index])
        for index, (lo, hi) in enumerate(tiles)
    ]
    parts = (
        (
            pltpu.make_async_copy(weighted_hbm, weighted, load_sem.at[0]),
            pltpu.make_async_copy(returned_hbm.at[0], returned.at[0], load_sem.at[1]),
        ),
        (
            pltpu.make_async_copy(placer_hbm, placer, load_sem.at[2]),
            pltpu.make_async_copy(returned_hbm.at[1], returned.at[1], load_sem.at[3]),
        ),
    )
    size = hidden_units // PIECES
    picks = [pl.ds(piece * size, size) for piece in range(PIECES)]
    loads = [
        pltpu.make_async_copy(down_hbm.at[0, pick], down.at[pick], in_sem.at[piece])
        for piece, pick in enumerate(picks)
    ]
    stores = [
        pltpu.make_async_copy(down.at[pick], down_grad.at[0, pick], copy_sem.at[piece])
        for piece, pick in enumerate(picks)
    ]
    outs = [
        pltpu.make_async_copy(layer_out, layer_hbm, out_sem.at[0]),
        pltpu.make_async_copy(token_grad, token_hbm, out_sem.at[1]),
    ]
    up_stores = [
        pltpu.make_async_copy(up.at[:, lo:hi], up_grad.at[0, :, lo:hi], up_sem.at[index])
        for index, (lo, hi) in enumerate(tiles)
    ]
    for load in (load_flipped, load_slope[0], loads[0], *load_slope[1:], *loads[1:], *parts[0], *parts[1]):
        load.start()
    load_flipped.wait()
    for index, (lo, hi) in enumerate(tiles):
        load_slope[index].wait()
        up[:, lo:hi] = jnp.dot(flipped[...], slope[:, lo:hi], preferred_element_type=F32).astype(BF16)
        up_stores[index].start()
        if index < PIECES:
            loads[index].wait()
            stores[index].start()
    for part, picker, result, out, k in zip(parts, (weighted, placer), (layer_out, token_grad), outs, range(2)):
        for load in part:
            load.wait()
        result[...] = contract_first(picker[...], returned[k].reshape(slots, features)).astype(BF16)
        out.start()
    for copy in (*up_stores, *stores, *outs):
        copy.wait()


def per_device(tokens, cotangent, routes, route_weights, capacity_plan, up_weight, down_weight):
    n_tok, features = tokens.shape
    hidden_units = up_weight.shape[2]
    slots = NX * NX * CAP
    hbm = pl.BlockSpec(memory_space=pl.ANY)
    dma = pltpu.SemaphoreType.DMA
    flops = 12 * slots * features * hidden_units
    n_chunks = len(CHUNKS)
    n_tiles = len(column_tiles(hidden_units))
    returned, slope, flipped, down_made, placer, weighted = pl.pallas_call(
        moe_kernel,
        out_shape=(
            jax.ShapeDtypeStruct((2, NX * NX, CAP, features), BF16),
            jax.ShapeDtypeStruct((slots, hidden_units), BF16),
            jax.ShapeDtypeStruct((features, slots), BF16),
            jax.ShapeDtypeStruct((1, hidden_units, features), BF16),
            jax.ShapeDtypeStruct((slots, n_tok), BF16),
            jax.ShapeDtypeStruct((slots, n_tok), BF16),
        ),
        in_specs=[pl.BlockSpec(memory_space=pltpu.HBM)] * 7,
        out_specs=(hbm,) * 6,
        scratch_shapes=[
            pltpu.VMEM((features, hidden_units), BF16),
            pltpu.VMEM((hidden_units, features), BF16),
            pltpu.VMEM((features, slots), BF16),
            pltpu.VMEM((slots, n_tok), BF16),
            pltpu.VMEM((slots, n_tok), BF16),
            pltpu.VMEM((n_tok, features), BF16),
            pltpu.VMEM((n_tok, features), BF16),
            pltpu.VMEM((2, n_tok), jnp.int32),
            pltpu.VMEM((2, n_tok), BF16),
            pltpu.VMEM((1, NX * NX), jnp.int32),
            pltpu.VMEM((2, slots, features), BF16),
            pltpu.VMEM((2, slots, features), BF16),
            pltpu.VMEM((2, slots, hidden_units), F32),
            pltpu.VMEM((2, slots // 2, hidden_units), BF16),
            pltpu.VMEM((2, slots // 2, hidden_units), BF16),
            pltpu.VMEM((2, slots // (2 * NZ), hidden_units), BF16),
            pltpu.VMEM((2, slots // (2 * NZ), hidden_units), BF16),
            pltpu.VMEM((2, 2, slots // (2 * NZ), hidden_units), BF16),
            pltpu.VMEM((2, 2, slots // (2 * NZ), hidden_units), BF16),
            pltpu.VMEM((2, slots, hidden_units), BF16),
            pltpu.VMEM((2, slots, features), BF16),
            dma((7,)),
            dma((2, 2)),
            dma((2,)),
            dma((n_chunks, 2)),
            dma((1,)),
            dma((n_chunks, 2)),
            dma((1,)),
            dma((n_chunks, 2)),
            dma((1,)),
            dma((n_chunks, 2)),
            dma((1,)),
            dma((n_chunks, 2)),
            dma((1,)),
            dma((n_chunks, 2)),
            dma((1,)),
            dma((n_chunks, 2)),
            dma((2,)),
            dma((2,)),
            dma((4,)),
            dma((n_chunks,)),
        ],
        compiler_params=pltpu.CompilerParams(
            collective_id=0, has_side_effects=True, vmem_limit_bytes=VMEM_LIMIT
        ),
        cost_estimate=pl.CostEstimate(
            flops=flops, bytes_accessed=4 * features * hidden_units, transcendentals=slots * hidden_units // 8
        ),
        name="moe_exchange",
    )(tokens, cotangent, routes.T, route_weights.T, capacity_plan[None], up_weight, down_weight)
    return pl.pallas_call(
        combine_kernel,
        out_shape=(
            jax.ShapeDtypeStruct((n_tok, features), BF16),
            jax.ShapeDtypeStruct((n_tok, features), BF16),
            jax.ShapeDtypeStruct((1, features, hidden_units), BF16),
            jax.ShapeDtypeStruct((1, hidden_units, features), BF16),
        ),
        in_specs=[hbm] * 6,
        out_specs=(hbm,) * 4,
        scratch_shapes=[
            pltpu.VMEM((2, NX * NX, CAP, features), BF16),
            pltpu.VMEM((slots, n_tok), BF16),
            pltpu.VMEM((slots, n_tok), BF16),
            pltpu.VMEM((features, slots), BF16),
            pltpu.VMEM((slots, hidden_units), BF16),
            pltpu.VMEM((n_tok, features), BF16),
            pltpu.VMEM((n_tok, features), BF16),
            pltpu.VMEM((features, hidden_units), BF16),
            pltpu.VMEM((hidden_units, features), BF16),
            dma((5,)),
            dma((2,)),
            dma((PIECES,)),
            dma((PIECES,)),
            dma((n_tiles,)),
            dma((n_tiles,)),
        ],
        compiler_params=pltpu.CompilerParams(vmem_limit_bytes=COMBINE_VMEM_LIMIT),
        cost_estimate=pl.CostEstimate(
            flops=4 * slots * n_tok * features, bytes_accessed=8 * features * hidden_units, transcendentals=0
        ),
        name="combine",
    )(returned, placer, weighted, flipped, slope, down_made)


def solution(mesh):
    placed = (
        P("expert", "tensor"),
        P("expert", "tensor"),
        P("expert", None),
        P("expert", None),
        P(),
        P("expert", "tensor", None),
        P("expert", None, "tensor"),
    )
    return jax.shard_map(
        per_device,
        mesh=mesh,
        in_specs=placed,
        out_specs=(
            P("expert", "tensor"),
            P("expert", "tensor"),
            P("expert", "tensor", None),
            P("expert", None, "tensor"),
        ),
        check_vma=False,
    )
```

```python
import functools

import jax
import jax.numpy as jnp
from jax import lax
from jax.experimental import pallas as pl
from jax.experimental.pallas import tpu as pltpu
from jax.sharding import PartitionSpec as P

MESH = pl.DeviceIdType.MESH
F32 = jnp.float32
BF16 = jnp.bfloat16
NX = 4
NZ = 4
CAP = 32
SOURCES = tuple((s % NX, (s + s // NX) % NX) for s in range(NX * NX))
CHUNKS = ((0, 4), (4, 8), (8, 12), (12, 16))
ORDER = (
    "P10", "P00", "P01", "P11", "A10", "P20", "A00", "B10", "A01", "B00", "B01", "A11",
    "C10", "C00", "B11", "P30", "C01", "D10", "P31", "C11", "D00", "A20", "D01", "P21",
    "B20", "D11", "E10", "E01", "A30", "E00", "C20", "A21", "B30", "E11", "A31", "B21",
    "C30", "F01", "F00", "B31", "D20", "F10", "F11", "G00", "C31", "D30", "G10", "E20",
    "C21", "D31", "G11", "E30", "F20", "D21", "G01", "E31", "F30", "X00", "G20", "E21",
    "F31", "G30", "G31", "F21", "G21", "Y00",
)
TILE = 512
PIECES = 4
VMEM_LIMIT = 60 * 1024 * 1024
COMBINE_VMEM_LIMIT = 60 * 1024 * 1024


def contract_last(left, right):
    return lax.dot_general(left, right, (((1,), (1,)), ((), ())), preferred_element_type=F32)


def contract_first(left, right):
    return lax.dot_general(left, right, (((0,), (0,)), ((), ())), preferred_element_type=F32)


def column_tiles(width, tile=TILE):
    return [(start, min(start + tile, width)) for start in range(0, width, tile)]


def wrap(value, size):
    return lax.rem(value + size, size)


def moe_kernel(
    tokens_hbm, cotangent_hbm, routes_hbm, weights_hbm, plan_hbm, up_hbm, down_hbm,
    returned, slope_hbm, flipped_hbm, down_grad, placer_hbm, weighted_hbm,
    up, down, flipped, placer, weighted, tokens, cotangent, routes, route_weights, plan, sent, rows, part, core_out, core_in,
    first_out, first_in, second_out, second_in, acts, results,
    load_sem, own_sem, sent_sem, rows_sem, core_send, core_recv,
    first_send, first_recv, second_send, second_recv,
    near_send, near_recv, far_send, far_recv, mate_send, mate_recv,
    ret_send, ret_recv, store_sem, slope_sem,
):
    expert = lax.axis_index("expert")
    place = lax.axis_index("tensor")
    x, y = lax.div(expert, NX), lax.rem(expert, NX)
    z, core = lax.div(place, 2), lax.rem(place, 2)
    z_next, z_prev, z_far = wrap(z + 1, NZ), wrap(z - 1, NZ), wrap(z + 2, NZ)
    other = 1 - core
    n_tok, features = tokens.shape
    hidden_units = up.shape[1]
    split = ((hidden_units // 128 + 1) // 2) * 128
    tiles = column_tiles(hidden_units)
    half_a, half_b = pl.ds(0, split), pl.ds(split, hidden_units - split)
    n_experts, slots = NX * NX, NX * NX * CAP

    def at_z(which):
        return {"expert": expert, "tensor": which * 2 + core}

    next_chip, prev_chip = at_z(z_next), at_z(z_prev)
    mate = {"expert": expert, "tensor": z * 2 + other}
    owners = [wrap(x - dx, NX) * NX + wrap(y - dy, NX) for dx, dy in SOURCES]
    sources = [wrap(x + dx, NX) * NX + wrap(y + dy, NX) for dx, dy in SOURCES]

    def remote(src, dst, send, recv, device):
        return pltpu.make_async_remote_copy(
            src_ref=src, dst_ref=dst, send_sem=send, recv_sem=recv, device_id=device, device_id_type=MESH
        )

    def await_received(ref, sem):
        remote(ref, ref, sem, sem, mate).wait_recv()

    def await_sent(ref, sem):
        remote(ref, ref, sem, sem, mate).wait_send()

    barrier = pltpu.get_barrier_semaphore()
    load_tokens = pltpu.make_async_copy(tokens_hbm, tokens, load_sem.at[2])
    load_cotangent = pltpu.make_async_copy(cotangent_hbm, cotangent, load_sem.at[3])
    load_up = pltpu.make_async_copy(up_hbm.at[0], up, load_sem.at[0])
    load_down = pltpu.make_async_copy(down_hbm.at[0], down, load_sem.at[1])
    load_routing = [
        pltpu.make_async_copy(source, target, load_sem.at[4 + which])
        for which, (source, target) in enumerate(
            ((routes_hbm, routes), (weights_hbm, route_weights), (plan_hbm, plan))
        )
    ]
    for load in (*load_routing, load_tokens, load_cotangent, load_up, load_down):
        load.start()
    for peer in sources[1:]:
        pl.semaphore_signal(barrier, inc=1, device_id={"expert": peer, "tensor": place}, device_id_type=MESH)
    for device in (next_chip, prev_chip, mate):
        pl.semaphore_signal(barrier, inc=1, device_id=device, device_id_type=MESH)

    for load in load_routing:
        load.wait()

    expert_id = lax.broadcasted_iota(jnp.int32, (n_experts, n_tok), 0)
    first, second = routes[0:1, :], routes[1:2, :]
    named_first = (expert_id == first).astype(F32)
    named_second = (expert_id == second).astype(F32)
    before = lax.broadcasted_iota(jnp.int32, (n_tok, n_tok), 0) < lax.broadcasted_iota(jnp.int32, (n_tok, n_tok), 1)
    earlier = jnp.dot(
        (named_first + named_second).astype(BF16), before.astype(F32).astype(BF16), preferred_element_type=F32
    )
    diagonal = lax.broadcasted_iota(jnp.int32, (n_experts, n_experts), 0) == lax.broadcasted_iota(
        jnp.int32, (n_experts, n_experts), 1
    )
    limit = jnp.sum(jnp.where(diagonal, plan[...].astype(F32), 0.0), axis=1, keepdims=True)
    slot_id = lax.broadcasted_iota(jnp.int32, (slots, n_tok), 0).astype(F32)
    ones = jnp.zeros((slots, n_tok), F32)
    scaled = jnp.zeros((slots, n_tok), F32)
    pairs = ((first, named_first, earlier), (second, named_second, earlier + named_first))
    for k, (named_id, named, count) in enumerate(pairs):
        position = jnp.sum(count * named, axis=0, keepdims=True)
        allowed = jnp.sum(limit * named, axis=0, keepdims=True)
        slot = jnp.where(position < allowed, named_id.astype(F32) * CAP + position, -1.0)
        hit = slot_id == slot
        ones = ones + jnp.where(hit, 1.0, 0.0)
        scaled = scaled + jnp.where(hit, route_weights[k : k + 1, :].astype(F32), 0.0)
    placer[...] = ones.astype(BF16)
    weighted[...] = scaled.astype(BF16)

    def source_rows(s, count=1):
        return pl.ds(s * CAP, count * CAP)

    def chunk_rows(c):
        lo, hi = CHUNKS[c]
        return pl.ds(lo * CAP, (hi - lo) * CAP)

    def block_size(c):
        lo, hi = CHUNKS[c]
        return (hi - lo) * CAP // (2 * NZ)

    def block(c, side, which, count=1):
        size = block_size(c)
        return pl.ds(pl.multiple_of(CHUNKS[c][0] * CAP + (side * NZ + which) * size, 16), count * size)

    def half_block(c, which, count=1):
        size = block_size(c)
        return pl.ds(pl.multiple_of(CHUNKS[c][0] * CAP // 2 + which * size, 16), count * size)

    def small_block(c):
        return pl.ds(CHUNKS[c][0] * CAP // (2 * NZ), block_size(c))

    def remote_sources(c):
        lo, hi = CHUNKS[c]
        return range(max(lo, 1), hi)

    dispatch_order = [(int(step[1]), int(step[2])) for step in ORDER if step[0] == "P"]

    def make_rows(c, k):
        matrix, picker = ((tokens, placer), (cotangent, weighted))[k]
        is_first = (c, k) == next((at, kind) for at, kind in dispatch_order if kind == k)
        if is_first:
            (load_tokens, load_cotangent)[k].wait()
        picked = [picker[pl.ds(pl.multiple_of(owners[s] * CAP, CAP), CAP), :] for s in range(*CHUNKS[c])]
        sent[k, chunk_rows(c), :] = jnp.dot(
            jnp.concatenate(picked, axis=0), matrix[...], preferred_element_type=F32
        ).astype(BF16)
        if c == 0:
            own_rows(k).start()
        if (c, k) == dispatch_order[0]:
            pl.semaphore_wait(barrier, n_experts - 1 + 3)
        for s in remote_sources(c):
            remote(
                sent.at[k, source_rows(s)], rows.at[k, source_rows(s)], sent_sem.at[k], rows_sem.at[c, k],
                {"expert": owners[s], "tensor": place},
            ).start()

    def own_rows(k):
        return pltpu.make_async_copy(sent.at[k, source_rows(0)], rows.at[k, source_rows(0)], own_sem.at[0, k])

    def own_back(k):
        return pltpu.make_async_copy(results.at[k, source_rows(0)], returned.at[k, expert], own_sem.at[1, k])

    partial_order = [(int(step[1]), int(step[2])) for step in ORDER if step[0] == "A"]

    def stage_partial(c, k):
        if c == 0:
            own_rows(k).wait()
        if (c, k) == next((step_c, step_k) for step_c, step_k in partial_order if step_k == k):
            (load_up if k == 0 else load_down).wait()
        arriving = remote_sources(c)
        await_received(rows.at[k, source_rows(arriving[0], len(arriving))], rows_sem.at[c, k])
        taken = rows[k, chunk_rows(c), :]
        for lo, hi in tiles:
            if k == 0:
                product = jnp.dot(taken, up[:, lo:hi], preferred_element_type=F32)
            else:
                product = contract_last(taken, down[lo:hi, :])
            part[k, chunk_rows(c), lo:hi] = product
        away = half_block(c, 0, NZ)
        core_out[k, away, :] = part[k, block(c, other, 0, NZ), :].astype(BF16)
        remote(core_out.at[k, away], core_in.at[k, away], core_send.at[0], core_recv.at[c, k], mate).start()

    def chip_sum(c, k, which, half):
        return part[k, block(c, core, which), half] + core_in[k, half_block(c, which), half].astype(F32)

    def send_second(c, k, side, half):
        remote(
            second_out.at[k, side, small_block(c), half], second_in.at[k, side, small_block(c), half],
            second_send.at[0], second_recv.at[c, k], next_chip if side == 0 else prev_chip,
        ).start()

    def stage_core(c, k):
        await_received(core_in.at[k, half_block(c, 0, NZ)], core_recv.at[c, k])
        here = small_block(c)
        for half in (half_a, half_b):
            first_out[k, here, half] = chip_sum(c, k, z_far, half).astype(BF16)
        second_out[k, 0, here, half_b] = chip_sum(c, k, z_next, half_b).astype(BF16)
        second_out[k, 1, here, half_a] = chip_sum(c, k, z_prev, half_a).astype(BF16)
        for half, device in ((half_a, next_chip), (half_b, prev_chip)):
            remote(
                first_out.at[k, here, half], first_in.at[k, here, half], first_send.at[0], first_recv.at[c, k], device
            ).start()
        send_second(c, k, 0, half_b)
        send_second(c, k, 1, half_a)

    def stage_relay(c, k):
        here = small_block(c)
        relays = ((0, z_next, half_a), (1, z_prev, half_b))
        await_received(first_in.at[k, here], first_recv.at[c, k])
        for side, which, half in relays:
            total = chip_sum(c, k, which, half) + first_in[k, here, half].astype(F32)
            second_out[k, side, here, half] = total.astype(BF16)
        for side, which, half in relays:
            send_second(c, k, side, half)

    def stage_activate(c, k):
        here = small_block(c)
        await_received(second_in.at[k, :, here], second_recv.at[c, k])
        total = chip_sum(c, k, z, pl.ds(0, hidden_units))
        total = total + (second_in[k, 0, here, :].astype(F32) + second_in[k, 1, here, :].astype(F32))
        mine = block(c, core, z)
        if k == 0:
            part[0, mine, :] = total
            acts[0, mine, :] = (total * jax.nn.sigmoid(total)).astype(BF16)
        else:
            pre = part[0, mine, :]
            gate = jax.nn.sigmoid(pre)
            acts[1, mine, :] = (total * gate * (1.0 + pre * (1.0 - gate))).astype(BF16)
        ref = acts.at[k, mine]
        remote(ref, ref, near_send.at[0], near_recv.at[c, k], next_chip).start()
        remote(ref, ref, near_send.at[0], near_recv.at[c, k], prev_chip).start()

    def stage_forward(c, k):
        await_received(acts.at[k, block(c, core, 0, 2)], near_recv.at[c, k])
        for which, half, device in ((z_prev, half_a, next_chip), (z_next, half_b, prev_chip)):
            ref = acts.at[k, block(c, core, which), half]
            remote(ref, ref, far_send.at[0], far_recv.at[c, k], device).start()

    def stage_last(c, k):
        await_received(acts.at[k, block(c, core, z_far)], far_recv.at[c, k])
        ref = acts.at[k, block(c, core, 0, NZ)]
        remote(ref, ref, mate_send.at[0], mate_recv.at[c, k], mate).start()

    def stage_result(c, k):
        await_received(acts.at[k, block(c, other, 0, NZ)], mate_recv.at[c, k])
        taken = acts[k, chunk_rows(c), :]
        for lo, hi in column_tiles(features):
            if k == 0:
                product = jnp.dot(taken, down[:, lo:hi], preferred_element_type=F32)
            else:
                product = contract_last(taken, up[lo:hi, :])
            results[k, chunk_rows(c), lo:hi] = product.astype(BF16)
        if c == 0:
            own_back(k).start()
        for s in remote_sources(c):
            remote(
                results.at[k, source_rows(s)], returned.at[k, expert], ret_send.at[k], ret_recv.at[k],
                {"expert": sources[s], "tensor": place},
            ).start()
        if k == 1:
            save_slope(c).start()

    def stage_flip(c, k):
        flipped[...] = rows[0].T
        save_flipped.start()

    def stage_down_grad(c, k):
        for lo, hi in tiles:
            down[lo:hi, :] = contract_first(acts[0, :, lo:hi], rows[1]).astype(BF16)
        save_down.start()

    save_placer = pltpu.make_async_copy(placer, placer_hbm, store_sem.at[0])
    save_weighted = pltpu.make_async_copy(weighted, weighted_hbm, store_sem.at[1])
    save_flipped = pltpu.make_async_copy(flipped, flipped_hbm, store_sem.at[2])
    save_down = pltpu.make_async_copy(down, down_grad.at[0], store_sem.at[3])

    def save_slope(c):
        return pltpu.make_async_copy(acts.at[1, chunk_rows(c)], slope_hbm.at[chunk_rows(c)], slope_sem.at[c])

    stages = {
        "P": make_rows, "A": stage_partial, "B": stage_core, "C": stage_relay, "D": stage_activate,
        "E": stage_forward, "F": stage_last, "G": stage_result, "X": stage_flip, "Y": stage_down_grad,
    }

    save_placer.start()
    save_weighted.start()
    for step in ORDER:
        stages[step[0]](int(step[1]), int(step[2]))

    for k in range(2):
        await_sent(sent.at[k, source_rows(1, n_experts - 1)], sent_sem.at[k])
        own_back(k).wait()
    for save in (save_placer, save_weighted, save_flipped, *map(save_slope, range(len(CHUNKS)))):
        save.wait()
    quarter = slots // NZ
    await_sent(core_out, core_send.at[0])
    await_sent(first_out, first_send.at[0])
    await_sent(second_out, second_send.at[0])
    await_sent(acts.at[:, pl.ds(0, quarter)], near_send.at[0])
    await_sent(acts.at[:, pl.ds(0, quarter // 2)], far_send.at[0])
    await_sent(acts.at[:, pl.ds(0, 2 * quarter)], mate_send.at[0])
    for k in range(2):
        await_received(returned.at[k, pl.ds(0, n_experts - 1)], ret_recv.at[k])
        await_sent(results.at[k, source_rows(1, n_experts - 1)], ret_send.at[k])
    save_down.wait()


def combine_kernel(
    returned_hbm, placer_hbm, weighted_hbm, flipped_hbm, slope_hbm, down_hbm,
    layer_hbm, token_hbm, up_grad, down_grad,
    returned, placer, weighted, flipped, slope, layer_out, token_grad, up, down,
    load_sem, out_sem, in_sem, copy_sem, slope_sem, up_sem,
):
    slots, features = placer.shape[0], layer_out.shape[1]
    hidden_units = up.shape[1]
    tiles = column_tiles(hidden_units)
    load_flipped = pltpu.make_async_copy(flipped_hbm, flipped, load_sem.at[4])
    load_slope = [
        pltpu.make_async_copy(slope_hbm.at[:, lo:hi], slope.at[:, lo:hi], slope_sem.at[index])
        for index, (lo, hi) in enumerate(tiles)
    ]
    parts = (
        (
            pltpu.make_async_copy(weighted_hbm, weighted, load_sem.at[0]),
            pltpu.make_async_copy(returned_hbm.at[0], returned.at[0], load_sem.at[1]),
        ),
        (
            pltpu.make_async_copy(placer_hbm, placer, load_sem.at[2]),
            pltpu.make_async_copy(returned_hbm.at[1], returned.at[1], load_sem.at[3]),
        ),
    )
    size = hidden_units // PIECES
    picks = [pl.ds(piece * size, size) for piece in range(PIECES)]
    loads = [
        pltpu.make_async_copy(down_hbm.at[0, pick], down.at[pick], in_sem.at[piece])
        for piece, pick in enumerate(picks)
    ]
    stores = [
        pltpu.make_async_copy(down.at[pick], down_grad.at[0, pick], copy_sem.at[piece])
        for piece, pick in enumerate(picks)
    ]
    outs = [
        pltpu.make_async_copy(layer_out, layer_hbm, out_sem.at[0]),
        pltpu.make_async_copy(token_grad, token_hbm, out_sem.at[1]),
    ]
    up_stores = [
        pltpu.make_async_copy(up.at[:, lo:hi], up_grad.at[0, :, lo:hi], up_sem.at[index])
        for index, (lo, hi) in enumerate(tiles)
    ]
    for load in (load_flipped, load_slope[0], loads[0], *load_slope[1:], *loads[1:], *parts[0], *parts[1]):
        load.start()
    load_flipped.wait()
    for index, (lo, hi) in enumerate(tiles):
        load_slope[index].wait()
        up[:, lo:hi] = jnp.dot(flipped[...], slope[:, lo:hi], preferred_element_type=F32).astype(BF16)
        up_stores[index].start()
        if index < PIECES:
            loads[index].wait()
            stores[index].start()
    for part, picker, result, out, k in zip(parts, (weighted, placer), (layer_out, token_grad), outs, range(2)):
        for load in part:
            load.wait()
        result[...] = contract_first(picker[...], returned[k].reshape(slots, features)).astype(BF16)
        out.start()
    for copy in (*up_stores, *stores, *outs):
        copy.wait()


def per_device(tokens, cotangent, routes, route_weights, capacity_plan, up_weight, down_weight):
    n_tok, features = tokens.shape
    hidden_units = up_weight.shape[2]
    slots = NX * NX * CAP
    hbm = pl.BlockSpec(memory_space=pl.ANY)
    dma = pltpu.SemaphoreType.DMA
    flops = 12 * slots * features * hidden_units
    n_chunks = len(CHUNKS)
    n_tiles = len(column_tiles(hidden_units))
    returned, slope, flipped, down_made, placer, weighted = pl.pallas_call(
        moe_kernel,
        out_shape=(
            jax.ShapeDtypeStruct((2, NX * NX, CAP, features), BF16),
            jax.ShapeDtypeStruct((slots, hidden_units), BF16),
            jax.ShapeDtypeStruct((features, slots), BF16),
            jax.ShapeDtypeStruct((1, hidden_units, features), BF16),
            jax.ShapeDtypeStruct((slots, n_tok), BF16),
            jax.ShapeDtypeStruct((slots, n_tok), BF16),
        ),
        in_specs=[pl.BlockSpec(memory_space=pltpu.HBM)] * 7,
        out_specs=(hbm,) * 6,
        scratch_shapes=[
            pltpu.VMEM((features, hidden_units), BF16),
            pltpu.VMEM((hidden_units, features), BF16),
            pltpu.VMEM((features, slots), BF16),
            pltpu.VMEM((slots, n_tok), BF16),
            pltpu.VMEM((slots, n_tok), BF16),
            pltpu.VMEM((n_tok, features), BF16),
            pltpu.VMEM((n_tok, features), BF16),
            pltpu.VMEM((2, n_tok), jnp.int32),
            pltpu.VMEM((2, n_tok), BF16),
            pltpu.VMEM((1, NX * NX), jnp.int32),
            pltpu.VMEM((2, slots, features), BF16),
            pltpu.VMEM((2, slots, features), BF16),
            pltpu.VMEM((2, slots, hidden_units), F32),
            pltpu.VMEM((2, slots // 2, hidden_units), BF16),
            pltpu.VMEM((2, slots // 2, hidden_units), BF16),
            pltpu.VMEM((2, slots // (2 * NZ), hidden_units), BF16),
            pltpu.VMEM((2, slots // (2 * NZ), hidden_units), BF16),
            pltpu.VMEM((2, 2, slots // (2 * NZ), hidden_units), BF16),
            pltpu.VMEM((2, 2, slots // (2 * NZ), hidden_units), BF16),
            pltpu.VMEM((2, slots, hidden_units), BF16),
            pltpu.VMEM((2, slots, features), BF16),
            dma((7,)),
            dma((2, 2)),
            dma((2,)),
            dma((n_chunks, 2)),
            dma((1,)),
            dma((n_chunks, 2)),
            dma((1,)),
            dma((n_chunks, 2)),
            dma((1,)),
            dma((n_chunks, 2)),
            dma((1,)),
            dma((n_chunks, 2)),
            dma((1,)),
            dma((n_chunks, 2)),
            dma((1,)),
            dma((n_chunks, 2)),
            dma((2,)),
            dma((2,)),
            dma((4,)),
            dma((n_chunks,)),
        ],
        compiler_params=pltpu.CompilerParams(
            collective_id=0, has_side_effects=True, vmem_limit_bytes=VMEM_LIMIT
        ),
        cost_estimate=pl.CostEstimate(
            flops=flops, bytes_accessed=4 * features * hidden_units, transcendentals=slots * hidden_units // 8
        ),
        name="moe_exchange",
    )(tokens, cotangent, routes.T, route_weights.T, capacity_plan[None], up_weight, down_weight)
    return pl.pallas_call(
        combine_kernel,
        out_shape=(
            jax.ShapeDtypeStruct((n_tok, features), BF16),
            jax.ShapeDtypeStruct((n_tok, features), BF16),
            jax.ShapeDtypeStruct((1, features, hidden_units), BF16),
            jax.ShapeDtypeStruct((1, hidden_units, features), BF16),
        ),
        in_specs=[hbm] * 6,
        out_specs=(hbm,) * 4,
        scratch_shapes=[
            pltpu.VMEM((2, NX * NX, CAP, features), BF16),
            pltpu.VMEM((slots, n_tok), BF16),
            pltpu.VMEM((slots, n_tok), BF16),
            pltpu.VMEM((features, slots), BF16),
            pltpu.VMEM((slots, hidden_units), BF16),
            pltpu.VMEM((n_tok, features), BF16),
            pltpu.VMEM((n_tok, features), BF16),
            pltpu.VMEM((features, hidden_units), BF16),
            pltpu.VMEM((hidden_units, features), BF16),
            dma((5,)),
            dma((2,)),
            dma((PIECES,)),
            dma((PIECES,)),
            dma((n_tiles,)),
            dma((n_tiles,)),
        ],
        compiler_params=pltpu.CompilerParams(vmem_limit_bytes=COMBINE_VMEM_LIMIT),
        cost_estimate=pl.CostEstimate(
            flops=4 * slots * n_tok * features, bytes_accessed=8 * features * hidden_units, transcendentals=0
        ),
        name="combine",
    )(returned, placer, weighted, flipped, slope, down_made)


def solution(mesh):
    placed = (
        P("expert", "tensor"),
        P("expert", "tensor"),
        P("expert", None),
        P("expert", None),
        P(),
        P("expert", "tensor", None),
        P("expert", None, "tensor"),
    )
    return jax.shard_map(
        per_device,
        mesh=mesh,
        in_specs=placed,
        out_specs=(
            P("expert", "tensor"),
            P("expert", "tensor"),
            P("expert", "tensor", None),
            P("expert", None, "tensor"),
        ),
        check_vma=False,
    )
```

```python
import functools

import jax
import jax.numpy as jnp
from jax import lax
from jax.experimental import pallas as pl
from jax.experimental.pallas import tpu as pltpu
from jax.sharding import PartitionSpec as P

MESH = pl.DeviceIdType.MESH
F32 = jnp.float32
BF16 = jnp.bfloat16
NX = 4
NZ = 4
CAP = 32
SOURCES = (
    (0, 0), (2, 0), (0, 2), (2, 2),
    (1, 0), (3, 0), (0, 1), (0, 3),
    (1, 1), (3, 3), (1, 3), (3, 1),
    (2, 1), (1, 2), (2, 3), (3, 2),
)
CHUNKS = ((0, 4), (4, 8), (8, 12), (12, 16))
ORDER = (
    "P10", "P00", "P01", "P11", "A10", "P20", "A00", "B10", "A01", "B00", "B01", "A11",
    "C10", "C00", "B11", "P30", "C01", "D10", "P31", "C11", "D00", "A20", "D01", "P21",
    "B20", "D11", "E10", "E01", "A30", "E00", "C20", "A21", "B30", "E11", "A31", "B21",
    "C30", "F01", "F00", "B31", "D20", "F10", "F11", "G00", "C31", "D30", "G10", "E20",
    "C21", "D31", "G11", "E30", "F20", "D21", "G01", "E31", "F30", "X00", "G20", "E21",
    "F31", "G30", "G31", "F21", "G21", "Y00",
)
TILE = 512
PIECES = 4
VMEM_LIMIT = 60 * 1024 * 1024
COMBINE_VMEM_LIMIT = 60 * 1024 * 1024


def contract_last(left, right):
    return lax.dot_general(left, right, (((1,), (1,)), ((), ())), preferred_element_type=F32)


def contract_first(left, right):
    return lax.dot_general(left, right, (((0,), (0,)), ((), ())), preferred_element_type=F32)


def column_tiles(width, tile=TILE):
    return [(start, min(start + tile, width)) for start in range(0, width, tile)]


def wrap(value, size):
    return lax.rem(value + size, size)


def moe_kernel(
    tokens_hbm, cotangent_hbm, routes_hbm, weights_hbm, plan_hbm, up_hbm, down_hbm,
    returned, slope_hbm, flipped_hbm, down_grad, placer_hbm, weighted_hbm,
    up, down, flipped, placer, weighted, tokens, cotangent, routes, route_weights, plan, sent, rows, part, core_out, core_in,
    first_out, first_in, second_out, second_in, acts, results,
    load_sem, own_sem, sent_sem, rows_sem, core_send, core_recv,
    first_send, first_recv, second_send, second_recv,
    near_send, near_recv, far_send, far_recv, mate_send, mate_recv,
    ret_send, ret_recv, store_sem, slope_sem,
):
    expert = lax.axis_index("expert")
    place = lax.axis_index("tensor")
    x, y = lax.div(expert, NX), lax.rem(expert, NX)
    z, core = lax.div(place, 2), lax.rem(place, 2)
    z_next, z_prev, z_far = wrap(z + 1, NZ), wrap(z - 1, NZ), wrap(z + 2, NZ)
    other = 1 - core
    n_tok, features = tokens.shape
    hidden_units = up.shape[1]
    split = ((hidden_units // 128 + 1) // 2) * 128
    tiles = column_tiles(hidden_units)
    half_a, half_b = pl.ds(0, split), pl.ds(split, hidden_units - split)
    n_experts, slots = NX * NX, NX * NX * CAP

    def at_z(which):
        return {"expert": expert, "tensor": which * 2 + core}

    next_chip, prev_chip = at_z(z_next), at_z(z_prev)
    mate = {"expert": expert, "tensor": z * 2 + other}
    owners = [wrap(x - dx, NX) * NX + wrap(y - dy, NX) for dx, dy in SOURCES]
    sources = [wrap(x + dx, NX) * NX + wrap(y + dy, NX) for dx, dy in SOURCES]

    def remote(src, dst, send, recv, device):
        return pltpu.make_async_remote_copy(
            src_ref=src, dst_ref=dst, send_sem=send, recv_sem=recv, device_id=device, device_id_type=MESH
        )

    def await_received(ref, sem):
        remote(ref, ref, sem, sem, mate).wait_recv()

    def await_sent(ref, sem):
        remote(ref, ref, sem, sem, mate).wait_send()

    barrier = pltpu.get_barrier_semaphore()
    load_tokens = pltpu.make_async_copy(tokens_hbm, tokens, load_sem.at[2])
    load_cotangent = pltpu.make_async_copy(cotangent_hbm, cotangent, load_sem.at[3])
    load_up = pltpu.make_async_copy(up_hbm.at[0], up, load_sem.at[0])
    load_down = pltpu.make_async_copy(down_hbm.at[0], down, load_sem.at[1])
    load_routing = [
        pltpu.make_async_copy(source, target, load_sem.at[4 + which])
        for which, (source, target) in enumerate(
            ((routes_hbm, routes), (weights_hbm, route_weights), (plan_hbm, plan))
        )
    ]
    for load in (*load_routing, load_tokens, load_cotangent, load_up, load_down):
        load.start()
    for peer in sources[1:]:
        pl.semaphore_signal(barrier, inc=1, device_id={"expert": peer, "tensor": place}, device_id_type=MESH)
    for device in (next_chip, prev_chip, mate):
        pl.semaphore_signal(barrier, inc=1, device_id=device, device_id_type=MESH)

    for load in load_routing:
        load.wait()

    expert_id = lax.broadcasted_iota(jnp.int32, (n_experts, n_tok), 0)
    first, second = routes[0:1, :], routes[1:2, :]
    named_first = (expert_id == first).astype(F32)
    named_second = (expert_id == second).astype(F32)
    before = lax.broadcasted_iota(jnp.int32, (n_tok, n_tok), 0) < lax.broadcasted_iota(jnp.int32, (n_tok, n_tok), 1)
    earlier = jnp.dot(
        (named_first + named_second).astype(BF16), before.astype(F32).astype(BF16), preferred_element_type=F32
    )
    diagonal = lax.broadcasted_iota(jnp.int32, (n_experts, n_experts), 0) == lax.broadcasted_iota(
        jnp.int32, (n_experts, n_experts), 1
    )
    limit = jnp.sum(jnp.where(diagonal, plan[...].astype(F32), 0.0), axis=1, keepdims=True)
    slot_id = lax.broadcasted_iota(jnp.int32, (slots, n_tok), 0).astype(F32)
    hits = []
    pairs = ((first, named_first, earlier), (second, named_second, earlier + named_first))
    for named_id, named, count in pairs:
        position = jnp.sum(count * named, axis=0, keepdims=True)
        allowed = jnp.sum(limit * named, axis=0, keepdims=True)
        hits.append(slot_id == jnp.where(position < allowed, named_id.astype(F32) * CAP + position, -1.0))
    placer[...] = jnp.where(hits[0], 1.0, jnp.where(hits[1], 1.0, 0.0)).astype(BF16)

    def make_weighted():
        scales = [route_weights[k : k + 1, :].astype(F32) for k in range(2)]
        weighted[...] = jnp.where(hits[0], scales[0], jnp.where(hits[1], scales[1], 0.0)).astype(BF16)
        save_placer.start()
        save_weighted.start()

    def source_rows(s, count=1):
        return pl.ds(s * CAP, count * CAP)

    def chunk_rows(c):
        lo, hi = CHUNKS[c]
        return pl.ds(lo * CAP, (hi - lo) * CAP)

    def block_size(c):
        lo, hi = CHUNKS[c]
        return (hi - lo) * CAP // (2 * NZ)

    def block(c, side, which, count=1):
        size = block_size(c)
        return pl.ds(pl.multiple_of(CHUNKS[c][0] * CAP + (side * NZ + which) * size, 16), count * size)

    def half_block(c, which, count=1):
        size = block_size(c)
        return pl.ds(pl.multiple_of(CHUNKS[c][0] * CAP // 2 + which * size, 16), count * size)

    def small_block(c):
        return pl.ds(CHUNKS[c][0] * CAP // (2 * NZ), block_size(c))

    def remote_sources(c):
        lo, hi = CHUNKS[c]
        return range(max(lo, 1), hi)

    dispatch_order = [(int(step[1]), int(step[2])) for step in ORDER if step[0] == "P"]

    def make_rows(c, k):
        matrix, picker = ((tokens, placer), (cotangent, weighted))[k]
        is_first = (c, k) == next((at, kind) for at, kind in dispatch_order if kind == k)
        if is_first:
            (load_tokens, load_cotangent)[k].wait()
            if k == 1:
                make_weighted()
        picked = [picker[pl.ds(pl.multiple_of(owners[s] * CAP, CAP), CAP), :] for s in range(*CHUNKS[c])]
        sent[k, chunk_rows(c), :] = jnp.dot(
            jnp.concatenate(picked, axis=0), matrix[...], preferred_element_type=F32
        ).astype(BF16)
        if c == 0:
            own_rows(k).start()
        if (c, k) == dispatch_order[0]:
            pl.semaphore_wait(barrier, n_experts - 1 + 3)
        for s in remote_sources(c):
            remote(
                sent.at[k, source_rows(s)], rows.at[k, source_rows(s)], sent_sem.at[k], rows_sem.at[c, k],
                {"expert": owners[s], "tensor": place},
            ).start()

    def own_rows(k):
        return pltpu.make_async_copy(sent.at[k, source_rows(0)], rows.at[k, source_rows(0)], own_sem.at[0, k])

    def own_back(k):
        return pltpu.make_async_copy(results.at[k, source_rows(0)], returned.at[k, expert], own_sem.at[1, k])

    partial_order = [(int(step[1]), int(step[2])) for step in ORDER if step[0] == "A"]

    def stage_partial(c, k):
        if c == 0:
            own_rows(k).wait()
        if (c, k) == next((step_c, step_k) for step_c, step_k in partial_order if step_k == k):
            (load_up if k == 0 else load_down).wait()
        arriving = remote_sources(c)
        await_received(rows.at[k, source_rows(arriving[0], len(arriving))], rows_sem.at[c, k])
        taken = rows[k, chunk_rows(c), :]
        for lo, hi in tiles:
            if k == 0:
                product = jnp.dot(taken, up[:, lo:hi], preferred_element_type=F32)
            else:
                product = contract_last(taken, down[lo:hi, :])
            part[k, chunk_rows(c), lo:hi] = product
        away = half_block(c, 0, NZ)
        core_out[k, away, :] = part[k, block(c, other, 0, NZ), :].astype(BF16)
        remote(core_out.at[k, away], core_in.at[k, away], core_send.at[0], core_recv.at[c, k], mate).start()

    def chip_sum(c, k, which, half):
        return part[k, block(c, core, which), half] + core_in[k, half_block(c, which), half].astype(F32)

    def send_second(c, k, side, half):
        remote(
            second_out.at[k, side, small_block(c), half], second_in.at[k, side, small_block(c), half],
            second_send.at[0], second_recv.at[c, k], next_chip if side == 0 else prev_chip,
        ).start()

    def stage_core(c, k):
        await_received(core_in.at[k, half_block(c, 0, NZ)], core_recv.at[c, k])
        here = small_block(c)
        for half in (half_a, half_b):
            first_out[k, here, half] = chip_sum(c, k, z_far, half).astype(BF16)
        second_out[k, 0, here, half_b] = chip_sum(c, k, z_next, half_b).astype(BF16)
        second_out[k, 1, here, half_a] = chip_sum(c, k, z_prev, half_a).astype(BF16)
        for half, device in ((half_a, next_chip), (half_b, prev_chip)):
            remote(
                first_out.at[k, here, half], first_in.at[k, here, half], first_send.at[0], first_recv.at[c, k], device
            ).start()
        send_second(c, k, 0, half_b)
        send_second(c, k, 1, half_a)

    def stage_relay(c, k):
        here = small_block(c)
        relays = ((0, z_next, half_a), (1, z_prev, half_b))
        await_received(first_in.at[k, here], first_recv.at[c, k])
        for side, which, half in relays:
            total = chip_sum(c, k, which, half) + first_in[k, here, half].astype(F32)
            second_out[k, side, here, half] = total.astype(BF16)
        for side, which, half in relays:
            send_second(c, k, side, half)

    def stage_activate(c, k):
        here = small_block(c)
        await_received(second_in.at[k, :, here], second_recv.at[c, k])
        total = chip_sum(c, k, z, pl.ds(0, hidden_units))
        total = total + (second_in[k, 0, here, :].astype(F32) + second_in[k, 1, here, :].astype(F32))
        mine = block(c, core, z)
        if k == 0:
            part[0, mine, :] = total
            acts[0, mine, :] = (total * jax.nn.sigmoid(total)).astype(BF16)
        else:
            pre = part[0, mine, :]
            gate = jax.nn.sigmoid(pre)
            acts[1, mine, :] = (total * gate * (1.0 + pre * (1.0 - gate))).astype(BF16)
        ref = acts.at[k, mine]
        remote(ref, ref, near_send.at[0], near_recv.at[c, k], next_chip).start()
        remote(ref, ref, near_send.at[0], near_recv.at[c, k], prev_chip).start()

    def stage_forward(c, k):
        await_received(acts.at[k, block(c, core, 0, 2)], near_recv.at[c, k])
        for which, half, device in ((z_prev, half_a, next_chip), (z_next, half_b, prev_chip)):
            ref = acts.at[k, block(c, core, which), half]
            remote(ref, ref, far_send.at[0], far_recv.at[c, k], device).start()

    def stage_last(c, k):
        await_received(acts.at[k, block(c, core, z_far)], far_recv.at[c, k])
        ref = acts.at[k, block(c, core, 0, NZ)]
        remote(ref, ref, mate_send.at[0], mate_recv.at[c, k], mate).start()

    def stage_result(c, k):
        await_received(acts.at[k, block(c, other, 0, NZ)], mate_recv.at[c, k])
        taken = acts[k, chunk_rows(c), :]
        for lo, hi in column_tiles(features):
            if k == 0:
                product = jnp.dot(taken, down[:, lo:hi], preferred_element_type=F32)
            else:
                product = contract_last(taken, up[lo:hi, :])
            results[k, chunk_rows(c), lo:hi] = product.astype(BF16)
        if c == 0:
            own_back(k).start()
        for s in remote_sources(c):
            remote(
                results.at[k, source_rows(s)], returned.at[k, expert], ret_send.at[k], ret_recv.at[k],
                {"expert": sources[s], "tensor": place},
            ).start()
        if k == 1:
            save_slope(c).start()

    def stage_flip(c, k):
        flipped[...] = rows[0].T
        save_flipped.start()

    def stage_down_grad(c, k):
        for lo, hi in tiles:
            down[lo:hi, :] = contract_first(acts[0, :, lo:hi], rows[1]).astype(BF16)
        save_down.start()

    save_placer = pltpu.make_async_copy(placer, placer_hbm, store_sem.at[0])
    save_weighted = pltpu.make_async_copy(weighted, weighted_hbm, store_sem.at[1])
    save_flipped = pltpu.make_async_copy(flipped, flipped_hbm, store_sem.at[2])
    save_down = pltpu.make_async_copy(down, down_grad.at[0], store_sem.at[3])

    def save_slope(c):
        return pltpu.make_async_copy(acts.at[1, chunk_rows(c)], slope_hbm.at[chunk_rows(c)], slope_sem.at[c])

    stages = {
        "P": make_rows, "A": stage_partial, "B": stage_core, "C": stage_relay, "D": stage_activate,
        "E": stage_forward, "F": stage_last, "G": stage_result, "X": stage_flip, "Y": stage_down_grad,
    }

    for step in ORDER:
        stages[step[0]](int(step[1]), int(step[2]))

    for k in range(2):
        await_sent(sent.at[k, source_rows(1, n_experts - 1)], sent_sem.at[k])
        own_back(k).wait()
    for save in (save_placer, save_weighted, save_flipped, *map(save_slope, range(len(CHUNKS)))):
        save.wait()
    quarter = slots // NZ
    await_sent(core_out, core_send.at[0])
    await_sent(first_out, first_send.at[0])
    await_sent(second_out, second_send.at[0])
    await_sent(acts.at[:, pl.ds(0, quarter)], near_send.at[0])
    await_sent(acts.at[:, pl.ds(0, quarter // 2)], far_send.at[0])
    await_sent(acts.at[:, pl.ds(0, 2 * quarter)], mate_send.at[0])
    for k in range(2):
        await_received(returned.at[k, pl.ds(0, n_experts - 1)], ret_recv.at[k])
        await_sent(results.at[k, source_rows(1, n_experts - 1)], ret_send.at[k])
    save_down.wait()


def combine_kernel(
    returned_hbm, placer_hbm, weighted_hbm, flipped_hbm, slope_hbm, down_hbm,
    layer_hbm, token_hbm, up_grad, down_grad,
    returned, placer, weighted, flipped, slope, layer_out, token_grad, up, down,
    load_sem, out_sem, in_sem, copy_sem, slope_sem, up_sem,
):
    slots, features = placer.shape[0], layer_out.shape[1]
    hidden_units = up.shape[1]
    tiles = column_tiles(hidden_units)
    load_flipped = pltpu.make_async_copy(flipped_hbm, flipped, load_sem.at[4])
    load_slope = [
        pltpu.make_async_copy(slope_hbm.at[:, lo:hi], slope.at[:, lo:hi], slope_sem.at[index])
        for index, (lo, hi) in enumerate(tiles)
    ]
    parts = (
        (
            pltpu.make_async_copy(weighted_hbm, weighted, load_sem.at[0]),
            pltpu.make_async_copy(returned_hbm.at[0], returned.at[0], load_sem.at[1]),
        ),
        (
            pltpu.make_async_copy(placer_hbm, placer, load_sem.at[2]),
            pltpu.make_async_copy(returned_hbm.at[1], returned.at[1], load_sem.at[3]),
        ),
    )
    size = hidden_units // PIECES
    picks = [pl.ds(piece * size, size) for piece in range(PIECES)]
    loads = [
        pltpu.make_async_copy(down_hbm.at[0, pick], down.at[pick], in_sem.at[piece])
        for piece, pick in enumerate(picks)
    ]
    stores = [
        pltpu.make_async_copy(down.at[pick], down_grad.at[0, pick], copy_sem.at[piece])
        for piece, pick in enumerate(picks)
    ]
    outs = [
        pltpu.make_async_copy(layer_out, layer_hbm, out_sem.at[0]),
        pltpu.make_async_copy(token_grad, token_hbm, out_sem.at[1]),
    ]
    up_stores = [
        pltpu.make_async_copy(up.at[:, lo:hi], up_grad.at[0, :, lo:hi], up_sem.at[index])
        for index, (lo, hi) in enumerate(tiles)
    ]
    for load in (load_flipped, load_slope[0], loads[0], *load_slope[1:], *loads[1:], *parts[0], *parts[1]):
        load.start()
    load_flipped.wait()
    for index, (lo, hi) in enumerate(tiles):
        load_slope[index].wait()
        up[:, lo:hi] = jnp.dot(flipped[...], slope[:, lo:hi], preferred_element_type=F32).astype(BF16)
        up_stores[index].start()
        if index < PIECES:
            loads[index].wait()
            stores[index].start()
    for part, picker, result, out, k in zip(parts, (weighted, placer), (layer_out, token_grad), outs, range(2)):
        for load in part:
            load.wait()
        result[...] = contract_first(picker[...], returned[k].reshape(slots, features)).astype(BF16)
        out.start()
    for copy in (*up_stores, *stores, *outs):
        copy.wait()


def per_device(tokens, cotangent, routes, route_weights, capacity_plan, up_weight, down_weight):
    n_tok, features = tokens.shape
    hidden_units = up_weight.shape[2]
    slots = NX * NX * CAP
    hbm = pl.BlockSpec(memory_space=pl.ANY)
    dma = pltpu.SemaphoreType.DMA
    flops = 12 * slots * features * hidden_units
    n_chunks = len(CHUNKS)
    n_tiles = len(column_tiles(hidden_units))
    returned, slope, flipped, down_made, placer, weighted = pl.pallas_call(
        moe_kernel,
        out_shape=(
            jax.ShapeDtypeStruct((2, NX * NX, CAP, features), BF16),
            jax.ShapeDtypeStruct((slots, hidden_units), BF16),
            jax.ShapeDtypeStruct((features, slots), BF16),
            jax.ShapeDtypeStruct((1, hidden_units, features), BF16),
            jax.ShapeDtypeStruct((slots, n_tok), BF16),
            jax.ShapeDtypeStruct((slots, n_tok), BF16),
        ),
        in_specs=[pl.BlockSpec(memory_space=pltpu.HBM)] * 7,
        out_specs=(hbm,) * 6,
        scratch_shapes=[
            pltpu.VMEM((features, hidden_units), BF16),
            pltpu.VMEM((hidden_units, features), BF16),
            pltpu.VMEM((features, slots), BF16),
            pltpu.VMEM((slots, n_tok), BF16),
            pltpu.VMEM((slots, n_tok), BF16),
            pltpu.VMEM((n_tok, features), BF16),
            pltpu.VMEM((n_tok, features), BF16),
            pltpu.VMEM((2, n_tok), jnp.int32),
            pltpu.VMEM((2, n_tok), BF16),
            pltpu.VMEM((1, NX * NX), jnp.int32),
            pltpu.VMEM((2, slots, features), BF16),
            pltpu.VMEM((2, slots, features), BF16),
            pltpu.VMEM((2, slots, hidden_units), F32),
            pltpu.VMEM((2, slots // 2, hidden_units), BF16),
            pltpu.VMEM((2, slots // 2, hidden_units), BF16),
            pltpu.VMEM((2, slots // (2 * NZ), hidden_units), BF16),
            pltpu.VMEM((2, slots // (2 * NZ), hidden_units), BF16),
            pltpu.VMEM((2, 2, slots // (2 * NZ), hidden_units), BF16),
            pltpu.VMEM((2, 2, slots // (2 * NZ), hidden_units), BF16),
            pltpu.VMEM((2, slots, hidden_units), BF16),
            pltpu.VMEM((2, slots, features), BF16),
            dma((7,)),
            dma((2, 2)),
            dma((2,)),
            dma((n_chunks, 2)),
            dma((1,)),
            dma((n_chunks, 2)),
            dma((1,)),
            dma((n_chunks, 2)),
            dma((1,)),
            dma((n_chunks, 2)),
            dma((1,)),
            dma((n_chunks, 2)),
            dma((1,)),
            dma((n_chunks, 2)),
            dma((1,)),
            dma((n_chunks, 2)),
            dma((2,)),
            dma((2,)),
            dma((4,)),
            dma((n_chunks,)),
        ],
        compiler_params=pltpu.CompilerParams(
            collective_id=0, has_side_effects=True, vmem_limit_bytes=VMEM_LIMIT
        ),
        cost_estimate=pl.CostEstimate(
            flops=flops, bytes_accessed=4 * features * hidden_units, transcendentals=slots * hidden_units // 8
        ),
        name="moe_exchange",
    )(tokens, cotangent, routes.T, route_weights.T, capacity_plan[None], up_weight, down_weight)
    return pl.pallas_call(
        combine_kernel,
        out_shape=(
            jax.ShapeDtypeStruct((n_tok, features), BF16),
            jax.ShapeDtypeStruct((n_tok, features), BF16),
            jax.ShapeDtypeStruct((1, features, hidden_units), BF16),
            jax.ShapeDtypeStruct((1, hidden_units, features), BF16),
        ),
        in_specs=[hbm] * 6,
        out_specs=(hbm,) * 4,
        scratch_shapes=[
            pltpu.VMEM((2, NX * NX, CAP, features), BF16),
            pltpu.VMEM((slots, n_tok), BF16),
            pltpu.VMEM((slots, n_tok), BF16),
            pltpu.VMEM((features, slots), BF16),
            pltpu.VMEM((slots, hidden_units), BF16),
            pltpu.VMEM((n_tok, features), BF16),
            pltpu.VMEM((n_tok, features), BF16),
            pltpu.VMEM((features, hidden_units), BF16),
            pltpu.VMEM((hidden_units, features), BF16),
            dma((5,)),
            dma((2,)),
            dma((PIECES,)),
            dma((PIECES,)),
            dma((n_tiles,)),
            dma((n_tiles,)),
        ],
        compiler_params=pltpu.CompilerParams(vmem_limit_bytes=COMBINE_VMEM_LIMIT),
        cost_estimate=pl.CostEstimate(
            flops=4 * slots * n_tok * features, bytes_accessed=8 * features * hidden_units, transcendentals=0
        ),
        name="combine",
    )(returned, placer, weighted, flipped, slope, down_made)


def solution(mesh):
    placed = (
        P("expert", "tensor"),
        P("expert", "tensor"),
        P("expert", None),
        P("expert", None),
        P(),
        P("expert", "tensor", None),
        P("expert", None, "tensor"),
    )
    return jax.shard_map(
        per_device,
        mesh=mesh,
        in_specs=placed,
        out_specs=(
            P("expert", "tensor"),
            P("expert", "tensor"),
            P("expert", "tensor", None),
            P("expert", None, "tensor"),
        ),
        check_vma=False,
    )
```

```python
import functools

import jax
import jax.numpy as jnp
from jax import lax
from jax.experimental import pallas as pl
from jax.experimental.pallas import tpu as pltpu
from jax.sharding import PartitionSpec as P

MESH = pl.DeviceIdType.MESH
F32 = jnp.float32
BF16 = jnp.bfloat16
NX = 4
NZ = 4
CAP = 32
SOURCES = (
    (0, 0), (2, 0), (0, 2), (2, 2),
    (1, 0), (3, 0), (0, 1), (0, 3),
    (1, 1), (3, 3), (1, 3), (3, 1),
    (2, 1), (1, 2), (2, 3), (3, 2),
)
CHUNKS = ((0, 4), (4, 8), (8, 12), (12, 16))
ORDER = (
    "P10", "P11", "P00", "P01", "A10", "A11", "P20", "B11", "B10", "A00", "P21", "C11",
    "A01", "B00", "C10", "B01", "A20", "C00", "P30", "B20", "D10", "A21", "D00", "P31",
    "C01", "C20", "D11", "E00", "E10", "B21", "D01", "A30", "F10", "D20", "A31", "F00",
    "B30", "E01", "B31", "G10", "C30", "E20", "E11", "C31", "G00", "F01", "D30", "F20",
    "C21", "F11", "G01", "D31", "G11", "E30", "D21", "G20", "E31", "X00", "F30", "G30",
    "F31", "E21", "G31", "F21", "G21", "Y00",
)
TILE = 512
PIECES = 4
VMEM_LIMIT = 60 * 1024 * 1024
COMBINE_VMEM_LIMIT = 60 * 1024 * 1024


def contract_last(left, right):
    return lax.dot_general(left, right, (((1,), (1,)), ((), ())), preferred_element_type=F32)


def contract_first(left, right):
    return lax.dot_general(left, right, (((0,), (0,)), ((), ())), preferred_element_type=F32)


def column_tiles(width, tile=TILE):
    return [(start, min(start + tile, width)) for start in range(0, width, tile)]


def wrap(value, size):
    return lax.rem(value + size, size)


def moe_kernel(
    tokens_hbm, cotangent_hbm, routes_hbm, weights_hbm, plan_hbm, up_hbm, down_hbm,
    returned, slope_hbm, flipped_hbm, down_grad, placer_hbm, weighted_hbm,
    up, down, flipped, placer, weighted, tokens, cotangent, routes, route_weights, plan, sent, rows, part, core_out, core_in,
    first_out, first_in, second_out, second_in, acts, results,
    load_sem, own_sem, sent_sem, rows_sem, core_send, core_recv,
    first_send, first_recv, second_send, second_recv,
    near_send, near_recv, far_send, far_recv, mate_send, mate_recv,
    ret_send, ret_recv, store_sem, slope_sem,
):
    expert = lax.axis_index("expert")
    place = lax.axis_index("tensor")
    x, y = lax.div(expert, NX), lax.rem(expert, NX)
    z, core = lax.div(place, 2), lax.rem(place, 2)
    z_next, z_prev, z_far = wrap(z + 1, NZ), wrap(z - 1, NZ), wrap(z + 2, NZ)
    other = 1 - core
    n_tok, features = tokens.shape
    hidden_units = up.shape[1]
    split = ((hidden_units // 128 + 1) // 2) * 128
    tiles = column_tiles(hidden_units)
    half_a, half_b = pl.ds(0, split), pl.ds(split, hidden_units - split)
    n_experts, slots = NX * NX, NX * NX * CAP

    def at_z(which):
        return {"expert": expert, "tensor": which * 2 + core}

    next_chip, prev_chip = at_z(z_next), at_z(z_prev)
    mate = {"expert": expert, "tensor": z * 2 + other}
    owners = [wrap(x - dx, NX) * NX + wrap(y - dy, NX) for dx, dy in SOURCES]
    sources = [wrap(x + dx, NX) * NX + wrap(y + dy, NX) for dx, dy in SOURCES]

    def remote(src, dst, send, recv, device):
        return pltpu.make_async_remote_copy(
            src_ref=src, dst_ref=dst, send_sem=send, recv_sem=recv, device_id=device, device_id_type=MESH
        )

    def await_received(ref, sem):
        remote(ref, ref, sem, sem, mate).wait_recv()

    def await_sent(ref, sem):
        remote(ref, ref, sem, sem, mate).wait_send()

    barrier = pltpu.get_barrier_semaphore()
    load_tokens = pltpu.make_async_copy(tokens_hbm, tokens, load_sem.at[2])
    load_cotangent = pltpu.make_async_copy(cotangent_hbm, cotangent, load_sem.at[3])
    load_up = pltpu.make_async_copy(up_hbm.at[0], up, load_sem.at[0])
    load_down = pltpu.make_async_copy(down_hbm.at[0], down, load_sem.at[1])
    load_routing = [
        pltpu.make_async_copy(source, target, load_sem.at[4 + which])
        for which, (source, target) in enumerate(
            ((routes_hbm, routes), (weights_hbm, route_weights), (plan_hbm, plan))
        )
    ]
    for load in (*load_routing, load_tokens):
        load.start()
    for peer in sources[1:]:
        pl.semaphore_signal(barrier, inc=1, device_id={"expert": peer, "tensor": place}, device_id_type=MESH)
    for device in (next_chip, prev_chip, mate):
        pl.semaphore_signal(barrier, inc=1, device_id=device, device_id_type=MESH)

    for load in load_routing:
        load.wait()

    expert_id = lax.broadcasted_iota(jnp.int32, (n_experts, n_tok), 0)
    first, second = routes[0:1, :], routes[1:2, :]
    named_first = (expert_id == first).astype(F32)
    named_second = (expert_id == second).astype(F32)
    before = lax.broadcasted_iota(jnp.int32, (n_tok, n_tok), 0) < lax.broadcasted_iota(jnp.int32, (n_tok, n_tok), 1)
    earlier = jnp.dot(
        (named_first + named_second).astype(BF16), before.astype(F32).astype(BF16), preferred_element_type=F32
    )
    diagonal = lax.broadcasted_iota(jnp.int32, (n_experts, n_experts), 0) == lax.broadcasted_iota(
        jnp.int32, (n_experts, n_experts), 1
    )
    limit = jnp.sum(jnp.where(diagonal, plan[...].astype(F32), 0.0), axis=1, keepdims=True)
    slot_id = lax.broadcasted_iota(jnp.int32, (slots, n_tok), 0).astype(F32)
    hits = []
    pairs = ((first, named_first, earlier), (second, named_second, earlier + named_first))
    for named_id, named, count in pairs:
        position = jnp.sum(count * named, axis=0, keepdims=True)
        allowed = jnp.sum(limit * named, axis=0, keepdims=True)
        hits.append(slot_id == jnp.where(position < allowed, named_id.astype(F32) * CAP + position, -1.0))
    placer[...] = jnp.where(hits[0], 1.0, jnp.where(hits[1], 1.0, 0.0)).astype(BF16)

    def make_weighted():
        scales = [route_weights[k : k + 1, :].astype(F32) for k in range(2)]
        weighted[...] = jnp.where(hits[0], scales[0], jnp.where(hits[1], scales[1], 0.0)).astype(BF16)
        save_placer.start()
        save_weighted.start()

    def source_rows(s, count=1):
        return pl.ds(s * CAP, count * CAP)

    def chunk_rows(c):
        lo, hi = CHUNKS[c]
        return pl.ds(lo * CAP, (hi - lo) * CAP)

    def block_size(c):
        lo, hi = CHUNKS[c]
        return (hi - lo) * CAP // (2 * NZ)

    def block(c, side, which, count=1):
        size = block_size(c)
        return pl.ds(pl.multiple_of(CHUNKS[c][0] * CAP + (side * NZ + which) * size, 16), count * size)

    def half_block(c, which, count=1):
        size = block_size(c)
        return pl.ds(pl.multiple_of(CHUNKS[c][0] * CAP // 2 + which * size, 16), count * size)

    def small_block(c):
        return pl.ds(CHUNKS[c][0] * CAP // (2 * NZ), block_size(c))

    def remote_sources(c):
        lo, hi = CHUNKS[c]
        return range(max(lo, 1), hi)

    dispatch_order = [(int(step[1]), int(step[2])) for step in ORDER if step[0] == "P"]

    def make_rows(c, k):
        matrix, picker = ((tokens, placer), (cotangent, weighted))[k]
        is_first = (c, k) == next((at, kind) for at, kind in dispatch_order if kind == k)
        if is_first:
            (load_tokens, load_cotangent)[k].wait()
            if k == 1:
                make_weighted()
        picked = [picker[pl.ds(pl.multiple_of(owners[s] * CAP, CAP), CAP), :] for s in range(*CHUNKS[c])]
        sent[k, chunk_rows(c), :] = jnp.dot(
            jnp.concatenate(picked, axis=0), matrix[...], preferred_element_type=F32
        ).astype(BF16)
        if c == 0:
            own_rows(k).start()
        if (c, k) == dispatch_order[0]:
            pl.semaphore_wait(barrier, n_experts - 1 + 3)
        for s in remote_sources(c):
            remote(
                sent.at[k, source_rows(s)], rows.at[k, source_rows(s)], sent_sem.at[k], rows_sem.at[c, k],
                {"expert": owners[s], "tensor": place},
            ).start()
        if (c, k) == dispatch_order[0]:
            for load in (load_cotangent, load_up, load_down):
                load.start()

    def own_rows(k):
        return pltpu.make_async_copy(sent.at[k, source_rows(0)], rows.at[k, source_rows(0)], own_sem.at[0, k])

    def own_back(k):
        return pltpu.make_async_copy(results.at[k, source_rows(0)], returned.at[k, expert], own_sem.at[1, k])

    partial_order = [(int(step[1]), int(step[2])) for step in ORDER if step[0] == "A"]

    def stage_partial(c, k):
        if c == 0:
            own_rows(k).wait()
        if (c, k) == next((step_c, step_k) for step_c, step_k in partial_order if step_k == k):
            (load_up if k == 0 else load_down).wait()
        arriving = remote_sources(c)
        await_received(rows.at[k, source_rows(arriving[0], len(arriving))], rows_sem.at[c, k])
        taken = rows[k, chunk_rows(c), :]
        for lo, hi in tiles:
            if k == 0:
                product = jnp.dot(taken, up[:, lo:hi], preferred_element_type=F32)
            else:
                product = contract_last(taken, down[lo:hi, :])
            part[k, chunk_rows(c), lo:hi] = product
        away = half_block(c, 0, NZ)
        core_out[k, away, :] = part[k, block(c, other, 0, NZ), :].astype(BF16)
        remote(core_out.at[k, away], core_in.at[k, away], core_send.at[0], core_recv.at[c, k], mate).start()

    def chip_sum(c, k, which, half):
        return part[k, block(c, core, which), half] + core_in[k, half_block(c, which), half].astype(F32)

    def send_second(c, k, side, half):
        remote(
            second_out.at[k, side, small_block(c), half], second_in.at[k, side, small_block(c), half],
            second_send.at[0], second_recv.at[c, k], next_chip if side == 0 else prev_chip,
        ).start()

    def stage_core(c, k):
        await_received(core_in.at[k, half_block(c, 0, NZ)], core_recv.at[c, k])
        here = small_block(c)
        for half in (half_a, half_b):
            first_out[k, here, half] = chip_sum(c, k, z_far, half).astype(BF16)
        second_out[k, 0, here, half_b] = chip_sum(c, k, z_next, half_b).astype(BF16)
        second_out[k, 1, here, half_a] = chip_sum(c, k, z_prev, half_a).astype(BF16)
        for half, device in ((half_a, next_chip), (half_b, prev_chip)):
            remote(
                first_out.at[k, here, half], first_in.at[k, here, half], first_send.at[0], first_recv.at[c, k], device
            ).start()
        send_second(c, k, 0, half_b)
        send_second(c, k, 1, half_a)

    def stage_relay(c, k):
        here = small_block(c)
        relays = ((0, z_next, half_a), (1, z_prev, half_b))
        await_received(first_in.at[k, here], first_recv.at[c, k])
        for side, which, half in relays:
            total = chip_sum(c, k, which, half) + first_in[k, here, half].astype(F32)
            second_out[k, side, here, half] = total.astype(BF16)
        for side, which, half in relays:
            send_second(c, k, side, half)

    def stage_activate(c, k):
        here = small_block(c)
        await_received(second_in.at[k, :, here], second_recv.at[c, k])
        total = chip_sum(c, k, z, pl.ds(0, hidden_units))
        total = total + (second_in[k, 0, here, :].astype(F32) + second_in[k, 1, here, :].astype(F32))
        mine = block(c, core, z)
        if k == 0:
            part[0, mine, :] = total
            acts[0, mine, :] = (total * jax.nn.sigmoid(total)).astype(BF16)
        else:
            pre = part[0, mine, :]
            gate = jax.nn.sigmoid(pre)
            acts[1, mine, :] = (total * gate * (1.0 + pre * (1.0 - gate))).astype(BF16)
        ref = acts.at[k, mine]
        remote(ref, ref, near_send.at[0], near_recv.at[c, k], next_chip).start()
        remote(ref, ref, near_send.at[0], near_recv.at[c, k], prev_chip).start()

    def stage_forward(c, k):
        await_received(acts.at[k, block(c, core, 0, 2)], near_recv.at[c, k])
        for which, half, device in ((z_prev, half_a, next_chip), (z_next, half_b, prev_chip)):
            ref = acts.at[k, block(c, core, which), half]
            remote(ref, ref, far_send.at[0], far_recv.at[c, k], device).start()

    def stage_last(c, k):
        await_received(acts.at[k, block(c, core, z_far)], far_recv.at[c, k])
        ref = acts.at[k, block(c, core, 0, NZ)]
        remote(ref, ref, mate_send.at[0], mate_recv.at[c, k], mate).start()

    def stage_result(c, k):
        await_received(acts.at[k, block(c, other, 0, NZ)], mate_recv.at[c, k])
        taken = acts[k, chunk_rows(c), :]
        for lo, hi in column_tiles(features):
            if k == 0:
                product = jnp.dot(taken, down[:, lo:hi], preferred_element_type=F32)
            else:
                product = contract_last(taken, up[lo:hi, :])
            results[k, chunk_rows(c), lo:hi] = product.astype(BF16)
        if c == 0:
            own_back(k).start()
        for s in remote_sources(c):
            remote(
                results.at[k, source_rows(s)], returned.at[k, expert], ret_send.at[k], ret_recv.at[k],
                {"expert": sources[s], "tensor": place},
            ).start()
        if k == 1:
            save_slope(c).start()

    def stage_flip(c, k):
        flipped[...] = rows[0].T
        save_flipped.start()

    def stage_down_grad(c, k):
        for lo, hi in tiles:
            down[lo:hi, :] = contract_first(acts[0, :, lo:hi], rows[1]).astype(BF16)
        save_down.start()

    save_placer = pltpu.make_async_copy(placer, placer_hbm, store_sem.at[0])
    save_weighted = pltpu.make_async_copy(weighted, weighted_hbm, store_sem.at[1])
    save_flipped = pltpu.make_async_copy(flipped, flipped_hbm, store_sem.at[2])
    save_down = pltpu.make_async_copy(down, down_grad.at[0], store_sem.at[3])

    def save_slope(c):
        return pltpu.make_async_copy(acts.at[1, chunk_rows(c)], slope_hbm.at[chunk_rows(c)], slope_sem.at[c])

    stages = {
        "P": make_rows, "A": stage_partial, "B": stage_core, "C": stage_relay, "D": stage_activate,
        "E": stage_forward, "F": stage_last, "G": stage_result, "X": stage_flip, "Y": stage_down_grad,
    }

    for step in ORDER:
        stages[step[0]](int(step[1]), int(step[2]))

    for k in range(2):
        await_sent(sent.at[k, source_rows(1, n_experts - 1)], sent_sem.at[k])
        own_back(k).wait()
    for save in (save_placer, save_weighted, save_flipped, *map(save_slope, range(len(CHUNKS)))):
        save.wait()
    quarter = slots // NZ
    await_sent(core_out, core_send.at[0])
    await_sent(first_out, first_send.at[0])
    await_sent(second_out, second_send.at[0])
    await_sent(acts.at[:, pl.ds(0, quarter)], near_send.at[0])
    await_sent(acts.at[:, pl.ds(0, quarter // 2)], far_send.at[0])
    await_sent(acts.at[:, pl.ds(0, 2 * quarter)], mate_send.at[0])
    for k in range(2):
        await_received(returned.at[k, pl.ds(0, n_experts - 1)], ret_recv.at[k])
        await_sent(results.at[k, source_rows(1, n_experts - 1)], ret_send.at[k])
    save_down.wait()


def combine_kernel(
    returned_hbm, placer_hbm, weighted_hbm, flipped_hbm, slope_hbm, down_hbm,
    layer_hbm, token_hbm, up_grad, down_grad,
    returned, placer, weighted, flipped, slope, layer_out, token_grad, up, down,
    load_sem, out_sem, in_sem, copy_sem, slope_sem, up_sem,
):
    slots, features = placer.shape[0], layer_out.shape[1]
    hidden_units = up.shape[1]
    tiles = column_tiles(hidden_units)
    load_flipped = pltpu.make_async_copy(flipped_hbm, flipped, load_sem.at[4])
    load_slope = [
        pltpu.make_async_copy(slope_hbm.at[:, lo:hi], slope.at[:, lo:hi], slope_sem.at[index])
        for index, (lo, hi) in enumerate(tiles)
    ]
    parts = (
        (
            pltpu.make_async_copy(weighted_hbm, weighted, load_sem.at[0]),
            pltpu.make_async_copy(returned_hbm.at[0], returned.at[0], load_sem.at[1]),
        ),
        (
            pltpu.make_async_copy(placer_hbm, placer, load_sem.at[2]),
            pltpu.make_async_copy(returned_hbm.at[1], returned.at[1], load_sem.at[3]),
        ),
    )
    size = hidden_units // PIECES
    picks = [pl.ds(piece * size, size) for piece in range(PIECES)]
    loads = [
        pltpu.make_async_copy(down_hbm.at[0, pick], down.at[pick], in_sem.at[piece])
        for piece, pick in enumerate(picks)
    ]
    stores = [
        pltpu.make_async_copy(down.at[pick], down_grad.at[0, pick], copy_sem.at[piece])
        for piece, pick in enumerate(picks)
    ]
    outs = [
        pltpu.make_async_copy(layer_out, layer_hbm, out_sem.at[0]),
        pltpu.make_async_copy(token_grad, token_hbm, out_sem.at[1]),
    ]
    up_stores = [
        pltpu.make_async_copy(up.at[:, lo:hi], up_grad.at[0, :, lo:hi], up_sem.at[index])
        for index, (lo, hi) in enumerate(tiles)
    ]
    for load in (load_flipped, *load_slope[:2]):
        load.start()
    load_flipped.wait()
    for index, (lo, hi) in enumerate(tiles):
        load_slope[index].wait()
        if index == 0:
            for load in (loads[0], *load_slope[2:], *loads[1:], *parts[0], *parts[1]):
                load.start()
        up[:, lo:hi] = jnp.dot(flipped[...], slope[:, lo:hi], preferred_element_type=F32).astype(BF16)
        up_stores[index].start()
        if index < PIECES:
            loads[index].wait()
            stores[index].start()
    for part, picker, result, out, k in zip(parts, (weighted, placer), (layer_out, token_grad), outs, range(2)):
        for load in part:
            load.wait()
        result[...] = contract_first(picker[...], returned[k].reshape(slots, features)).astype(BF16)
        out.start()
    for copy in (*up_stores, *stores, *outs):
        copy.wait()


def per_device(tokens, cotangent, routes, route_weights, capacity_plan, up_weight, down_weight):
    n_tok, features = tokens.shape
    hidden_units = up_weight.shape[2]
    slots = NX * NX * CAP
    hbm = pl.BlockSpec(memory_space=pl.ANY)
    dma = pltpu.SemaphoreType.DMA
    flops = 12 * slots * features * hidden_units
    n_chunks = len(CHUNKS)
    n_tiles = len(column_tiles(hidden_units))
    returned, slope, flipped, down_made, placer, weighted = pl.pallas_call(
        moe_kernel,
        out_shape=(
            jax.ShapeDtypeStruct((2, NX * NX, CAP, features), BF16),
            jax.ShapeDtypeStruct((slots, hidden_units), BF16),
            jax.ShapeDtypeStruct((features, slots), BF16),
            jax.ShapeDtypeStruct((1, hidden_units, features), BF16),
            jax.ShapeDtypeStruct((slots, n_tok), BF16),
            jax.ShapeDtypeStruct((slots, n_tok), BF16),
        ),
        in_specs=[pl.BlockSpec(memory_space=pltpu.HBM)] * 7,
        out_specs=(hbm,) * 6,
        scratch_shapes=[
            pltpu.VMEM((features, hidden_units), BF16),
            pltpu.VMEM((hidden_units, features), BF16),
            pltpu.VMEM((features, slots), BF16),
            pltpu.VMEM((slots, n_tok), BF16),
            pltpu.VMEM((slots, n_tok), BF16),
            pltpu.VMEM((n_tok, features), BF16),
            pltpu.VMEM((n_tok, features), BF16),
            pltpu.VMEM((2, n_tok), jnp.int32),
            pltpu.VMEM((2, n_tok), BF16),
            pltpu.VMEM((1, NX * NX), jnp.int32),
            pltpu.VMEM((2, slots, features), BF16),
            pltpu.VMEM((2, slots, features), BF16),
            pltpu.VMEM((2, slots, hidden_units), F32),
            pltpu.VMEM((2, slots // 2, hidden_units), BF16),
            pltpu.VMEM((2, slots // 2, hidden_units), BF16),
            pltpu.VMEM((2, slots // (2 * NZ), hidden_units), BF16),
            pltpu.VMEM((2, slots // (2 * NZ), hidden_units), BF16),
            pltpu.VMEM((2, 2, slots // (2 * NZ), hidden_units), BF16),
            pltpu.VMEM((2, 2, slots // (2 * NZ), hidden_units), BF16),
            pltpu.VMEM((2, slots, hidden_units), BF16),
            pltpu.VMEM((2, slots, features), BF16),
            dma((7,)),
            dma((2, 2)),
            dma((2,)),
            dma((n_chunks, 2)),
            dma((1,)),
            dma((n_chunks, 2)),
            dma((1,)),
            dma((n_chunks, 2)),
            dma((1,)),
            dma((n_chunks, 2)),
            dma((1,)),
            dma((n_chunks, 2)),
            dma((1,)),
            dma((n_chunks, 2)),
            dma((1,)),
            dma((n_chunks, 2)),
            dma((2,)),
            dma((2,)),
            dma((4,)),
            dma((n_chunks,)),
        ],
        compiler_params=pltpu.CompilerParams(
            collective_id=0, has_side_effects=True, vmem_limit_bytes=VMEM_LIMIT
        ),
        cost_estimate=pl.CostEstimate(
            flops=flops, bytes_accessed=4 * features * hidden_units, transcendentals=slots * hidden_units // 8
        ),
        name="moe_exchange",
    )(tokens, cotangent, routes.T, route_weights.T, capacity_plan[None], up_weight, down_weight)
    return pl.pallas_call(
        combine_kernel,
        out_shape=(
            jax.ShapeDtypeStruct((n_tok, features), BF16),
            jax.ShapeDtypeStruct((n_tok, features), BF16),
            jax.ShapeDtypeStruct((1, features, hidden_units), BF16),
            jax.ShapeDtypeStruct((1, hidden_units, features), BF16),
        ),
        in_specs=[hbm] * 6,
        out_specs=(hbm,) * 4,
        scratch_shapes=[
            pltpu.VMEM((2, NX * NX, CAP, features), BF16),
            pltpu.VMEM((slots, n_tok), BF16),
            pltpu.VMEM((slots, n_tok), BF16),
            pltpu.VMEM((features, slots), BF16),
            pltpu.VMEM((slots, hidden_units), BF16),
            pltpu.VMEM((n_tok, features), BF16),
            pltpu.VMEM((n_tok, features), BF16),
            pltpu.VMEM((features, hidden_units), BF16),
            pltpu.VMEM((hidden_units, features), BF16),
            dma((5,)),
            dma((2,)),
            dma((PIECES,)),
            dma((PIECES,)),
            dma((n_tiles,)),
            dma((n_tiles,)),
        ],
        compiler_params=pltpu.CompilerParams(vmem_limit_bytes=COMBINE_VMEM_LIMIT),
        cost_estimate=pl.CostEstimate(
            flops=4 * slots * n_tok * features, bytes_accessed=8 * features * hidden_units, transcendentals=0
        ),
        name="combine",
    )(returned, placer, weighted, flipped, slope, down_made)


def solution(mesh):
    placed = (
        P("expert", "tensor"),
        P("expert", "tensor"),
        P("expert", None),
        P("expert", None),
        P(),
        P("expert", "tensor", None),
        P("expert", None, "tensor"),
    )
    return jax.shard_map(
        per_device,
        mesh=mesh,
        in_specs=placed,
        out_specs=(
            P("expert", "tensor"),
            P("expert", "tensor"),
            P("expert", "tensor", None),
            P("expert", None, "tensor"),
        ),
        check_vma=False,
    )
```

```python
import functools

import jax
import jax.numpy as jnp
from jax import lax
from jax.experimental import pallas as pl
from jax.experimental.pallas import tpu as pltpu
from jax.sharding import PartitionSpec as P

MESH = pl.DeviceIdType.MESH
F32 = jnp.float32
BF16 = jnp.bfloat16
NX = 4
NZ = 4
CAP = 32
SOURCES = (
    (0, 0), (2, 0), (0, 2), (2, 2),
    (1, 0), (3, 0), (0, 1), (0, 3),
    (1, 1), (3, 3), (1, 3), (3, 1),
    (2, 1), (1, 2), (2, 3), (3, 2),
)
CHUNKS = ((0, 4), (4, 8), (8, 12), (12, 16))
ORDER = (
    "P10", "P11", "P00", "P01", "A10", "A11", "P20", "B11", "B10", "A00", "P21", "C11",
    "A01", "B00", "C10", "B01", "A20", "C00", "P30", "B20", "D10", "A21", "D00", "P31",
    "C01", "C20", "D11", "E00", "E10", "B21", "D01", "A30", "F10", "D20", "A31", "F00",
    "B30", "E01", "B31", "G10", "C30", "E20", "E11", "C31", "G00", "F01", "D30", "F20",
    "C21", "F11", "G01", "D31", "G11", "E30", "D21", "G20", "E31", "X00", "F30", "G30",
    "F31", "E21", "G31", "F21", "G21", "Y00",
)
TILE = 512
PIECES = 4
ROUTE_VMEM_LIMIT = 60 * 1024 * 1024
VMEM_LIMIT = 41 * 1024 * 1024
COMBINE_VMEM_LIMIT = 28 * 1024 * 1024


def contract_last(left, right):
    return lax.dot_general(left, right, (((1,), (1,)), ((), ())), preferred_element_type=F32)


def contract_first(left, right):
    return lax.dot_general(left, right, (((0,), (0,)), ((), ())), preferred_element_type=F32)


def column_tiles(width, tile=TILE):
    return [(start, min(start + tile, width)) for start in range(0, width, tile)]


def wrap(value, size):
    return lax.rem(value + size, size)


def route_kernel(
    tokens_hbm, cotangent_hbm, routes_hbm, weights_hbm, plan_hbm,
    sent_hbm, placer_hbm, weighted_hbm,
    tokens, cotangent, routes, route_weights, plan, placer, weighted, sent, load_sem, store_sem,
):
    n_tok, features = tokens.shape
    n_experts, slots = NX * NX, NX * NX * CAP
    loads = [
        pltpu.make_async_copy(source, target, load_sem.at[which])
        for which, (source, target) in enumerate(
            (
                (routes_hbm, routes), (weights_hbm, route_weights), (plan_hbm, plan),
                (tokens_hbm, tokens), (cotangent_hbm, cotangent),
            )
        )
    ]
    for load in loads:
        load.start()
    for load in loads[:3]:
        load.wait()

    expert_id = lax.broadcasted_iota(jnp.int32, (n_experts, n_tok), 0)
    first, second = routes[0:1, :], routes[1:2, :]
    named_first = (expert_id == first).astype(F32)
    named_second = (expert_id == second).astype(F32)
    before = lax.broadcasted_iota(jnp.int32, (n_tok, n_tok), 0) < lax.broadcasted_iota(jnp.int32, (n_tok, n_tok), 1)
    earlier = jnp.dot(
        (named_first + named_second).astype(BF16), before.astype(F32).astype(BF16), preferred_element_type=F32
    )
    diagonal = lax.broadcasted_iota(jnp.int32, (n_experts, n_experts), 0) == lax.broadcasted_iota(
        jnp.int32, (n_experts, n_experts), 1
    )
    limit = jnp.sum(jnp.where(diagonal, plan[...].astype(F32), 0.0), axis=1, keepdims=True)
    slot_id = lax.broadcasted_iota(jnp.int32, (slots, n_tok), 0).astype(F32)
    hits = []
    pairs = ((first, named_first, earlier), (second, named_second, earlier + named_first))
    for named_id, named, count in pairs:
        position = jnp.sum(count * named, axis=0, keepdims=True)
        allowed = jnp.sum(limit * named, axis=0, keepdims=True)
        hits.append(slot_id == jnp.where(position < allowed, named_id.astype(F32) * CAP + position, -1.0))
    placer[...] = jnp.where(hits[0], 1.0, jnp.where(hits[1], 1.0, 0.0)).astype(BF16)

    scales = [route_weights[k : k + 1, :].astype(F32) for k in range(2)]
    weighted[...] = jnp.where(hits[0], scales[0], jnp.where(hits[1], scales[1], 0.0)).astype(BF16)
    stores = [
        pltpu.make_async_copy(placer, placer_hbm, store_sem.at[0]),
        pltpu.make_async_copy(weighted, weighted_hbm, store_sem.at[1]),
    ]
    for store in stores:
        store.start()
    for k, (matrix, picker) in enumerate(((tokens, placer), (cotangent, weighted))):
        loads[3 + k].wait()
        sent[k] = jnp.dot(picker[...], matrix[...], preferred_element_type=F32).astype(BF16)
        stores.append(pltpu.make_async_copy(sent.at[k], sent_hbm.at[k], store_sem.at[2 + k]))
        stores[-1].start()
    for store in stores:
        store.wait()


def moe_kernel(
    sent, up_hbm, down_hbm,
    returned, slope_hbm, flipped_hbm, down_grad,
    up, down, flipped, rows, part, core_out, core_in,
    first_out, first_in, second_out, second_in, acts, results,
    load_sem, own_sem, sent_sem, rows_sem, core_send, core_recv,
    first_send, first_recv, second_send, second_recv,
    near_send, near_recv, far_send, far_recv, mate_send, mate_recv,
    ret_send, ret_recv, store_sem, slope_sem,
):
    expert = lax.axis_index("expert")
    place = lax.axis_index("tensor")
    x, y = lax.div(expert, NX), lax.rem(expert, NX)
    z, core = lax.div(place, 2), lax.rem(place, 2)
    z_next, z_prev, z_far = wrap(z + 1, NZ), wrap(z - 1, NZ), wrap(z + 2, NZ)
    other = 1 - core
    features, hidden_units = up.shape
    split = ((hidden_units // 128 + 1) // 2) * 128
    tiles = column_tiles(hidden_units)
    half_a, half_b = pl.ds(0, split), pl.ds(split, hidden_units - split)
    n_experts, slots = NX * NX, NX * NX * CAP

    def at_z(which):
        return {"expert": expert, "tensor": which * 2 + core}

    next_chip, prev_chip = at_z(z_next), at_z(z_prev)
    mate = {"expert": expert, "tensor": z * 2 + other}
    owners = [wrap(x - dx, NX) * NX + wrap(y - dy, NX) for dx, dy in SOURCES]
    sources = [wrap(x + dx, NX) * NX + wrap(y + dy, NX) for dx, dy in SOURCES]

    def remote(src, dst, send, recv, device):
        return pltpu.make_async_remote_copy(
            src_ref=src, dst_ref=dst, send_sem=send, recv_sem=recv, device_id=device, device_id_type=MESH
        )

    def await_received(ref, sem):
        remote(ref, ref, sem, sem, mate).wait_recv()

    def await_sent(ref, sem):
        remote(ref, ref, sem, sem, mate).wait_send()

    barrier = pltpu.get_barrier_semaphore()
    load_up = pltpu.make_async_copy(up_hbm.at[0], up, load_sem.at[0])
    load_down = pltpu.make_async_copy(down_hbm.at[0], down, load_sem.at[1])
    for peer in sources[1:]:
        pl.semaphore_signal(barrier, inc=1, device_id={"expert": peer, "tensor": place}, device_id_type=MESH)
    for device in (next_chip, prev_chip, mate):
        pl.semaphore_signal(barrier, inc=1, device_id=device, device_id_type=MESH)

    def source_rows(s, count=1):
        return pl.ds(s * CAP, count * CAP)

    def chunk_rows(c):
        lo, hi = CHUNKS[c]
        return pl.ds(lo * CAP, (hi - lo) * CAP)

    def block_size(c):
        lo, hi = CHUNKS[c]
        return (hi - lo) * CAP // (2 * NZ)

    def block(c, side, which, count=1):
        size = block_size(c)
        return pl.ds(pl.multiple_of(CHUNKS[c][0] * CAP + (side * NZ + which) * size, 16), count * size)

    def half_block(c, which, count=1):
        size = block_size(c)
        return pl.ds(pl.multiple_of(CHUNKS[c][0] * CAP // 2 + which * size, 16), count * size)

    def small_block(c):
        return pl.ds(CHUNKS[c][0] * CAP // (2 * NZ), block_size(c))

    def remote_sources(c):
        lo, hi = CHUNKS[c]
        return range(max(lo, 1), hi)

    dispatch_order = [(int(step[1]), int(step[2])) for step in ORDER if step[0] == "P"]

    def expert_rows(which):
        return pl.ds(pl.multiple_of(which * CAP, CAP), CAP)

    def stage_dispatch(c, k):
        if (c, k) == dispatch_order[0]:
            pl.semaphore_wait(barrier, n_experts - 1 + 3)
        if c == 0:
            own_rows(k).start()
        for s in remote_sources(c):
            remote(
                sent.at[k, expert_rows(owners[s])], rows.at[k, source_rows(s)], sent_sem.at[k], rows_sem.at[c, k],
                {"expert": owners[s], "tensor": place},
            ).start()
        if (c, k) == dispatch_order[0]:
            load_up.start()
            load_down.start()

    def own_rows(k):
        return pltpu.make_async_copy(sent.at[k, expert_rows(expert)], rows.at[k, source_rows(0)], own_sem.at[0, k])

    def own_back(k):
        return pltpu.make_async_copy(results.at[k, source_rows(0)], returned.at[k, expert], own_sem.at[1, k])

    partial_order = [(int(step[1]), int(step[2])) for step in ORDER if step[0] == "A"]

    def stage_partial(c, k):
        if c == 0:
            own_rows(k).wait()
        if (c, k) == next((step_c, step_k) for step_c, step_k in partial_order if step_k == k):
            (load_up if k == 0 else load_down).wait()
        arriving = remote_sources(c)
        await_received(rows.at[k, source_rows(arriving[0], len(arriving))], rows_sem.at[c, k])
        taken = rows[k, chunk_rows(c), :]
        for lo, hi in tiles:
            if k == 0:
                product = jnp.dot(taken, up[:, lo:hi], preferred_element_type=F32)
            else:
                product = contract_last(taken, down[lo:hi, :])
            part[k, chunk_rows(c), lo:hi] = product
        away = half_block(c, 0, NZ)
        core_out[k, away, :] = part[k, block(c, other, 0, NZ), :].astype(BF16)
        remote(core_out.at[k, away], core_in.at[k, away], core_send.at[0], core_recv.at[c, k], mate).start()

    def chip_sum(c, k, which, half):
        return part[k, block(c, core, which), half] + core_in[k, half_block(c, which), half].astype(F32)

    def send_second(c, k, side, half):
        remote(
            second_out.at[k, side, small_block(c), half], second_in.at[k, side, small_block(c), half],
            second_send.at[0], second_recv.at[c, k], next_chip if side == 0 else prev_chip,
        ).start()

    def stage_core(c, k):
        await_received(core_in.at[k, half_block(c, 0, NZ)], core_recv.at[c, k])
        here = small_block(c)
        for half in (half_a, half_b):
            first_out[k, here, half] = chip_sum(c, k, z_far, half).astype(BF16)
        second_out[k, 0, here, half_b] = chip_sum(c, k, z_next, half_b).astype(BF16)
        second_out[k, 1, here, half_a] = chip_sum(c, k, z_prev, half_a).astype(BF16)
        for half, device in ((half_a, next_chip), (half_b, prev_chip)):
            remote(
                first_out.at[k, here, half], first_in.at[k, here, half], first_send.at[0], first_recv.at[c, k], device
            ).start()
        send_second(c, k, 0, half_b)
        send_second(c, k, 1, half_a)

    def stage_relay(c, k):
        here = small_block(c)
        relays = ((0, z_next, half_a), (1, z_prev, half_b))
        await_received(first_in.at[k, here], first_recv.at[c, k])
        for side, which, half in relays:
            total = chip_sum(c, k, which, half) + first_in[k, here, half].astype(F32)
            second_out[k, side, here, half] = total.astype(BF16)
        for side, which, half in relays:
            send_second(c, k, side, half)

    def stage_activate(c, k):
        here = small_block(c)
        await_received(second_in.at[k, :, here], second_recv.at[c, k])
        total = chip_sum(c, k, z, pl.ds(0, hidden_units))
        total = total + (second_in[k, 0, here, :].astype(F32) + second_in[k, 1, here, :].astype(F32))
        mine = block(c, core, z)
        if k == 0:
            part[0, mine, :] = total
            acts[0, mine, :] = (total * jax.nn.sigmoid(total)).astype(BF16)
        else:
            pre = part[0, mine, :]
            gate = jax.nn.sigmoid(pre)
            acts[1, mine, :] = (total * gate * (1.0 + pre * (1.0 - gate))).astype(BF16)
        ref = acts.at[k, mine]
        remote(ref, ref, near_send.at[0], near_recv.at[c, k], next_chip).start()
        remote(ref, ref, near_send.at[0], near_recv.at[c, k], prev_chip).start()

    def stage_forward(c, k):
        await_received(acts.at[k, block(c, core, 0, 2)], near_recv.at[c, k])
        for which, half, device in ((z_prev, half_a, next_chip), (z_next, half_b, prev_chip)):
            ref = acts.at[k, block(c, core, which), half]
            remote(ref, ref, far_send.at[0], far_recv.at[c, k], device).start()

    def stage_last(c, k):
        await_received(acts.at[k, block(c, core, z_far)], far_recv.at[c, k])
        ref = acts.at[k, block(c, core, 0, NZ)]
        remote(ref, ref, mate_send.at[0], mate_recv.at[c, k], mate).start()

    def stage_result(c, k):
        await_received(acts.at[k, block(c, other, 0, NZ)], mate_recv.at[c, k])
        taken = acts[k, chunk_rows(c), :]
        for lo, hi in column_tiles(features):
            if k == 0:
                product = jnp.dot(taken, down[:, lo:hi], preferred_element_type=F32)
            else:
                product = contract_last(taken, up[lo:hi, :])
            results[k, chunk_rows(c), lo:hi] = product.astype(BF16)
        if c == 0:
            own_back(k).start()
        for s in remote_sources(c):
            remote(
                results.at[k, source_rows(s)], returned.at[k, expert], ret_send.at[k], ret_recv.at[k],
                {"expert": sources[s], "tensor": place},
            ).start()
        if k == 1:
            save_slope(c).start()

    def stage_flip(c, k):
        flipped[...] = rows[0].T
        save_flipped.start()

    def stage_down_grad(c, k):
        for lo, hi in tiles:
            down[lo:hi, :] = contract_first(acts[0, :, lo:hi], rows[1]).astype(BF16)
        save_down.start()

    save_flipped = pltpu.make_async_copy(flipped, flipped_hbm, store_sem.at[0])
    save_down = pltpu.make_async_copy(down, down_grad.at[0], store_sem.at[1])

    def save_slope(c):
        return pltpu.make_async_copy(acts.at[1, chunk_rows(c)], slope_hbm.at[chunk_rows(c)], slope_sem.at[c])

    stages = {
        "P": stage_dispatch, "A": stage_partial, "B": stage_core, "C": stage_relay, "D": stage_activate,
        "E": stage_forward, "F": stage_last, "G": stage_result, "X": stage_flip, "Y": stage_down_grad,
    }

    for step in ORDER:
        stages[step[0]](int(step[1]), int(step[2]))

    for k in range(2):
        await_sent(sent.at[k, source_rows(1, n_experts - 1)], sent_sem.at[k])
        own_back(k).wait()
    for save in (save_flipped, *map(save_slope, range(len(CHUNKS)))):
        save.wait()
    quarter = slots // NZ
    await_sent(core_out, core_send.at[0])
    await_sent(first_out, first_send.at[0])
    await_sent(second_out, second_send.at[0])
    await_sent(acts.at[:, pl.ds(0, quarter)], near_send.at[0])
    await_sent(acts.at[:, pl.ds(0, quarter // 2)], far_send.at[0])
    await_sent(acts.at[:, pl.ds(0, 2 * quarter)], mate_send.at[0])
    for k in range(2):
        await_received(returned.at[k, pl.ds(0, n_experts - 1)], ret_recv.at[k])
        await_sent(results.at[k, source_rows(1, n_experts - 1)], ret_send.at[k])
    save_down.wait()


def combine_kernel(
    returned_hbm, placer_hbm, weighted_hbm, flipped_hbm, slope_hbm, down_hbm,
    layer_hbm, token_hbm, up_grad, down_grad,
    returned, placer, weighted, flipped, slope, layer_out, token_grad, up, down,
    load_sem, out_sem, in_sem, copy_sem, slope_sem, up_sem,
):
    slots, features = placer.shape[0], layer_out.shape[1]
    hidden_units = up.shape[1]
    tiles = column_tiles(hidden_units)
    load_flipped = pltpu.make_async_copy(flipped_hbm, flipped, load_sem.at[4])
    load_slope = [
        pltpu.make_async_copy(slope_hbm.at[:, lo:hi], slope.at[:, lo:hi], slope_sem.at[index])
        for index, (lo, hi) in enumerate(tiles)
    ]
    parts = (
        (
            pltpu.make_async_copy(weighted_hbm, weighted, load_sem.at[0]),
            pltpu.make_async_copy(returned_hbm.at[0], returned.at[0], load_sem.at[1]),
        ),
        (
            pltpu.make_async_copy(placer_hbm, placer, load_sem.at[2]),
            pltpu.make_async_copy(returned_hbm.at[1], returned.at[1], load_sem.at[3]),
        ),
    )
    size = hidden_units // PIECES
    picks = [pl.ds(piece * size, size) for piece in range(PIECES)]
    loads = [
        pltpu.make_async_copy(down_hbm.at[0, pick], down.at[pick], in_sem.at[piece])
        for piece, pick in enumerate(picks)
    ]
    stores = [
        pltpu.make_async_copy(down.at[pick], down_grad.at[0, pick], copy_sem.at[piece])
        for piece, pick in enumerate(picks)
    ]
    outs = [
        pltpu.make_async_copy(layer_out, layer_hbm, out_sem.at[0]),
        pltpu.make_async_copy(token_grad, token_hbm, out_sem.at[1]),
    ]
    up_stores = [
        pltpu.make_async_copy(up.at[:, lo:hi], up_grad.at[0, :, lo:hi], up_sem.at[index])
        for index, (lo, hi) in enumerate(tiles)
    ]
    for load in (load_flipped, *load_slope[:2]):
        load.start()
    load_flipped.wait()
    for index, (lo, hi) in enumerate(tiles):
        load_slope[index].wait()
        if index == 0:
            for load in (loads[0], *load_slope[2:], *loads[1:], *parts[0], *parts[1]):
                load.start()
        up[:, lo:hi] = jnp.dot(flipped[...], slope[:, lo:hi], preferred_element_type=F32).astype(BF16)
        up_stores[index].start()
        if index < PIECES:
            loads[index].wait()
            stores[index].start()
    for part, picker, result, out, k in zip(parts, (weighted, placer), (layer_out, token_grad), outs, range(2)):
        for load in part:
            load.wait()
        result[...] = contract_first(picker[...], returned[k].reshape(slots, features)).astype(BF16)
        out.start()
    for copy in (*up_stores, *stores, *outs):
        copy.wait()


def per_device(tokens, cotangent, routes, route_weights, capacity_plan, up_weight, down_weight):
    n_tok, features = tokens.shape
    hidden_units = up_weight.shape[2]
    slots = NX * NX * CAP
    hbm = pl.BlockSpec(memory_space=pl.ANY)
    dma = pltpu.SemaphoreType.DMA
    flops = 12 * slots * features * hidden_units
    n_chunks = len(CHUNKS)
    n_tiles = len(column_tiles(hidden_units))
    sent, placer, weighted = pl.pallas_call(
        route_kernel,
        out_shape=(
            jax.ShapeDtypeStruct((2, slots, features), BF16),
            jax.ShapeDtypeStruct((slots, n_tok), BF16),
            jax.ShapeDtypeStruct((slots, n_tok), BF16),
        ),
        in_specs=[hbm] * 5,
        out_specs=(hbm,) * 3,
        scratch_shapes=[
            pltpu.VMEM((n_tok, features), BF16),
            pltpu.VMEM((n_tok, features), BF16),
            pltpu.VMEM((2, n_tok), jnp.int32),
            pltpu.VMEM((2, n_tok), BF16),
            pltpu.VMEM((1, NX * NX), jnp.int32),
            pltpu.VMEM((slots, n_tok), BF16),
            pltpu.VMEM((slots, n_tok), BF16),
            pltpu.VMEM((2, slots, features), BF16),
            dma((5,)),
            dma((4,)),
        ],
        compiler_params=pltpu.CompilerParams(vmem_limit_bytes=ROUTE_VMEM_LIMIT),
        cost_estimate=pl.CostEstimate(
            flops=4 * slots * n_tok * features, bytes_accessed=6 * slots * features, transcendentals=0
        ),
        name="route",
    )(tokens, cotangent, routes.T, route_weights.T, capacity_plan[None])
    returned, slope, flipped, down_made = pl.pallas_call(
        moe_kernel,
        out_shape=(
            jax.ShapeDtypeStruct((2, NX * NX, CAP, features), BF16),
            jax.ShapeDtypeStruct((slots, hidden_units), BF16),
            jax.ShapeDtypeStruct((features, slots), BF16),
            jax.ShapeDtypeStruct((1, hidden_units, features), BF16),
        ),
        in_specs=[hbm] * 3,
        out_specs=(hbm,) * 4,
        scratch_shapes=[
            pltpu.VMEM((features, hidden_units), BF16),
            pltpu.VMEM((hidden_units, features), BF16),
            pltpu.VMEM((features, slots), BF16),
            pltpu.VMEM((2, slots, features), BF16),
            pltpu.VMEM((2, slots, hidden_units), F32),
            pltpu.VMEM((2, slots // 2, hidden_units), BF16),
            pltpu.VMEM((2, slots // 2, hidden_units), BF16),
            pltpu.VMEM((2, slots // (2 * NZ), hidden_units), BF16),
            pltpu.VMEM((2, slots // (2 * NZ), hidden_units), BF16),
            pltpu.VMEM((2, 2, slots // (2 * NZ), hidden_units), BF16),
            pltpu.VMEM((2, 2, slots // (2 * NZ), hidden_units), BF16),
            pltpu.VMEM((2, slots, hidden_units), BF16),
            pltpu.VMEM((2, slots, features), BF16),
            dma((2,)),
            dma((2, 2)),
            dma((2,)),
            dma((n_chunks, 2)),
            dma((1,)),
            dma((n_chunks, 2)),
            dma((1,)),
            dma((n_chunks, 2)),
            dma((1,)),
            dma((n_chunks, 2)),
            dma((1,)),
            dma((n_chunks, 2)),
            dma((1,)),
            dma((n_chunks, 2)),
            dma((1,)),
            dma((n_chunks, 2)),
            dma((2,)),
            dma((2,)),
            dma((2,)),
            dma((n_chunks,)),
        ],
        compiler_params=pltpu.CompilerParams(
            collective_id=0, has_side_effects=True, vmem_limit_bytes=VMEM_LIMIT
        ),
        cost_estimate=pl.CostEstimate(
            flops=flops, bytes_accessed=4 * features * hidden_units, transcendentals=slots * hidden_units // 8
        ),
        name="moe_exchange",
    )(sent, up_weight, down_weight)
    return pl.pallas_call(
        combine_kernel,
        out_shape=(
            jax.ShapeDtypeStruct((n_tok, features), BF16),
            jax.ShapeDtypeStruct((n_tok, features), BF16),
            jax.ShapeDtypeStruct((1, features, hidden_units), BF16),
            jax.ShapeDtypeStruct((1, hidden_units, features), BF16),
        ),
        in_specs=[hbm] * 6,
        out_specs=(hbm,) * 4,
        scratch_shapes=[
            pltpu.VMEM((2, NX * NX, CAP, features), BF16),
            pltpu.VMEM((slots, n_tok), BF16),
            pltpu.VMEM((slots, n_tok), BF16),
            pltpu.VMEM((features, slots), BF16),
            pltpu.VMEM((slots, hidden_units), BF16),
            pltpu.VMEM((n_tok, features), BF16),
            pltpu.VMEM((n_tok, features), BF16),
            pltpu.VMEM((features, hidden_units), BF16),
            pltpu.VMEM((hidden_units, features), BF16),
            dma((5,)),
            dma((2,)),
            dma((PIECES,)),
            dma((PIECES,)),
            dma((n_tiles,)),
            dma((n_tiles,)),
        ],
        compiler_params=pltpu.CompilerParams(vmem_limit_bytes=COMBINE_VMEM_LIMIT),
        cost_estimate=pl.CostEstimate(
            flops=4 * slots * n_tok * features, bytes_accessed=8 * features * hidden_units, transcendentals=0
        ),
        name="combine",
    )(returned, placer, weighted, flipped, slope, down_made)


def solution(mesh):
    placed = (
        P("expert", "tensor"),
        P("expert", "tensor"),
        P("expert", None),
        P("expert", None),
        P(),
        P("expert", "tensor", None),
        P("expert", None, "tensor"),
    )
    return jax.shard_map(
        per_device,
        mesh=mesh,
        in_specs=placed,
        out_specs=(
            P("expert", "tensor"),
            P("expert", "tensor"),
            P("expert", "tensor", None),
            P("expert", None, "tensor"),
        ),
        check_vma=False,
    )
```

```python
import functools

import jax
import jax.numpy as jnp
from jax import lax
from jax.experimental import pallas as pl
from jax.experimental.pallas import tpu as pltpu
from jax.sharding import PartitionSpec as P

MESH = pl.DeviceIdType.MESH
F32 = jnp.float32
BF16 = jnp.bfloat16
NX = 4
NZ = 4
CAP = 32
SOURCES = (
    (0, 0), (2, 0), (0, 2), (2, 2),
    (1, 0), (3, 0), (0, 1), (0, 3),
    (1, 1), (3, 3), (1, 3), (3, 1),
    (2, 1), (1, 2), (2, 3), (3, 2),
)
CHUNKS = ((0, 4), (4, 8), (8, 12), (12, 16))
ORDER = (
    "P10", "P11", "P00", "P01", "A10", "A11", "P20", "B11", "B10", "A00", "P21", "C11",
    "A01", "B00", "C10", "B01", "A20", "C00", "P30", "B20", "D10", "A21", "D00", "P31",
    "C01", "C20", "D11", "E00", "E10", "B21", "D01", "A30", "F10", "D20", "A31", "F00",
    "B30", "E01", "B31", "G10", "C30", "E20", "E11", "C31", "G00", "F01", "D30", "F20",
    "C21", "F11", "G01", "D31", "G11", "E30", "D21", "G20", "E31", "X00", "F30", "G30",
    "F31", "E21", "G31", "F21", "G21", "Y00",
)
TILE = 512
PIECES = 4
VMEM_LIMIT = 60 * 1024 * 1024
COMBINE_VMEM_LIMIT = 60 * 1024 * 1024


def contract_last(left, right):
    return lax.dot_general(left, right, (((1,), (1,)), ((), ())), preferred_element_type=F32)


def contract_first(left, right):
    return lax.dot_general(left, right, (((0,), (0,)), ((), ())), preferred_element_type=F32)


def column_tiles(width, tile=TILE):
    return [(start, min(start + tile, width)) for start in range(0, width, tile)]


def wrap(value, size):
    return lax.rem(value + size, size)


def moe_kernel(
    tokens_hbm, cotangent_hbm, routes_hbm, weights_hbm, plan_hbm, up_hbm, down_hbm,
    returned, slope_hbm, flipped_hbm, down_grad, placer_hbm, weighted_hbm,
    up, down, flipped, placer, weighted, tokens, cotangent, routes, route_weights, plan, sent, rows, part, core_out, core_in,
    first_out, first_in, second_out, second_in, acts, results,
    load_sem, own_sem, sent_sem, rows_sem, core_send, core_recv,
    first_send, first_recv, second_send, second_recv,
    near_send, near_recv, far_send, far_recv, mate_send, mate_recv,
    ret_send, ret_recv, store_sem, slope_sem,
):
    expert = lax.axis_index("expert")
    place = lax.axis_index("tensor")
    x, y = lax.div(expert, NX), lax.rem(expert, NX)
    z, core = lax.div(place, 2), lax.rem(place, 2)
    z_next, z_prev, z_far = wrap(z + 1, NZ), wrap(z - 1, NZ), wrap(z + 2, NZ)
    other = 1 - core
    n_tok, features = tokens.shape
    hidden_units = up.shape[1]
    split = ((hidden_units // 128 + 1) // 2) * 128
    tiles = column_tiles(hidden_units)
    half_a, half_b = pl.ds(0, split), pl.ds(split, hidden_units - split)
    n_experts, slots = NX * NX, NX * NX * CAP

    def at_z(which):
        return {"expert": expert, "tensor": which * 2 + core}

    next_chip, prev_chip = at_z(z_next), at_z(z_prev)
    mate = {"expert": expert, "tensor": z * 2 + other}
    owners = [wrap(x - dx, NX) * NX + wrap(y - dy, NX) for dx, dy in SOURCES]
    sources = [wrap(x + dx, NX) * NX + wrap(y + dy, NX) for dx, dy in SOURCES]

    def remote(src, dst, send, recv, device):
        return pltpu.make_async_remote_copy(
            src_ref=src, dst_ref=dst, send_sem=send, recv_sem=recv, device_id=device, device_id_type=MESH
        )

    def await_received(ref, sem):
        remote(ref, ref, sem, sem, mate).wait_recv()

    def await_sent(ref, sem):
        remote(ref, ref, sem, sem, mate).wait_send()

    barrier = pltpu.get_barrier_semaphore()
    for peer in sources[1:]:
        pl.semaphore_signal(barrier, inc=1, device_id={"expert": peer, "tensor": place}, device_id_type=MESH)
    for device in (next_chip, prev_chip, mate):
        pl.semaphore_signal(barrier, inc=1, device_id=device, device_id_type=MESH)
    load_tokens = pltpu.make_async_copy(tokens_hbm, tokens, load_sem.at[2])
    load_cotangent = pltpu.make_async_copy(cotangent_hbm, cotangent, load_sem.at[3])
    load_up = pltpu.make_async_copy(up_hbm.at[0], up, load_sem.at[0])
    load_down = pltpu.make_async_copy(down_hbm.at[0], down, load_sem.at[1])
    load_routing = [
        pltpu.make_async_copy(source, target, load_sem.at[4 + which])
        for which, (source, target) in enumerate(
            ((routes_hbm, routes), (weights_hbm, route_weights), (plan_hbm, plan))
        )
    ]
    for load in (*load_routing, load_tokens):
        load.start()

    for load in load_routing:
        load.wait()

    expert_id = lax.broadcasted_iota(jnp.int32, (n_experts, n_tok), 0)
    first, second = routes[0:1, :], routes[1:2, :]
    named_first = (expert_id == first).astype(F32)
    named_second = (expert_id == second).astype(F32)
    before = lax.broadcasted_iota(jnp.int32, (n_tok, n_tok), 0) < lax.broadcasted_iota(jnp.int32, (n_tok, n_tok), 1)
    earlier = jnp.dot(
        (named_first + named_second).astype(BF16), before.astype(F32).astype(BF16), preferred_element_type=F32
    )
    diagonal = lax.broadcasted_iota(jnp.int32, (n_experts, n_experts), 0) == lax.broadcasted_iota(
        jnp.int32, (n_experts, n_experts), 1
    )
    limit = jnp.sum(jnp.where(diagonal, plan[...].astype(F32), 0.0), axis=1, keepdims=True)
    slot_id = lax.broadcasted_iota(jnp.int32, (slots, n_tok), 0).astype(F32)
    hits = []
    pairs = ((first, named_first, earlier), (second, named_second, earlier + named_first))
    for named_id, named, count in pairs:
        position = jnp.sum(count * named, axis=0, keepdims=True)
        allowed = jnp.sum(limit * named, axis=0, keepdims=True)
        hits.append(slot_id == jnp.where(position < allowed, named_id.astype(F32) * CAP + position, -1.0))
    placer[...] = jnp.where(hits[0], 1.0, jnp.where(hits[1], 1.0, 0.0)).astype(BF16)

    def make_weighted():
        scales = [route_weights[k : k + 1, :].astype(F32) for k in range(2)]
        weighted[...] = jnp.where(hits[0], scales[0], jnp.where(hits[1], scales[1], 0.0)).astype(BF16)
        save_placer.start()
        save_weighted.start()

    def source_rows(s, count=1):
        return pl.ds(s * CAP, count * CAP)

    def chunk_rows(c):
        lo, hi = CHUNKS[c]
        return pl.ds(lo * CAP, (hi - lo) * CAP)

    def block_size(c):
        lo, hi = CHUNKS[c]
        return (hi - lo) * CAP // (2 * NZ)

    def block(c, side, which, count=1):
        size = block_size(c)
        return pl.ds(pl.multiple_of(CHUNKS[c][0] * CAP + (side * NZ + which) * size, 16), count * size)

    def half_block(c, which, count=1):
        size = block_size(c)
        return pl.ds(pl.multiple_of(CHUNKS[c][0] * CAP // 2 + which * size, 16), count * size)

    def small_block(c):
        return pl.ds(CHUNKS[c][0] * CAP // (2 * NZ), block_size(c))

    def remote_sources(c):
        lo, hi = CHUNKS[c]
        return range(max(lo, 1), hi)

    dispatch_order = [(int(step[1]), int(step[2])) for step in ORDER if step[0] == "P"]

    def make_rows(c, k):
        matrix, picker = ((tokens, placer), (cotangent, weighted))[k]
        is_first = (c, k) == next((at, kind) for at, kind in dispatch_order if kind == k)
        if is_first:
            (load_tokens, load_cotangent)[k].wait()
            if k == 1:
                make_weighted()
        picked = [picker[pl.ds(pl.multiple_of(owners[s] * CAP, CAP), CAP), :] for s in range(*CHUNKS[c])]
        sent[k, chunk_rows(c), :] = jnp.dot(
            jnp.concatenate(picked, axis=0), matrix[...], preferred_element_type=F32
        ).astype(BF16)
        if c == 0:
            own_rows(k).start()
        if (c, k) == dispatch_order[0]:
            pl.semaphore_wait(barrier, n_experts - 1 + 3)
        for s in remote_sources(c):
            remote(
                sent.at[k, source_rows(s)], rows.at[k, source_rows(s)], sent_sem.at[k], rows_sem.at[c, k],
                {"expert": owners[s], "tensor": place},
            ).start()
        if (c, k) == dispatch_order[0]:
            for load in (load_cotangent, load_up, load_down):
                load.start()

    def own_rows(k):
        return pltpu.make_async_copy(sent.at[k, source_rows(0)], rows.at[k, source_rows(0)], own_sem.at[0, k])

    def own_back(k):
        return pltpu.make_async_copy(results.at[k, source_rows(0)], returned.at[k, expert], own_sem.at[1, k])

    partial_order = [(int(step[1]), int(step[2])) for step in ORDER if step[0] == "A"]

    def stage_partial(c, k):
        if c == 0:
            own_rows(k).wait()
        if (c, k) == next((step_c, step_k) for step_c, step_k in partial_order if step_k == k):
            (load_up if k == 0 else load_down).wait()
        arriving = remote_sources(c)
        await_received(rows.at[k, source_rows(arriving[0], len(arriving))], rows_sem.at[c, k])
        taken = rows[k, chunk_rows(c), :]
        for lo, hi in tiles:
            if k == 0:
                product = jnp.dot(taken, up[:, lo:hi], preferred_element_type=F32)
            else:
                product = contract_last(taken, down[lo:hi, :])
            part[k, chunk_rows(c), lo:hi] = product
        away = half_block(c, 0, NZ)
        core_out[k, away, :] = part[k, block(c, other, 0, NZ), :].astype(BF16)
        remote(core_out.at[k, away], core_in.at[k, away], core_send.at[0], core_recv.at[c, k], mate).start()

    def chip_sum(c, k, which, half):
        return part[k, block(c, core, which), half] + core_in[k, half_block(c, which), half].astype(F32)

    def send_second(c, k, side, half):
        remote(
            second_out.at[k, side, small_block(c), half], second_in.at[k, side, small_block(c), half],
            second_send.at[0], second_recv.at[c, k], next_chip if side == 0 else prev_chip,
        ).start()

    def stage_core(c, k):
        await_received(core_in.at[k, half_block(c, 0, NZ)], core_recv.at[c, k])
        here = small_block(c)
        for half in (half_a, half_b):
            first_out[k, here, half] = chip_sum(c, k, z_far, half).astype(BF16)
        second_out[k, 0, here, half_b] = chip_sum(c, k, z_next, half_b).astype(BF16)
        second_out[k, 1, here, half_a] = chip_sum(c, k, z_prev, half_a).astype(BF16)
        for half, device in ((half_a, next_chip), (half_b, prev_chip)):
            remote(
                first_out.at[k, here, half], first_in.at[k, here, half], first_send.at[0], first_recv.at[c, k], device
            ).start()
        send_second(c, k, 0, half_b)
        send_second(c, k, 1, half_a)

    def stage_relay(c, k):
        here = small_block(c)
        relays = ((0, z_next, half_a), (1, z_prev, half_b))
        await_received(first_in.at[k, here], first_recv.at[c, k])
        for side, which, half in relays:
            total = chip_sum(c, k, which, half) + first_in[k, here, half].astype(F32)
            second_out[k, side, here, half] = total.astype(BF16)
        for side, which, half in relays:
            send_second(c, k, side, half)

    def stage_activate(c, k):
        here = small_block(c)
        await_received(second_in.at[k, :, here], second_recv.at[c, k])
        total = chip_sum(c, k, z, pl.ds(0, hidden_units))
        total = total + (second_in[k, 0, here, :].astype(F32) + second_in[k, 1, here, :].astype(F32))
        mine = block(c, core, z)
        if k == 0:
            part[0, mine, :] = total
            acts[0, mine, :] = (total * jax.nn.sigmoid(total)).astype(BF16)
        else:
            pre = part[0, mine, :]
            gate = jax.nn.sigmoid(pre)
            acts[1, mine, :] = (total * gate * (1.0 + pre * (1.0 - gate))).astype(BF16)
        ref = acts.at[k, mine]
        remote(ref, ref, near_send.at[0], near_recv.at[c, k], next_chip).start()
        remote(ref, ref, near_send.at[0], near_recv.at[c, k], prev_chip).start()

    def stage_forward(c, k):
        await_received(acts.at[k, block(c, core, 0, 2)], near_recv.at[c, k])
        for which, half, device in ((z_prev, half_a, next_chip), (z_next, half_b, prev_chip)):
            ref = acts.at[k, block(c, core, which), half]
            remote(ref, ref, far_send.at[0], far_recv.at[c, k], device).start()

    def stage_last(c, k):
        await_received(acts.at[k, block(c, core, z_far)], far_recv.at[c, k])
        ref = acts.at[k, block(c, core, 0, NZ)]
        remote(ref, ref, mate_send.at[0], mate_recv.at[c, k], mate).start()

    def stage_result(c, k):
        await_received(acts.at[k, block(c, other, 0, NZ)], mate_recv.at[c, k])
        taken = acts[k, chunk_rows(c), :]
        for lo, hi in column_tiles(features):
            if k == 0:
                product = jnp.dot(taken, down[:, lo:hi], preferred_element_type=F32)
            else:
                product = contract_last(taken, up[lo:hi, :])
            results[k, chunk_rows(c), lo:hi] = product.astype(BF16)
        if c == 0:
            own_back(k).start()
        for s in remote_sources(c):
            remote(
                results.at[k, source_rows(s)], returned.at[k, expert], ret_send.at[k], ret_recv.at[k],
                {"expert": sources[s], "tensor": place},
            ).start()
        if k == 1:
            save_slope(c).start()

    def stage_flip(c, k):
        flipped[...] = rows[0].T
        save_flipped.start()

    def stage_down_grad(c, k):
        for lo, hi in tiles:
            down[lo:hi, :] = contract_first(acts[0, :, lo:hi], rows[1]).astype(BF16)
        save_down.start()

    save_placer = pltpu.make_async_copy(placer, placer_hbm, store_sem.at[0])
    save_weighted = pltpu.make_async_copy(weighted, weighted_hbm, store_sem.at[1])
    save_flipped = pltpu.make_async_copy(flipped, flipped_hbm, store_sem.at[2])
    save_down = pltpu.make_async_copy(down, down_grad.at[0], store_sem.at[3])

    def save_slope(c):
        return pltpu.make_async_copy(acts.at[1, chunk_rows(c)], slope_hbm.at[chunk_rows(c)], slope_sem.at[c])

    stages = {
        "P": make_rows, "A": stage_partial, "B": stage_core, "C": stage_relay, "D": stage_activate,
        "E": stage_forward, "F": stage_last, "G": stage_result, "X": stage_flip, "Y": stage_down_grad,
    }

    for step in ORDER:
        stages[step[0]](int(step[1]), int(step[2]))

    for k in range(2):
        await_sent(sent.at[k, source_rows(1, n_experts - 1)], sent_sem.at[k])
        own_back(k).wait()
    for save in (save_placer, save_weighted, save_flipped, *map(save_slope, range(len(CHUNKS)))):
        save.wait()
    quarter = slots // NZ
    await_sent(core_out, core_send.at[0])
    await_sent(first_out, first_send.at[0])
    await_sent(second_out, second_send.at[0])
    await_sent(acts.at[:, pl.ds(0, quarter)], near_send.at[0])
    await_sent(acts.at[:, pl.ds(0, quarter // 2)], far_send.at[0])
    await_sent(acts.at[:, pl.ds(0, 2 * quarter)], mate_send.at[0])
    for k in range(2):
        await_received(returned.at[k, pl.ds(0, n_experts - 1)], ret_recv.at[k])
        await_sent(results.at[k, source_rows(1, n_experts - 1)], ret_send.at[k])
    save_down.wait()


def combine_kernel(
    returned_hbm, placer_hbm, weighted_hbm, flipped_hbm, slope_hbm, down_hbm,
    layer_hbm, token_hbm, up_grad, down_grad,
    returned, placer, weighted, flipped, slope, layer_out, token_grad, up, down,
    load_sem, out_sem, in_sem, copy_sem, slope_sem, up_sem,
):
    slots, features = placer.shape[0], layer_out.shape[1]
    hidden_units = up.shape[1]
    tiles = column_tiles(hidden_units)
    load_flipped = pltpu.make_async_copy(flipped_hbm, flipped, load_sem.at[4])
    load_slope = [
        pltpu.make_async_copy(slope_hbm.at[:, lo:hi], slope.at[:, lo:hi], slope_sem.at[index])
        for index, (lo, hi) in enumerate(tiles)
    ]
    parts = (
        (
            pltpu.make_async_copy(weighted_hbm, weighted, load_sem.at[0]),
            pltpu.make_async_copy(returned_hbm.at[0], returned.at[0], load_sem.at[1]),
        ),
        (
            pltpu.make_async_copy(placer_hbm, placer, load_sem.at[2]),
            pltpu.make_async_copy(returned_hbm.at[1], returned.at[1], load_sem.at[3]),
        ),
    )
    size = hidden_units // PIECES
    picks = [pl.ds(piece * size, size) for piece in range(PIECES)]
    loads = [
        pltpu.make_async_copy(down_hbm.at[0, pick], down.at[pick], in_sem.at[piece])
        for piece, pick in enumerate(picks)
    ]
    stores = [
        pltpu.make_async_copy(down.at[pick], down_grad.at[0, pick], copy_sem.at[piece])
        for piece, pick in enumerate(picks)
    ]
    outs = [
        pltpu.make_async_copy(layer_out, layer_hbm, out_sem.at[0]),
        pltpu.make_async_copy(token_grad, token_hbm, out_sem.at[1]),
    ]
    up_stores = [
        pltpu.make_async_copy(up.at[:, lo:hi], up_grad.at[0, :, lo:hi], up_sem.at[index])
        for index, (lo, hi) in enumerate(tiles)
    ]
    for load in (load_flipped, load_slope[0], loads[0], *load_slope[1:], *loads[1:], *parts[0], *parts[1]):
        load.start()
    load_flipped.wait()
    for index, (lo, hi) in enumerate(tiles):
        load_slope[index].wait()
        up[:, lo:hi] = jnp.dot(flipped[...], slope[:, lo:hi], preferred_element_type=F32).astype(BF16)
        up_stores[index].start()
        if index < PIECES:
            loads[index].wait()
            stores[index].start()
    for part, picker, result, out, k in zip(parts, (weighted, placer), (layer_out, token_grad), outs, range(2)):
        for load in part:
            load.wait()
        result[...] = contract_first(picker[...], returned[k].reshape(slots, features)).astype(BF16)
        out.start()
    for copy in (*up_stores, *stores, *outs):
        copy.wait()


def per_device(tokens, cotangent, routes, route_weights, capacity_plan, up_weight, down_weight):
    n_tok, features = tokens.shape
    hidden_units = up_weight.shape[2]
    slots = NX * NX * CAP
    hbm = pl.BlockSpec(memory_space=pl.ANY)
    dma = pltpu.SemaphoreType.DMA
    flops = 12 * slots * features * hidden_units
    n_chunks = len(CHUNKS)
    n_tiles = len(column_tiles(hidden_units))
    returned, slope, flipped, down_made, placer, weighted = pl.pallas_call(
        moe_kernel,
        out_shape=(
            jax.ShapeDtypeStruct((2, NX * NX, CAP, features), BF16),
            jax.ShapeDtypeStruct((slots, hidden_units), BF16),
            jax.ShapeDtypeStruct((features, slots), BF16),
            jax.ShapeDtypeStruct((1, hidden_units, features), BF16),
            jax.ShapeDtypeStruct((slots, n_tok), BF16),
            jax.ShapeDtypeStruct((slots, n_tok), BF16),
        ),
        in_specs=[pl.BlockSpec(memory_space=pltpu.HBM)] * 7,
        out_specs=(hbm,) * 6,
        scratch_shapes=[
            pltpu.VMEM((features, hidden_units), BF16),
            pltpu.VMEM((hidden_units, features), BF16),
            pltpu.VMEM((features, slots), BF16),
            pltpu.VMEM((slots, n_tok), BF16),
            pltpu.VMEM((slots, n_tok), BF16),
            pltpu.VMEM((n_tok, features), BF16),
            pltpu.VMEM((n_tok, features), BF16),
            pltpu.VMEM((2, n_tok), jnp.int32),
            pltpu.VMEM((2, n_tok), BF16),
            pltpu.VMEM((1, NX * NX), jnp.int32),
            pltpu.VMEM((2, slots, features), BF16),
            pltpu.VMEM((2, slots, features), BF16),
            pltpu.VMEM((2, slots, hidden_units), F32),
            pltpu.VMEM((2, slots // 2, hidden_units), BF16),
            pltpu.VMEM((2, slots // 2, hidden_units), BF16),
            pltpu.VMEM((2, slots // (2 * NZ), hidden_units), BF16),
            pltpu.VMEM((2, slots // (2 * NZ), hidden_units), BF16),
            pltpu.VMEM((2, 2, slots // (2 * NZ), hidden_units), BF16),
            pltpu.VMEM((2, 2, slots // (2 * NZ), hidden_units), BF16),
            pltpu.VMEM((2, slots, hidden_units), BF16),
            pltpu.VMEM((2, slots, features), BF16),
            dma((7,)),
            dma((2, 2)),
            dma((2,)),
            dma((n_chunks, 2)),
            dma((1,)),
            dma((n_chunks, 2)),
            dma((1,)),
            dma((n_chunks, 2)),
            dma((1,)),
            dma((n_chunks, 2)),
            dma((1,)),
            dma((n_chunks, 2)),
            dma((1,)),
            dma((n_chunks, 2)),
            dma((1,)),
            dma((n_chunks, 2)),
            dma((2,)),
            dma((2,)),
            dma((4,)),
            dma((n_chunks,)),
        ],
        compiler_params=pltpu.CompilerParams(
            collective_id=0, has_side_effects=True, vmem_limit_bytes=VMEM_LIMIT
        ),
        cost_estimate=pl.CostEstimate(
            flops=flops, bytes_accessed=4 * features * hidden_units, transcendentals=slots * hidden_units // 8
        ),
        name="moe_exchange",
    )(tokens, cotangent, routes.T, route_weights.T, capacity_plan[None], up_weight, down_weight)
    return pl.pallas_call(
        combine_kernel,
        out_shape=(
            jax.ShapeDtypeStruct((n_tok, features), BF16),
            jax.ShapeDtypeStruct((n_tok, features), BF16),
            jax.ShapeDtypeStruct((1, features, hidden_units), BF16),
            jax.ShapeDtypeStruct((1, hidden_units, features), BF16),
        ),
        in_specs=[hbm] * 6,
        out_specs=(hbm,) * 4,
        scratch_shapes=[
            pltpu.VMEM((2, NX * NX, CAP, features), BF16),
            pltpu.VMEM((slots, n_tok), BF16),
            pltpu.VMEM((slots, n_tok), BF16),
            pltpu.VMEM((features, slots), BF16),
            pltpu.VMEM((slots, hidden_units), BF16),
            pltpu.VMEM((n_tok, features), BF16),
            pltpu.VMEM((n_tok, features), BF16),
            pltpu.VMEM((features, hidden_units), BF16),
            pltpu.VMEM((hidden_units, features), BF16),
            dma((5,)),
            dma((2,)),
            dma((PIECES,)),
            dma((PIECES,)),
            dma((n_tiles,)),
            dma((n_tiles,)),
        ],
        compiler_params=pltpu.CompilerParams(vmem_limit_bytes=COMBINE_VMEM_LIMIT),
        cost_estimate=pl.CostEstimate(
            flops=4 * slots * n_tok * features, bytes_accessed=8 * features * hidden_units, transcendentals=0
        ),
        name="combine",
    )(returned, placer, weighted, flipped, slope, down_made)


def solution(mesh):
    placed = (
        P("expert", "tensor"),
        P("expert", "tensor"),
        P("expert", None),
        P("expert", None),
        P(),
        P("expert", "tensor", None),
        P("expert", None, "tensor"),
    )
    return jax.shard_map(
        per_device,
        mesh=mesh,
        in_specs=placed,
        out_specs=(
            P("expert", "tensor"),
            P("expert", "tensor"),
            P("expert", "tensor", None),
            P("expert", None, "tensor"),
        ),
        check_vma=False,
    )
```

```python
import functools

import jax
import jax.numpy as jnp
from jax import lax
from jax.experimental import pallas as pl
from jax.experimental.pallas import tpu as pltpu
from jax.sharding import PartitionSpec as P

MESH = pl.DeviceIdType.MESH
F32 = jnp.float32
BF16 = jnp.bfloat16
NX = 4
NZ = 4
CAP = 32
SOURCES = (
    (0, 0), (2, 0), (0, 2), (2, 2),
    (1, 0), (3, 0), (0, 1), (0, 3),
    (1, 1), (3, 3), (1, 3), (3, 1),
    (2, 1), (1, 2), (2, 3), (3, 2),
)
CHUNKS = ((0, 4), (4, 8), (8, 12), (12, 16))
ORDER = (
    "P10", "P11", "P00", "P01", "A10", "A11", "P20", "B11", "B10", "A00", "A01", "B00",
    "P21", "A20", "C11", "C10", "B01", "C00", "P30", "B20", "D10", "A21", "D00", "P31",
    "C01", "C20", "D11", "E00", "E10", "B21", "A30", "D01", "F10", "D20", "A31", "F00",
    "B30", "E01", "B31", "G10", "C30", "E20", "E11", "C31", "G00", "F01", "D30", "C21",
    "F20", "F11", "G01", "D31", "G11", "E30", "D21", "G20", "E31", "X00", "F30", "G30",
    "F31", "E21", "G31", "F21", "G21", "Y00",
)
TILE = 512
PIECES = 4
VMEM_LIMIT = 60 * 1024 * 1024
COMBINE_VMEM_LIMIT = 60 * 1024 * 1024


def contract_last(left, right):
    return lax.dot_general(left, right, (((1,), (1,)), ((), ())), preferred_element_type=F32)


def contract_first(left, right):
    return lax.dot_general(left, right, (((0,), (0,)), ((), ())), preferred_element_type=F32)


def column_tiles(width, tile=TILE):
    return [(start, min(start + tile, width)) for start in range(0, width, tile)]


def wrap(value, size):
    return lax.rem(value + size, size)


def moe_kernel(
    tokens_hbm, cotangent_hbm, routes_hbm, weights_hbm, plan_hbm, up_hbm, down_hbm,
    returned, slope_hbm, flipped_hbm, down_grad, placer_hbm, weighted_hbm,
    up, down, flipped, placer, weighted, tokens, cotangent, routes, route_weights, plan, sent, rows, part, core_out, core_in,
    first_out, first_in, second_out, second_in, acts, results,
    load_sem, own_sem, sent_sem, rows_sem, core_send, core_recv,
    first_send, first_recv, second_send, second_recv,
    near_send, near_recv, far_send, far_recv, mate_send, mate_recv,
    ret_send, ret_recv, store_sem, slope_sem,
):
    expert = lax.axis_index("expert")
    place = lax.axis_index("tensor")
    x, y = lax.div(expert, NX), lax.rem(expert, NX)
    z, core = lax.div(place, 2), lax.rem(place, 2)
    z_next, z_prev, z_far = wrap(z + 1, NZ), wrap(z - 1, NZ), wrap(z + 2, NZ)
    other = 1 - core
    n_tok, features = tokens.shape
    hidden_units = up.shape[1]
    split = ((hidden_units // 128 + 1) // 2) * 128
    tiles = column_tiles(hidden_units)
    half_a, half_b = pl.ds(0, split), pl.ds(split, hidden_units - split)
    n_experts, slots = NX * NX, NX * NX * CAP

    def at_z(which):
        return {"expert": expert, "tensor": which * 2 + core}

    next_chip, prev_chip = at_z(z_next), at_z(z_prev)
    mate = {"expert": expert, "tensor": z * 2 + other}
    owners = [wrap(x - dx, NX) * NX + wrap(y - dy, NX) for dx, dy in SOURCES]
    sources = [wrap(x + dx, NX) * NX + wrap(y + dy, NX) for dx, dy in SOURCES]

    def remote(src, dst, send, recv, device):
        return pltpu.make_async_remote_copy(
            src_ref=src, dst_ref=dst, send_sem=send, recv_sem=recv, device_id=device, device_id_type=MESH
        )

    def await_received(ref, sem):
        remote(ref, ref, sem, sem, mate).wait_recv()

    def await_sent(ref, sem):
        remote(ref, ref, sem, sem, mate).wait_send()

    barrier = pltpu.get_barrier_semaphore()
    load_tokens = pltpu.make_async_copy(tokens_hbm, tokens, load_sem.at[2])
    load_cotangent = pltpu.make_async_copy(cotangent_hbm, cotangent, load_sem.at[3])
    load_up = pltpu.make_async_copy(up_hbm.at[0], up, load_sem.at[0])
    load_down = pltpu.make_async_copy(down_hbm.at[0], down, load_sem.at[1])
    load_routing = [
        pltpu.make_async_copy(source, target, load_sem.at[4 + which])
        for which, (source, target) in enumerate(
            ((routes_hbm, routes), (weights_hbm, route_weights), (plan_hbm, plan))
        )
    ]
    for load in (*load_routing, load_tokens):
        load.start()
    for peer in sources[1:]:
        pl.semaphore_signal(barrier, inc=1, device_id={"expert": peer, "tensor": place}, device_id_type=MESH)
    for device in (next_chip, prev_chip, mate):
        pl.semaphore_signal(barrier, inc=1, device_id=device, device_id_type=MESH)

    for load in load_routing:
        load.wait()

    expert_id = lax.broadcasted_iota(jnp.int32, (n_experts, n_tok), 0)
    first, second = routes[0:1, :], routes[1:2, :]
    named_first = (expert_id == first).astype(F32)
    named_second = (expert_id == second).astype(F32)
    before = lax.broadcasted_iota(jnp.int32, (n_tok, n_tok), 0) < lax.broadcasted_iota(jnp.int32, (n_tok, n_tok), 1)
    earlier = jnp.dot(
        (named_first + named_second).astype(BF16), before.astype(F32).astype(BF16), preferred_element_type=F32
    )
    diagonal = lax.broadcasted_iota(jnp.int32, (n_experts, n_experts), 0) == lax.broadcasted_iota(
        jnp.int32, (n_experts, n_experts), 1
    )
    limit = jnp.sum(jnp.where(diagonal, plan[...].astype(F32), 0.0), axis=1, keepdims=True)
    slot_id = lax.broadcasted_iota(jnp.int32, (slots, n_tok), 0).astype(F32)
    hits = []
    pairs = ((first, named_first, earlier), (second, named_second, earlier + named_first))
    for named_id, named, count in pairs:
        position = jnp.sum(count * named, axis=0, keepdims=True)
        allowed = jnp.sum(limit * named, axis=0, keepdims=True)
        hits.append(slot_id == jnp.where(position < allowed, named_id.astype(F32) * CAP + position, -1.0))
    placer[...] = jnp.where(hits[0], 1.0, jnp.where(hits[1], 1.0, 0.0)).astype(BF16)

    def make_weighted():
        scales = [route_weights[k : k + 1, :].astype(F32) for k in range(2)]
        weighted[...] = jnp.where(hits[0], scales[0], jnp.where(hits[1], scales[1], 0.0)).astype(BF16)
        save_placer.start()
        save_weighted.start()

    def source_rows(s, count=1):
        return pl.ds(s * CAP, count * CAP)

    def chunk_rows(c):
        lo, hi = CHUNKS[c]
        return pl.ds(lo * CAP, (hi - lo) * CAP)

    def block_size(c):
        lo, hi = CHUNKS[c]
        return (hi - lo) * CAP // (2 * NZ)

    def block(c, side, which, count=1):
        size = block_size(c)
        return pl.ds(pl.multiple_of(CHUNKS[c][0] * CAP + (side * NZ + which) * size, 16), count * size)

    def half_block(c, which, count=1):
        size = block_size(c)
        return pl.ds(pl.multiple_of(CHUNKS[c][0] * CAP // 2 + which * size, 16), count * size)

    def small_block(c):
        return pl.ds(CHUNKS[c][0] * CAP // (2 * NZ), block_size(c))

    def remote_sources(c):
        lo, hi = CHUNKS[c]
        return range(max(lo, 1), hi)

    dispatch_order = [(int(step[1]), int(step[2])) for step in ORDER if step[0] == "P"]

    def make_rows(c, k):
        matrix, picker = ((tokens, placer), (cotangent, weighted))[k]
        is_first = (c, k) == next((at, kind) for at, kind in dispatch_order if kind == k)
        if is_first:
            (load_tokens, load_cotangent)[k].wait()
            if k == 1:
                make_weighted()
        picked = [picker[pl.ds(pl.multiple_of(owners[s] * CAP, CAP), CAP), :] for s in range(*CHUNKS[c])]
        sent[k, chunk_rows(c), :] = jnp.dot(
            jnp.concatenate(picked, axis=0), matrix[...], preferred_element_type=F32
        ).astype(BF16)
        if c == 0:
            own_rows(k).start()
        if (c, k) == dispatch_order[0]:
            pl.semaphore_wait(barrier, n_experts - 1 + 3)
        for s in remote_sources(c):
            remote(
                sent.at[k, source_rows(s)], rows.at[k, source_rows(s)], sent_sem.at[k], rows_sem.at[c, k],
                {"expert": owners[s], "tensor": place},
            ).start()
        if (c, k) == dispatch_order[0]:
            for load in (load_cotangent, load_up, load_down):
                load.start()

    def own_rows(k):
        return pltpu.make_async_copy(sent.at[k, source_rows(0)], rows.at[k, source_rows(0)], own_sem.at[0, k])

    def own_back(k):
        return pltpu.make_async_copy(results.at[k, source_rows(0)], returned.at[k, expert], own_sem.at[1, k])

    partial_order = [(int(step[1]), int(step[2])) for step in ORDER if step[0] == "A"]

    def stage_partial(c, k):
        if c == 0:
            own_rows(k).wait()
        if (c, k) == next((step_c, step_k) for step_c, step_k in partial_order if step_k == k):
            (load_up if k == 0 else load_down).wait()
        arriving = remote_sources(c)
        await_received(rows.at[k, source_rows(arriving[0], len(arriving))], rows_sem.at[c, k])
        taken = rows[k, chunk_rows(c), :]
        for lo, hi in tiles:
            if k == 0:
                product = jnp.dot(taken, up[:, lo:hi], preferred_element_type=F32)
            else:
                product = contract_last(taken, down[lo:hi, :])
            part[k, chunk_rows(c), lo:hi] = product
        away = half_block(c, 0, NZ)
        core_out[k, away, :] = part[k, block(c, other, 0, NZ), :].astype(BF16)
        remote(core_out.at[k, away], core_in.at[k, away], core_send.at[0], core_recv.at[c, k], mate).start()

    def chip_sum(c, k, which, half):
        return part[k, block(c, core, which), half] + core_in[k, half_block(c, which), half].astype(F32)

    def stage_core(c, k):
        await_received(core_in.at[k, half_block(c, 0, NZ)], core_recv.at[c, k])
        here = small_block(c)
        for side, (for_a, for_b) in enumerate(((z_far, z_next), (z_prev, z_far))):
            first_out[k, side, here, half_a] = chip_sum(c, k, for_a, half_a).astype(BF16)
            first_out[k, side, here, half_b] = chip_sum(c, k, for_b, half_b).astype(BF16)
        for side, device in ((0, next_chip), (1, prev_chip)):
            remote(
                first_out.at[k, side, here], first_in.at[k, side, here], first_send.at[0], first_recv.at[c, k], device
            ).start()

    def stage_relay(c, k):
        here = small_block(c)
        relays = ((0, z_next, half_a, next_chip), (1, z_prev, half_b, prev_chip))
        await_received(first_in.at[k, :, here], first_recv.at[c, k])
        for side, which, half, device in relays:
            total = chip_sum(c, k, which, half) + first_in[k, side, here, half].astype(F32)
            second_out[k, here, half] = total.astype(BF16)
        for side, which, half, device in relays:
            remote(
                second_out.at[k, here, half], second_in.at[k, here, half], second_send.at[0], second_recv.at[c, k],
                device,
            ).start()

    def stage_activate(c, k):
        here = small_block(c)
        await_received(second_in.at[k, here], second_recv.at[c, k])
        total = chip_sum(c, k, z, pl.ds(0, hidden_units)) + second_in[k, here, :].astype(F32)
        total = total + jnp.concatenate(
            [first_in[k, 1, here, half_a].astype(F32), first_in[k, 0, here, half_b].astype(F32)], axis=1
        )
        mine = block(c, core, z)
        if k == 0:
            part[0, mine, :] = total
            acts[0, mine, :] = (total * jax.nn.sigmoid(total)).astype(BF16)
        else:
            pre = part[0, mine, :]
            gate = jax.nn.sigmoid(pre)
            acts[1, mine, :] = (total * gate * (1.0 + pre * (1.0 - gate))).astype(BF16)
        ref = acts.at[k, mine]
        remote(ref, ref, near_send.at[0], near_recv.at[c, k], next_chip).start()
        remote(ref, ref, near_send.at[0], near_recv.at[c, k], prev_chip).start()

    def stage_forward(c, k):
        await_received(acts.at[k, block(c, core, 0, 2)], near_recv.at[c, k])
        for which, half, device in ((z_prev, half_a, next_chip), (z_next, half_b, prev_chip)):
            ref = acts.at[k, block(c, core, which), half]
            remote(ref, ref, far_send.at[0], far_recv.at[c, k], device).start()

    def stage_last(c, k):
        await_received(acts.at[k, block(c, core, z_far)], far_recv.at[c, k])
        ref = acts.at[k, block(c, core, 0, NZ)]
        remote(ref, ref, mate_send.at[0], mate_recv.at[c, k], mate).start()

    def stage_result(c, k):
        await_received(acts.at[k, block(c, other, 0, NZ)], mate_recv.at[c, k])
        taken = acts[k, chunk_rows(c), :]
        for lo, hi in column_tiles(features):
            if k == 0:
                product = jnp.dot(taken, down[:, lo:hi], preferred_element_type=F32)
            else:
                product = contract_last(taken, up[lo:hi, :])
            results[k, chunk_rows(c), lo:hi] = product.astype(BF16)
        if c == 0:
            own_back(k).start()
        for s in remote_sources(c):
            remote(
                results.at[k, source_rows(s)], returned.at[k, expert], ret_send.at[k], ret_recv.at[k],
                {"expert": sources[s], "tensor": place},
            ).start()
        if k == 1:
            save_slope(c).start()

    def stage_flip(c, k):
        flipped[...] = rows[0].T
        save_flipped.start()

    def stage_down_grad(c, k):
        for lo, hi in tiles:
            down[lo:hi, :] = contract_first(acts[0, :, lo:hi], rows[1]).astype(BF16)
        save_down.start()

    save_placer = pltpu.make_async_copy(placer, placer_hbm, store_sem.at[0])
    save_weighted = pltpu.make_async_copy(weighted, weighted_hbm, store_sem.at[1])
    save_flipped = pltpu.make_async_copy(flipped, flipped_hbm, store_sem.at[2])
    save_down = pltpu.make_async_copy(down, down_grad.at[0], store_sem.at[3])

    def save_slope(c):
        return pltpu.make_async_copy(acts.at[1, chunk_rows(c)], slope_hbm.at[chunk_rows(c)], slope_sem.at[c])

    stages = {
        "P": make_rows, "A": stage_partial, "B": stage_core, "C": stage_relay, "D": stage_activate,
        "E": stage_forward, "F": stage_last, "G": stage_result, "X": stage_flip, "Y": stage_down_grad,
    }

    for step in ORDER:
        stages[step[0]](int(step[1]), int(step[2]))

    for k in range(2):
        await_sent(sent.at[k, source_rows(1, n_experts - 1)], sent_sem.at[k])
        own_back(k).wait()
    for save in (save_placer, save_weighted, save_flipped, *map(save_slope, range(len(CHUNKS)))):
        save.wait()
    quarter = slots // NZ
    await_sent(core_out, core_send.at[0])
    await_sent(first_out, first_send.at[0])
    await_sent(second_out, second_send.at[0])
    await_sent(acts.at[:, pl.ds(0, quarter)], near_send.at[0])
    await_sent(acts.at[:, pl.ds(0, quarter // 2)], far_send.at[0])
    await_sent(acts.at[:, pl.ds(0, 2 * quarter)], mate_send.at[0])
    for k in range(2):
        await_received(returned.at[k, pl.ds(0, n_experts - 1)], ret_recv.at[k])
        await_sent(results.at[k, source_rows(1, n_experts - 1)], ret_send.at[k])
    save_down.wait()


def combine_kernel(
    returned_hbm, placer_hbm, weighted_hbm, flipped_hbm, slope_hbm, down_hbm,
    layer_hbm, token_hbm, up_grad, down_grad,
    returned, placer, weighted, flipped, slope, layer_out, token_grad, up, down,
    load_sem, out_sem, in_sem, copy_sem, slope_sem, up_sem,
):
    slots, features = placer.shape[0], layer_out.shape[1]
    hidden_units = up.shape[1]
    tiles = column_tiles(hidden_units)
    load_flipped = pltpu.make_async_copy(flipped_hbm, flipped, load_sem.at[4])
    load_slope = [
        pltpu.make_async_copy(slope_hbm.at[:, lo:hi], slope.at[:, lo:hi], slope_sem.at[index])
        for index, (lo, hi) in enumerate(tiles)
    ]
    parts = (
        (
            pltpu.make_async_copy(weighted_hbm, weighted, load_sem.at[0]),
            pltpu.make_async_copy(returned_hbm.at[0], returned.at[0], load_sem.at[1]),
        ),
        (
            pltpu.make_async_copy(placer_hbm, placer, load_sem.at[2]),
            pltpu.make_async_copy(returned_hbm.at[1], returned.at[1], load_sem.at[3]),
        ),
    )
    size = hidden_units // PIECES
    picks = [pl.ds(piece * size, size) for piece in range(PIECES)]
    loads = [
        pltpu.make_async_copy(down_hbm.at[0, pick], down.at[pick], in_sem.at[piece])
        for piece, pick in enumerate(picks)
    ]
    stores = [
        pltpu.make_async_copy(down.at[pick], down_grad.at[0, pick], copy_sem.at[piece])
        for piece, pick in enumerate(picks)
    ]
    outs = [
        pltpu.make_async_copy(layer_out, layer_hbm, out_sem.at[0]),
        pltpu.make_async_copy(token_grad, token_hbm, out_sem.at[1]),
    ]
    up_stores = [
        pltpu.make_async_copy(up.at[:, lo:hi], up_grad.at[0, :, lo:hi], up_sem.at[index])
        for index, (lo, hi) in enumerate(tiles)
    ]
    for load in (load_flipped, *load_slope[:2]):
        load.start()
    load_flipped.wait()
    for index, (lo, hi) in enumerate(tiles):
        load_slope[index].wait()
        if index == 0:
            for load in (loads[0], *load_slope[2:], *loads[1:], *parts[0], *parts[1]):
                load.start()
        up[:, lo:hi] = jnp.dot(flipped[...], slope[:, lo:hi], preferred_element_type=F32).astype(BF16)
        up_stores[index].start()
        if index < PIECES:
            loads[index].wait()
            stores[index].start()
    for part, picker, result, out, k in zip(parts, (weighted, placer), (layer_out, token_grad), outs, range(2)):
        for load in part:
            load.wait()
        result[...] = contract_first(picker[...], returned[k].reshape(slots, features)).astype(BF16)
        out.start()
    for copy in (*up_stores, *stores, *outs):
        copy.wait()


def per_device(tokens, cotangent, routes, route_weights, capacity_plan, up_weight, down_weight):
    n_tok, features = tokens.shape
    hidden_units = up_weight.shape[2]
    slots = NX * NX * CAP
    hbm = pl.BlockSpec(memory_space=pl.ANY)
    dma = pltpu.SemaphoreType.DMA
    flops = 12 * slots * features * hidden_units
    n_chunks = len(CHUNKS)
    n_tiles = len(column_tiles(hidden_units))
    returned, slope, flipped, down_made, placer, weighted = pl.pallas_call(
        moe_kernel,
        out_shape=(
            jax.ShapeDtypeStruct((2, NX * NX, CAP, features), BF16),
            jax.ShapeDtypeStruct((slots, hidden_units), BF16),
            jax.ShapeDtypeStruct((features, slots), BF16),
            jax.ShapeDtypeStruct((1, hidden_units, features), BF16),
            jax.ShapeDtypeStruct((slots, n_tok), BF16),
            jax.ShapeDtypeStruct((slots, n_tok), BF16),
        ),
        in_specs=[pl.BlockSpec(memory_space=pltpu.HBM)] * 7,
        out_specs=(hbm,) * 6,
        scratch_shapes=[
            pltpu.VMEM((features, hidden_units), BF16),
            pltpu.VMEM((hidden_units, features), BF16),
            pltpu.VMEM((features, slots), BF16),
            pltpu.VMEM((slots, n_tok), BF16),
            pltpu.VMEM((slots, n_tok), BF16),
            pltpu.VMEM((n_tok, features), BF16),
            pltpu.VMEM((n_tok, features), BF16),
            pltpu.VMEM((2, n_tok), jnp.int32),
            pltpu.VMEM((2, n_tok), BF16),
            pltpu.VMEM((1, NX * NX), jnp.int32),
            pltpu.VMEM((2, slots, features), BF16),
            pltpu.VMEM((2, slots, features), BF16),
            pltpu.VMEM((2, slots, hidden_units), F32),
            pltpu.VMEM((2, slots // 2, hidden_units), BF16),
            pltpu.VMEM((2, slots // 2, hidden_units), BF16),
            pltpu.VMEM((2, 2, slots // (2 * NZ), hidden_units), BF16),
            pltpu.VMEM((2, 2, slots // (2 * NZ), hidden_units), BF16),
            pltpu.VMEM((2, slots // (2 * NZ), hidden_units), BF16),
            pltpu.VMEM((2, slots // (2 * NZ), hidden_units), BF16),
            pltpu.VMEM((2, slots, hidden_units), BF16),
            pltpu.VMEM((2, slots, features), BF16),
            dma((7,)),
            dma((2, 2)),
            dma((2,)),
            dma((n_chunks, 2)),
            dma((1,)),
            dma((n_chunks, 2)),
            dma((1,)),
            dma((n_chunks, 2)),
            dma((1,)),
            dma((n_chunks, 2)),
            dma((1,)),
            dma((n_chunks, 2)),
            dma((1,)),
            dma((n_chunks, 2)),
            dma((1,)),
            dma((n_chunks, 2)),
            dma((2,)),
            dma((2,)),
            dma((4,)),
            dma((n_chunks,)),
        ],
        compiler_params=pltpu.CompilerParams(
            collective_id=0, has_side_effects=True, vmem_limit_bytes=VMEM_LIMIT
        ),
        cost_estimate=pl.CostEstimate(
            flops=flops, bytes_accessed=4 * features * hidden_units, transcendentals=slots * hidden_units // 8
        ),
        name="moe_exchange",
    )(tokens, cotangent, routes.T, route_weights.T, capacity_plan[None], up_weight, down_weight)
    return pl.pallas_call(
        combine_kernel,
        out_shape=(
            jax.ShapeDtypeStruct((n_tok, features), BF16),
            jax.ShapeDtypeStruct((n_tok, features), BF16),
            jax.ShapeDtypeStruct((1, features, hidden_units), BF16),
            jax.ShapeDtypeStruct((1, hidden_units, features), BF16),
        ),
        in_specs=[hbm] * 6,
        out_specs=(hbm,) * 4,
        scratch_shapes=[
            pltpu.VMEM((2, NX * NX, CAP, features), BF16),
            pltpu.VMEM((slots, n_tok), BF16),
            pltpu.VMEM((slots, n_tok), BF16),
            pltpu.VMEM((features, slots), BF16),
            pltpu.VMEM((slots, hidden_units), BF16),
            pltpu.VMEM((n_tok, features), BF16),
            pltpu.VMEM((n_tok, features), BF16),
            pltpu.VMEM((features, hidden_units), BF16),
            pltpu.VMEM((hidden_units, features), BF16),
            dma((5,)),
            dma((2,)),
            dma((PIECES,)),
            dma((PIECES,)),
            dma((n_tiles,)),
            dma((n_tiles,)),
        ],
        compiler_params=pltpu.CompilerParams(vmem_limit_bytes=COMBINE_VMEM_LIMIT),
        cost_estimate=pl.CostEstimate(
            flops=4 * slots * n_tok * features, bytes_accessed=8 * features * hidden_units, transcendentals=0
        ),
        name="combine",
    )(returned, placer, weighted, flipped, slope, down_made)


def solution(mesh):
    placed = (
        P("expert", "tensor"),
        P("expert", "tensor"),
        P("expert", None),
        P("expert", None),
        P(),
        P("expert", "tensor", None),
        P("expert", None, "tensor"),
    )
    return jax.shard_map(
        per_device,
        mesh=mesh,
        in_specs=placed,
        out_specs=(
            P("expert", "tensor"),
            P("expert", "tensor"),
            P("expert", "tensor", None),
            P("expert", None, "tensor"),
        ),
        check_vma=False,
    )
```
